32 devices in a mesh: req: 8 (over z, y), mdl: 4 (over x, core).
Axes of the slice: x: 2, y: 2, z: 4, core: 2. Of those that a mesh axis runs over, the one named last changes fastest.
Arguments:
- stream: bfloat16 [6144, 1792], P('req'), may hold values from -6 to 6
- attention_projection_weight: bfloat16 [3, 1792, 1792], P(None, 'mdl'), may hold values from -0.125 to 0.125
- head_output_weight: bfloat16 [1792, 1792], P('mdl'), may hold values from -0.125 to 0.125
- adapter_down_maps: bfloat16 [64, 1792, 16], P('mdl'), may hold values from -0.125 to 0.125
- adapter_up_maps: bfloat16 [2, 1792, 1024], P(None, 'mdl'), may hold values from -1.5 to 1.5
- tenant_adapter_scale: float32 [4], replicated, may hold values from 0.5 to 2
- feedforward_norm_gain: bfloat16 [1792], replicated, may hold values from 0.099609375 to 1.8984375
- feedforward_weight: bfloat16 [3, 1792, 4864], P(None, 'req', 'mdl'), may hold values from -0.125 to 0.125
- prefix_cache_store: bfloat16 [256, 2, 1792, 128], P('req', None, 'mdl'), may hold values from -140 to 140
- token_adapter_index: int32 [6144], P('req'), may hold values from 0 to 63
- request_token_lengths: int32 [8, 24], P('req'), may hold values from 1 to 192, 768 in all within a row
- request_tenant_index: int32 [192], P('req'), may hold values from 0 to 3
- last_page_holder: int32 [192, 1], replicated, may hold values from 0 to 7; in each aligned block of 24 rows (0 to 23, 24 to 47, ...) at most 4 rows name the same one
- holder_page_slot: int32 [192], replicated, may hold values from 0 to 31
- page_filled_rows: int32 [192], replicated, may hold values from 64 to 128
Outputs:
- layer_out: bfloat16 [6144, 1792], P(('req', 'mdl'))
The draws below stay inside these ranges and needn't reach their ends.
Inputs may be any that keep to these rules, and one draw needn't show every extreme that they name: `last_page_holder`: within the rows of one index of req (aligned blocks of 24 rows) no holder is named more than 4 times, and one holder exactly 4 times in some blocks. `request_token_lengths`: each row sums to 768; its longest request has exactly 192 tokens.
All inputs are finite; a program needn't handle non-finite values.
Results may differ from the reference program's by a relative error of at most 0.025.
Values may be sent and summed in bfloat16 or wider, within the bound.
No kernel may reach another device: no remote copies, remote signals or barrier semaphores. Data moves between devices by JAX's collectives and lax.ppermute only.
A program may use at most 128 MiB of HBM per device.

```python
import math
import jax
import jax.numpy as jnp
import numpy as np
from jax import lax

MODEL_DIMENSION = 1792
ATTENTION_HEADS = 16
HEAD_SIZE = 112
FF = 4864
WINDOW = 64
PAGE = 128
ADAPTER_RANK = 16
ADAPTER_TOTAL = 64
TENANTS = 4
TOKEN_SLOTS = 768
REQ_DEV = 24
POOL_DEV = 32
MOST_LEN = 192
CAP = 4
TOKENS = 6144
REQS = 192
POOLS = 256
N_REQ = 8
N_MDL = 4


def draw_prefix_cache_store(key, part):
    array_shape = (POOLS, 2, ATTENTION_HEADS * HEAD_SIZE, PAGE)
    return jax.random.truncated_normal(jax.random.fold_in(key, 73), -6.0, 6.0, array_shape, jnp.float32).astype(jnp.bfloat16)


def with_ends(entries, rng, low, high):
    shape = entries.shape
    spot = [jax.random.randint(jax.random.fold_in(rng, axis), (), 0, shape[axis]) for axis in range(len(shape))]
    entries = entries.at[tuple(spot)].set(low)
    longest = shape.index(max(shape))
    spot[longest] = (spot[longest] + 1) % shape[longest]
    return entries.at[tuple(spot)].set(high)


def block_scale(own_key, extent, shards, low, top_value):
    def one(axis_at, blocks):
        steps = jax.random.uniform(jax.random.fold_in(jax.random.fold_in(own_key, 6), axis_at), (blocks,), jnp.float32, low / len(shards), top_value / len(shards))
        return jnp.repeat(jnp.exp(steps), extent[axis_at] // blocks).reshape((-1,) + (1,) * (len(extent) - axis_at - 1))

    level = one(*shards[0])
    for cut in shards[1:]:
        level = level * one(*cut)
    return level


def profile(count, total, reach, slope):
    weights = [(1 << 20) // math.isqrt(standing ** slope) + 1 for standing in range(2, count + 1)]
    rest, counts = total - reach - (count - 1), [1] * (count - 1)
    while rest > 0:
        movable = [i for i in range(count - 1) if counts[i] < reach]
        mass, remaining = sum([weights[i] for i in movable]), rest
        for i in movable:
            addition = min(reach - counts[i], max(1, remaining * weights[i] // mass), rest)
            counts[i] = counts[i] + addition
            rest = rest - addition
    return np.array([reach] + counts)


def ragged_sizes(key, count, total, bound, slope):
    if count == 2:
        one = jax.random.randint(key, (), max(1, total - bound), min(bound, total - 1) + 1)
        return jnp.stack([one, total - one])
    tallies = jnp.asarray(profile(count, total, bound, slope), jnp.int32)
    twos = (count - 1) // 2
    donor, sink = tallies[1:1 + 2 * twos:2], tallies[2:2 + 2 * twos:2]
    slack = jnp.minimum(donor - 1, bound - sink)
    moved = jax.random.randint(jax.random.fold_in(key, 1), (twos,), 0, 1 << 20) % (slack + 1)
    tallies = tallies.at[1:1 + 2 * twos:2].set(donor - moved).at[2:2 + 2 * twos:2].set(sink + moved)
    return tallies[jax.random.permutation(jax.random.fold_in(key, 2), count)]


def deal_out(own_key, own, number, rows, number_of, top, bound, lean):
    sequence = jax.random.permutation(own_key, number_of)
    crowded, ordinary = shares(number_of, rows * top, bound, lean, True), shares(number_of, rows * top, bound, lean, False)
    places = jnp.arange(number_of)

    def named(lengths, rotation):
        used = int((lengths > 0).sum())
        fixed = max(1, used // 4)
        passed = fixed + (places - fixed + rotation * (used - fixed)) % max(1, number_of - fixed)
        return jnp.zeros((number_of,), jnp.int32).at[sequence[jnp.where(places < fixed, places, passed)]].set(jnp.asarray(lengths, jnp.int32))

    lengths = jnp.where(number % 4 == 0, named(crowded, number // 4), named(ordinary, number - number // 4 - 1))
    mixed = jax.random.permutation(jax.random.fold_in(own, 3), number_of)
    giver, receiver = mixed[0:number_of // 2 * 2:2], mixed[1:number_of // 2 * 2:2]
    slack = jnp.minimum(lengths[giver] - 1, bound - lengths[receiver]) // 2
    slack = jnp.where((giver == sequence[0]) | (receiver == sequence[0]) | (lengths[receiver] == 0), 0, jnp.maximum(slack, 0))
    passed = jax.random.randint(jax.random.fold_in(own, 4), (number_of // 2,), 0, 1 << 20) % (slack + 1)
    lengths = lengths.at[giver].add(-passed).at[receiver].add(passed)
    labels = jnp.searchsorted(jnp.cumsum(lengths), jnp.arange(rows * top), side="right").astype(jnp.int32)
    listing = labels.reshape(top, rows).T
    listing = listing[jax.random.permutation(jax.random.fold_in(own, 1), rows)]
    rotation = jax.random.randint(jax.random.fold_in(own, 2), (rows, 1), 0, top)
    return jnp.take_along_axis(listing, (jnp.arange(top)[None, :] + rotation) % top, axis=1)


def shares(number_of, total, bound, lean, full):
    loads = [(1 << 20) // math.isqrt(rank ** lean) + 1 for rank in range(1, number_of + 1)]
    largest = bound if full else min(bound, max(-(-total // number_of), total * loads[0] // sum(loads)))
    least = 1 if total - largest >= number_of - 1 else 0
    counts, rest = [largest] + [least] * (number_of - 1), total - largest - least * (number_of - 1)
    while rest > 0:
        free = [i for i in range(1, number_of) if counts[i] < largest] or [i for i in range(1, number_of) if counts[i] < bound]
        mass, remaining = sum([loads[i] for i in free]), rest
        for i in free:
            extra = min(bound - counts[i], max(1, remaining * loads[i] // mass), rest)
            counts[i] = counts[i] + extra
            rest = rest - extra
    return np.array(counts)


def centred(stream_key, extent, width, bound, cuts=(), kind=jnp.bfloat16):
    array = jax.random.normal(stream_key, extent, jnp.float32) * width
    if len(cuts) > 0:
        array = block_scale(stream_key, extent, cuts, -0.22, 0.18) * array
    return jnp.clip(array, min=-bound, max=bound).astype(kind)


def setup_inputs(seed: int = 0) -> dict:
    key_list = jax.random.split(jax.random.key(seed), 16)
    stream = centred(key_list[0], (TOKENS, MODEL_DIMENSION), 1.0, 6.0, ((0, 8),))
    attention_projection_weight = centred(key_list[1], (3, ATTENTION_HEADS * HEAD_SIZE, MODEL_DIMENSION), MODEL_DIMENSION ** -0.5, 0.125, ((1, 4),))
    head_output_weight = centred(key_list[2], (ATTENTION_HEADS * HEAD_SIZE, MODEL_DIMENSION), (ATTENTION_HEADS * HEAD_SIZE) ** -0.5, 0.125, ((0, 4),))
    adapter_down_maps = centred(key_list[3], (ADAPTER_TOTAL, MODEL_DIMENSION, ADAPTER_RANK), MODEL_DIMENSION ** -0.5, 0.125, ((0, 4),))
    adapter_up_maps = centred(key_list[4], (2, ATTENTION_HEADS * HEAD_SIZE, ADAPTER_TOTAL * ADAPTER_RANK), ADAPTER_RANK ** -0.5, 1.5, ((1, 4),))
    tenant_adapter_scale = jnp.clip(jnp.exp(jax.random.uniform(key_list[5], (TENANTS,), jnp.float32, math.log(0.5), math.log(2.0))), 0.5, 2.0)
    feedforward_norm_gain = jnp.clip(1.0 + 0.18 * jax.random.normal(key_list[6], (MODEL_DIMENSION,), jnp.float32), 0.099609375, 1.8984375).astype(jnp.bfloat16)
    feedforward_weight = centred(key_list[7], (3, MODEL_DIMENSION, FF), MODEL_DIMENSION ** -0.5, 0.125, ((1, 8), (2, 4)))
    prefix_cache_store = draw_prefix_cache_store(jax.random.fold_in(key_list[15], 71), 0)
    token_adapter_index = with_ends(jax.random.randint(key_list[9], (TOKENS,), 0, ADAPTER_TOTAL), jax.random.fold_in(key_list[9], 1), 0, ADAPTER_TOTAL - 1).astype(jnp.int32)
    request_token_lengths = jax.vmap(lambda own: ragged_sizes(own, REQ_DEV, TOKEN_SLOTS, MOST_LEN, 2))(jax.random.split(key_list[10], N_REQ)).reshape((N_REQ, REQ_DEV)).astype(jnp.int32)
    request_tenant_index = with_ends(jax.random.randint(key_list[11], (REQS,), 0, TENANTS), jax.random.fold_in(key_list[11], 1), 0, TENANTS - 1).astype(jnp.int32)
    last_page_holder_keys = jax.random.split(jax.random.fold_in(key_list[12], 1), REQS // REQ_DEV)
    last_page_holder_turns = jax.random.permutation(jax.random.fold_in(key_list[12], 3), REQS // REQ_DEV)
    last_page_holder = jax.vmap(lambda own, number: deal_out(jax.random.fold_in(key_list[12], 2), own, number, REQ_DEV, N_REQ, 1, CAP, 2))(last_page_holder_keys, last_page_holder_turns).reshape((REQS, 1))
    holder_page_slot = with_ends(jax.random.randint(key_list[13], (REQS,), 0, POOL_DEV), jax.random.fold_in(key_list[13], 1), 0, POOL_DEV - 1).astype(jnp.int32)
    page_filled_rows = with_ends(jax.random.randint(key_list[14], (REQS,), WINDOW, PAGE + 1), jax.random.fold_in(key_list[14], 1), WINDOW, PAGE).astype(jnp.int32)
    return dict(stream=stream, attention_projection_weight=attention_projection_weight, head_output_weight=head_output_weight, adapter_down_maps=adapter_down_maps, adapter_up_maps=adapter_up_maps, tenant_adapter_scale=tenant_adapter_scale, feedforward_norm_gain=feedforward_norm_gain, feedforward_weight=feedforward_weight, prefix_cache_store=prefix_cache_store, token_adapter_index=token_adapter_index, request_token_lengths=request_token_lengths, request_tenant_index=request_tenant_index, last_page_holder=last_page_holder, holder_page_slot=holder_page_slot, page_filled_rows=page_filled_rows)


def fetch_rows(prefix_cache_store, page_index, fill_rows):
    zero_index = jnp.zeros((), jnp.int32)
    block_rows = lax.dynamic_slice(prefix_cache_store, (page_index, zero_index, zero_index, fill_rows - WINDOW), (1, 2, ATTENTION_HEADS * HEAD_SIZE, WINDOW))
    return jnp.transpose(block_rows[0], (2, 0, 1))

def reference(stream, attention_projection_weight, head_output_weight, adapter_down_maps, adapter_up_maps, tenant_adapter_scale, feedforward_norm_gain, feedforward_weight, prefix_cache_store, token_adapter_index, request_token_lengths, request_tenant_index, last_page_holder, holder_page_slot, page_filled_rows):
    head_column_set = ATTENTION_HEADS * HEAD_SIZE
    owners = last_page_holder[:, 0].astype(jnp.int32)
    page_index = (owners * POOL_DEV + holder_page_slot).astype(jnp.int32)
    prefix_all = jax.vmap(lambda one_page, fill_rows: fetch_rows(prefix_cache_store, one_page, fill_rows))(page_index, page_filled_rows.astype(jnp.int32))
    down_flattened = jnp.transpose(adapter_down_maps, (1, 0, 2)).reshape(MODEL_DIMENSION, ADAPTER_TOTAL * ADAPTER_RANK)
    up_flattened = jnp.transpose(adapter_up_maps.reshape(2 * head_column_set, ADAPTER_TOTAL * ADAPTER_RANK))
    attn_f32 = attention_projection_weight.astype(jnp.float32)
    out_groups = head_output_weight.astype(jnp.float32).reshape(N_MDL, head_column_set // N_MDL, MODEL_DIMENSION)
    down_groups = feedforward_weight[2].astype(jnp.float32).reshape(MODEL_DIMENSION, N_MDL, FF // N_MDL)
    inv_scale = 1.0 / math.sqrt(HEAD_SIZE)

    def group_layer(group):
        first_row = group * TOKEN_SLOTS
        tokens = lax.dynamic_slice_in_dim(stream, first_row, TOKEN_SLOTS, 0)
        tok_adapters = lax.dynamic_slice_in_dim(token_adapter_index, first_row, TOKEN_SLOTS, 0)
        lengths_row = lax.dynamic_slice_in_dim(request_token_lengths, group, 1, 0)[0]
        tenants = lax.dynamic_slice_in_dim(request_tenant_index, group * REQ_DEV, REQ_DEV, 0)
        prefix = lax.dynamic_slice_in_dim(prefix_all, group * REQ_DEV, REQ_DEV, 0)
        projected_rows = jnp.einsum('td,kcd->ktc', tokens.astype(jnp.float32), attn_f32)
        onehot = tok_adapters[:, None] == jnp.arange(ADAPTER_TOTAL, dtype=jnp.int32)[None, :]
        rank_all = jnp.dot(tokens, down_flattened, preferred_element_type=jnp.float32).reshape(TOKEN_SLOTS, ADAPTER_TOTAL, ADAPTER_RANK)
        rank_feat = lax.optimization_barrier(jnp.sum(rank_all * onehot.astype(jnp.float32)[:, :, None], axis=1)).astype(jnp.bfloat16)
        broadcast_result = (onehot.astype(jnp.bfloat16)[:, :, None] * rank_feat[:, None, :]).reshape(TOKEN_SLOTS, ADAPTER_TOTAL * ADAPTER_RANK)
        adapter_column_set = jnp.dot(broadcast_result, up_flattened, preferred_element_type=jnp.float32).reshape(TOKEN_SLOTS, 2, head_column_set)
        positions = jnp.arange(TOKEN_SLOTS, dtype=jnp.int32)
        starts = jnp.cumsum(lengths_row) - lengths_row
        member = (positions[:, None] >= starts[None, :]) & (positions[:, None] < (starts + lengths_row)[None, :])
        member_int = member.astype(jnp.int32)
        request_of = lax.optimization_barrier(jnp.sum(member_int * jnp.arange(REQ_DEV, dtype=jnp.int32)[None, :], axis=1))
        relative = positions - lax.optimization_barrier(jnp.sum(member_int * starts[None, :], axis=1))
        request_scale = tenant_adapter_scale[tenants]
        per_token_scale = lax.optimization_barrier(jnp.sum(member.astype(jnp.float32) * request_scale[None, :], axis=1))[:, None]
        query_rows = (projected_rows[0] + per_token_scale * adapter_column_set[:, 0]).astype(jnp.bfloat16)
        key_rows = projected_rows[1].astype(jnp.bfloat16)
        value_row_block = (projected_rows[2] + per_token_scale * adapter_column_set[:, 1]).astype(jnp.bfloat16)
        key_all = jnp.concatenate([key_rows, prefix[:, :, 0].reshape(REQ_DEV * WINDOW, head_column_set)], axis=0)
        value_all = jnp.concatenate([value_row_block, prefix[:, :, 1].reshape(REQ_DEV * WINDOW, head_column_set)], axis=0)
        distance = positions[:, None] - positions[None, :]
        local_ok = (request_of[:, None] == request_of[None, :]) & (distance >= 0) & (distance <= WINDOW)
        key_request = jnp.repeat(jnp.arange(REQ_DEV, dtype=jnp.int32), WINDOW)
        key_offset = jnp.tile(jnp.arange(WINDOW, dtype=jnp.int32), REQ_DEV)
        prefix_ok = (request_of[:, None] == key_request[None, :]) & (key_offset[None, :] >= relative[:, None])
        allowed = jnp.concatenate([local_ok, prefix_ok], axis=1)
        query_heads = query_rows.astype(jnp.float32).reshape(TOKEN_SLOTS, ATTENTION_HEADS, HEAD_SIZE)
        key_heads = key_all.astype(jnp.float32).reshape(-1, ATTENTION_HEADS, HEAD_SIZE)
        value_heads = value_all.astype(jnp.float32).reshape(-1, ATTENTION_HEADS, HEAD_SIZE)
        scores = jnp.einsum('thd,shd->hts', query_heads, key_heads) * inv_scale
        masked = jnp.where(allowed[None], scores, -1e+30)
        row_max = lax.optimization_barrier(jnp.max(masked, axis=-1, keepdims=True))
        exp_scores = jnp.exp(masked - row_max)
        weights = (exp_scores / lax.optimization_barrier(jnp.sum(exp_scores, axis=-1, keepdims=True))).astype(jnp.bfloat16)
        mixed = jnp.einsum('hts,shd->thd', weights.astype(jnp.float32), value_heads).astype(jnp.bfloat16)
        mixed_groups = mixed.reshape(TOKEN_SLOTS, N_MDL, head_column_set // N_MDL).astype(jnp.float32)
        attn_parts = jnp.einsum('tgc,gcd->gtd', mixed_groups, out_groups).astype(jnp.bfloat16)
        attn = lax.optimization_barrier(jnp.sum(attn_parts.astype(jnp.float32), axis=0))
        resid = (tokens.astype(jnp.float32) + attn).astype(jnp.bfloat16)
        resid32 = resid.astype(jnp.float32)
        mean_sq = lax.optimization_barrier(jnp.mean(resid32 * resid32, axis=1, keepdims=True))
        normed = (resid32 * lax.rsqrt(mean_sq + 1e-06) * feedforward_norm_gain.astype(jnp.float32)[None, :]).astype(jnp.bfloat16)
        gate_part = jnp.dot(normed, feedforward_weight[0], preferred_element_type=jnp.float32)
        up_part = jnp.dot(normed, feedforward_weight[1], preferred_element_type=jnp.float32)
        hidden = (jax.nn.silu(gate_part) * up_part).astype(jnp.bfloat16)
        hidden_groups = hidden.reshape(TOKEN_SLOTS, N_MDL, FF // N_MDL).astype(jnp.float32)
        mlp_parts = jnp.einsum('tgf,dgf->gtd', hidden_groups, down_groups).astype(jnp.bfloat16)
        mlp_sum = lax.optimization_barrier(jnp.sum(mlp_parts.astype(jnp.float32), axis=0))
        return (resid32 + mlp_sum).astype(jnp.bfloat16)
    outputs = lax.map(group_layer, jnp.arange(N_REQ, dtype=jnp.int32))
    return outputs.reshape(N_REQ * TOKEN_SLOTS, MODEL_DIMENSION)
```

```python
import functools
import math

import jax
import jax.numpy as jnp
from jax import lax
from jax.experimental import pallas as pl
from jax.experimental.pallas import tpu as pltpu
from jax.sharding import PartitionSpec as P

HEAD_SIZE = 112
WINDOW = 64
BLOCK = 256
HALO = 128
VMEM_LIMIT = 48 * 1024 * 1024
NT = (((1,), (1,)), ((), ()))


def pack_kernel(cap, table_ref, offset_ref, *refs):
    page_refs, out_ref = refs[:cap], refs[cap]
    dest = pl.program_id(0)
    lane = lax.broadcasted_iota(jnp.int32, out_ref.shape[3:], 1)
    for pair in range(cap // 2):
        first = offset_ref[dest * cap + 2 * pair]
        second = offset_ref[dest * cap + 2 * pair + 1]
        for part in range(2):
            left = page_refs[2 * pair][0, part].astype(jnp.float32)
            right = page_refs[2 * pair + 1][0, part].astype(jnp.float32)
            left = pltpu.roll(left, lax.rem(2 * WINDOW - first, 2 * WINDOW), 1)
            right = pltpu.roll(right, WINDOW - second, 1)
            out_ref[0, pair, part] = jnp.where(lane < WINDOW, left, right).astype(out_ref.dtype)


def pack_windows(pages, table, offsets, cap):
    parts = pages.shape[1:]
    dests = table.shape[0]

    def page_spec(place):
        return pl.BlockSpec(
            (1,) + parts, lambda dest, tbl, off: (tbl[dest * cap + place], 0, 0, 0)
        )

    return pl.pallas_call(
        functools.partial(pack_kernel, cap),
        grid_spec=pltpu.PrefetchScalarGridSpec(
            num_scalar_prefetch=2,
            grid=(dests,),
            in_specs=[page_spec(place) for place in range(cap)],
            out_specs=pl.BlockSpec(
                (1, cap // 2) + parts, lambda dest, tbl, off: (dest, 0, 0, 0, 0)
            ),
        ),
        out_shape=jax.ShapeDtypeStruct((dests, cap // 2) + parts, pages.dtype),
        compiler_params=pltpu.CompilerParams(vmem_limit_bytes=VMEM_LIMIT),
        cost_estimate=pl.CostEstimate(
            flops=0, bytes_accessed=dests * cap * 3 * math.prod(parts), transcendentals=0
        ),
    )(table.reshape(-1), offsets.reshape(-1), *([pages] * cap))


def attention_kernel(
    query_ref, key_before_ref, key_ref, value_before_ref, value_ref, start_ref, slot_ref, prefix_ref,
    weight_ref, out_ref, mixed_ref,
):
    block = pl.program_id(0)
    pairs = prefix_ref.shape[0]
    heads = query_ref.shape[1] // HEAD_SIZE
    inv_scale = 1.0 / math.sqrt(HEAD_SIZE)
    start = start_ref[...]
    slot = slot_ref[...]
    own = block * BLOCK + lax.broadcasted_iota(jnp.int32, (BLOCK, 1), 0)
    other = block * BLOCK - HALO + lax.broadcasted_iota(jnp.int32, (1, HALO + BLOCK), 1)
    local_ok = (other >= jnp.maximum(start, own - WINDOW)) & (other <= own)
    lane = lax.broadcasted_iota(jnp.int32, (1, 2 * WINDOW), 1)
    pair_of = lax.shift_right_logical(slot, 1)
    lane_low = lax.bitwise_and(slot, 1) * WINDOW
    prefix_ok = (lane >= lane_low + (own - start)) & (lane < lane_low + WINDOW)
    in_pair = [jnp.broadcast_to(pair_of == pair, (BLOCK, 2 * WINDOW)) for pair in range(pairs)]
    for head in range(heads):
        columns = slice(head * HEAD_SIZE, (head + 1) * HEAD_SIZE)
        query = query_ref[:, columns]
        keys = jnp.concatenate([key_before_ref[:, columns], key_ref[:, columns]], axis=0)
        values = jnp.concatenate([value_before_ref[:, columns], value_ref[:, columns]], axis=0)
        local = lax.dot_general(query, keys, NT, preferred_element_type=jnp.float32)
        local = jnp.where(local_ok, local * inv_scale, -1e30)
        remote = jnp.zeros((BLOCK, 2 * WINDOW), jnp.float32)
        for pair in range(0, pairs, 2):
            wide = jnp.dot(
                query,
                jnp.concatenate([prefix_ref[pair, 0, columns], prefix_ref[pair + 1, 0, columns]], axis=1),
                preferred_element_type=jnp.float32,
            )
            remote = jnp.where(in_pair[pair], wide[:, : 2 * WINDOW], remote)
            remote = jnp.where(in_pair[pair + 1], wide[:, 2 * WINDOW :], remote)
        remote = jnp.where(prefix_ok, remote * inv_scale, -1e30)
        top = jnp.maximum(
            jnp.max(local, axis=1, keepdims=True), jnp.max(remote, axis=1, keepdims=True)
        )
        local = jnp.exp(local - top)
        remote = jnp.exp(remote - top)
        total = jnp.sum(local, axis=1, keepdims=True) + jnp.sum(remote, axis=1, keepdims=True)
        remote = remote.astype(jnp.bfloat16)
        spread = jnp.concatenate(
            [jnp.where(in_pair[pair], remote, jnp.zeros_like(remote)) for pair in range(pairs)], axis=1
        )
        held = jnp.concatenate([prefix_ref[pair, 1, columns] for pair in range(pairs)], axis=1)
        mixed = jnp.dot(local.astype(jnp.bfloat16), values, preferred_element_type=jnp.float32)
        mixed = mixed + lax.dot_general(spread, held, NT, preferred_element_type=jnp.float32)
        mixed_ref[:, columns] = (mixed * (1.0 / total)).astype(jnp.bfloat16)
    out_ref[...] = jnp.dot(
        mixed_ref[...], weight_ref[...], preferred_element_type=jnp.float32
    ).astype(out_ref.dtype)


def attention(query, key, value, start, slot, prefix, weight):
    tokens, width = query.shape
    model = weight.shape[1]
    step = BLOCK // HALO
    own = pl.BlockSpec((BLOCK, width), lambda i: (i, 0))
    before = pl.BlockSpec((HALO, width), lambda i: (jnp.maximum(i * step - 1, 0), 0))
    column = pl.BlockSpec((BLOCK, 1), lambda i: (i, 0))
    return pl.pallas_call(
        attention_kernel,
        grid=(tokens // BLOCK,),
        in_specs=[
            own, before, own, before, own, column, column,
            pl.BlockSpec(prefix.shape, lambda i: (0, 0, 0, 0)),
            pl.BlockSpec(weight.shape, lambda i: (0, 0)),
        ],
        out_specs=pl.BlockSpec((BLOCK, model), lambda i: (i, 0)),
        out_shape=jax.ShapeDtypeStruct((tokens, model), jnp.bfloat16),
        scratch_shapes=[pltpu.VMEM((BLOCK, width), jnp.bfloat16)],
        compiler_params=pltpu.CompilerParams(vmem_limit_bytes=VMEM_LIMIT),
        cost_estimate=pl.CostEstimate(
            flops=2 * tokens * width * (model + 2 * 2 * WINDOW * prefix.shape[0] + 2 * BLOCK),
            bytes_accessed=2 * (prefix.size + weight.size + tokens * model),
            transcendentals=0,
        ),
    )(query, key, key, value, value, start, slot, prefix, weight)


def per_device(
    stream,
    attention_projection_weight,
    head_output_weight,
    adapter_down_maps,
    adapter_up_maps,
    tenant_adapter_scale,
    feedforward_norm_gain,
    feedforward_weight,
    prefix_cache_store,
    token_adapter_index,
    request_token_lengths,
    request_tenant_index,
    last_page_holder,
    holder_page_slot,
    page_filled_rows,
):
    tok_count, model_width = stream.shape
    req_per_dev = request_token_lengths.shape[1]
    rank_total_width = adapter_down_maps.shape[2]
    adapter_number = adapter_up_maps.shape[2] // rank_total_width
    req_devices = lax.axis_size("req")
    req_index = lax.axis_index("req")
    mdl_index = lax.axis_index("mdl")
    row_share = tok_count // lax.axis_size("mdl")
    cap_slots = max(2, (req_per_dev + req_devices - 1) // req_devices + 1)
    cap_slots += cap_slots % 2

    order_ids = jnp.arange(req_per_dev, dtype=jnp.int32)
    owner_table = last_page_holder[:, 0].reshape(req_devices, req_per_dev)
    slot_table = holder_page_slot.reshape(req_devices, req_per_dev)
    offset_table = page_filled_rows.reshape(req_devices, req_per_dev) - WINDOW
    owned = (owner_table == req_index).astype(jnp.int32)
    earlier_one = (order_ids[:, None] > order_ids[None, :]).astype(jnp.int32)
    owned_rank = jnp.sum(owned[:, None, :] * earlier_one[None], axis=2)
    picked = owned[:, None, :] * (
        owned_rank[:, None, :] == jnp.arange(cap_slots, dtype=jnp.int32)[None, :, None]
    ).astype(jnp.int32)
    send_slot = jnp.sum(picked * slot_table[:, None, :], axis=2)
    send_offset = jnp.sum(picked * offset_table[:, None, :], axis=2)
    packed = pack_windows(prefix_cache_store, send_slot, send_offset, cap_slots)
    arrived = lax.all_to_all(packed, "req", split_axis=0, concat_axis=0, tiled=True)

    projected_rows = [
        lax.dot_general(
            stream, attention_projection_weight[k], NT, preferred_element_type=jnp.float32
        )
        for k in range(3)
    ]
    holder_count = adapter_down_maps.shape[0]
    holder_rank_rows = jnp.einsum(
        "qf,kfn->qkn", stream, adapter_down_maps, preferred_element_type=jnp.float32
    )
    held_onehot = (
        token_adapter_index[:, None]
        == (mdl_index * holder_count + jnp.arange(holder_count, dtype=jnp.int32))[None, :]
    )
    rank_part = jnp.sum(holder_rank_rows * held_onehot.astype(jnp.float32)[:, :, None], axis=1)
    rank_feat = lax.psum(rank_part.astype(jnp.bfloat16), "mdl")
    all_onehot = (
        token_adapter_index[:, None] == jnp.arange(adapter_number, dtype=jnp.int32)[None, :]
    )
    broadcast_result = (
        all_onehot.astype(jnp.bfloat16)[:, :, None] * rank_feat[:, None, :]
    ).reshape(tok_count, adapter_number * rank_total_width)
    lora_query = lax.dot_general(
        broadcast_result, adapter_up_maps[0], NT, preferred_element_type=jnp.float32
    )
    lora_value = lax.dot_general(
        broadcast_result, adapter_up_maps[1], NT, preferred_element_type=jnp.float32
    )

    positions = jnp.arange(tok_count, dtype=jnp.int32)
    lengths_row = request_token_lengths[0]
    ends = jnp.sum(
        jnp.where(order_ids[:, None] >= order_ids[None, :], lengths_row[None, :], 0), axis=1
    )
    starts = ends - lengths_row
    member = (positions[:, None] >= starts[None, :]) & (positions[:, None] < ends[None, :])
    member_int = member.astype(jnp.int32)
    start_of = jnp.sum(member_int * starts[None, :], axis=1, keepdims=True)
    my_owner = lax.dynamic_slice_in_dim(owner_table, req_index, 1, 0)[0]
    earlier = (my_owner[:, None] == my_owner[None, :]).astype(jnp.int32) * earlier_one
    slot_in = my_owner * cap_slots + jnp.sum(earlier, axis=1)
    slot_of = jnp.sum(member_int * slot_in[None, :], axis=1, keepdims=True)
    tenant_hot = (
        request_tenant_index[:, None]
        == jnp.arange(tenant_adapter_scale.shape[0], dtype=jnp.int32)[None, :]
    ).astype(jnp.float32)
    request_scale = jnp.sum(tenant_hot * tenant_adapter_scale[None, :], axis=1)
    per_token_scale = jnp.sum(member.astype(jnp.float32) * request_scale[None, :], axis=1)[:, None]
    query_rows = (projected_rows[0] + per_token_scale * lora_query).astype(jnp.bfloat16)
    key_rows = projected_rows[1].astype(jnp.bfloat16)
    value_rows = (projected_rows[2] + per_token_scale * lora_value).astype(jnp.bfloat16)

    attn_part = attention(
        query_rows, key_rows, value_rows, start_of, slot_of,
        arrived.reshape((-1,) + arrived.shape[2:]), head_output_weight,
    )

    gain_wide = feedforward_norm_gain.astype(jnp.float32)[None, :]
    attn_full = lax.psum(attn_part, "mdl").astype(jnp.float32)
    resid_full = (stream.astype(jnp.float32) + attn_full).astype(jnp.bfloat16)
    resid_wide = resid_full.astype(jnp.float32)
    mean_sq = jnp.mean(resid_wide * resid_wide, axis=1, keepdims=True)
    normed = (resid_wide * lax.rsqrt(mean_sq + 1e-06) * gain_wide).astype(jnp.bfloat16)
    resid_mine = lax.dynamic_slice_in_dim(resid_full, mdl_index * row_share, row_share, 0)
    full_mlp = lax.all_gather(feedforward_weight, "req", axis=1, tiled=True)
    gate_part = jnp.dot(normed, full_mlp[0], preferred_element_type=jnp.float32)
    up_part = jnp.dot(normed, full_mlp[1], preferred_element_type=jnp.float32)
    hidden = (jax.nn.silu(gate_part) * up_part).astype(jnp.bfloat16)
    mlp_part = jnp.einsum(
        "tf,df->td", hidden, full_mlp[2], preferred_element_type=jnp.float32
    ).astype(jnp.bfloat16)
    mlp_mine = lax.psum_scatter(mlp_part, "mdl", scatter_dimension=0, tiled=True)
    return (resid_mine.astype(jnp.float32) + mlp_mine.astype(jnp.float32)).astype(jnp.bfloat16)


def solution(mesh):
    return jax.shard_map(
        per_device,
        mesh=mesh,
        in_specs=(
            P("req", None),
            P(None, "mdl", None),
            P("mdl", None),
            P("mdl", None, None),
            P(None, "mdl", None),
            P(),
            P(),
            P(None, "req", "mdl"),
            P("req", None, "mdl", None),
            P("req"),
            P("req", None),
            P("req"),
            P(),
            P(),
            P(),
        ),
        out_specs=P(("req", "mdl"), None),
        check_vma=False,
    )
```

```python
import functools
import math

import jax
import jax.numpy as jnp
from jax import lax
from jax.experimental import pallas as pl
from jax.experimental.pallas import tpu as pltpu
from jax.sharding import PartitionSpec as P

HEAD_SIZE = 112
WINDOW = 64
BLOCK = 192
HALO = 64
LANES = 256
VMEM_LIMIT = 48 * 1024 * 1024
NT = (((1,), (1,)), ((), ()))


def pack_kernel(cap, table_ref, offset_ref, *refs):
    page_refs, out_ref = refs[:cap], refs[cap]
    dest = pl.program_id(0)
    lane = lax.broadcasted_iota(jnp.int32, out_ref.shape[3:], 1)
    for pair in range(cap // 2):
        first = offset_ref[dest * cap + 2 * pair]
        second = offset_ref[dest * cap + 2 * pair + 1]
        for part in range(2):
            left = page_refs[2 * pair][0, part].astype(jnp.float32)
            right = page_refs[2 * pair + 1][0, part].astype(jnp.float32)
            left = pltpu.roll(left, lax.rem(2 * WINDOW - first, 2 * WINDOW), 1)
            right = pltpu.roll(right, WINDOW - second, 1)
            out_ref[0, pair, part] = jnp.where(lane < WINDOW, left, right).astype(out_ref.dtype)


def pack_windows(pages, table, offsets, cap):
    parts = pages.shape[1:]
    dests = table.shape[0]

    def page_spec(place):
        return pl.BlockSpec(
            (1,) + parts, lambda dest, tbl, off: (tbl[dest * cap + place], 0, 0, 0)
        )

    return pl.pallas_call(
        functools.partial(pack_kernel, cap),
        grid_spec=pltpu.PrefetchScalarGridSpec(
            num_scalar_prefetch=2,
            grid=(dests,),
            in_specs=[page_spec(place) for place in range(cap)],
            out_specs=pl.BlockSpec(
                (1, cap // 2) + parts, lambda dest, tbl, off: (dest, 0, 0, 0, 0)
            ),
        ),
        out_shape=jax.ShapeDtypeStruct((dests, cap // 2) + parts, pages.dtype),
        compiler_params=pltpu.CompilerParams(vmem_limit_bytes=VMEM_LIMIT),
        cost_estimate=pl.CostEstimate(
            flops=0, bytes_accessed=dests * cap * 3 * math.prod(parts), transcendentals=0
        ),
    )(table.reshape(-1), offsets.reshape(-1), *([pages] * cap))


def attention_kernel(
    order_ref, query_ref, key_before_ref, key_ref, value_before_ref, value_ref, start_ref, slot_ref,
    prefix_ref, weight_ref, *out_refs,
):
    *out_refs, mixed_ref = out_refs
    step = pl.program_id(0)
    block = order_ref[step]
    pairs = prefix_ref.shape[0]
    heads = query_ref.shape[1] // HEAD_SIZE
    inv_scale = 1.0 / math.sqrt(HEAD_SIZE)
    start = start_ref[...]
    slot = slot_ref[...]
    own = block * BLOCK + lax.broadcasted_iota(jnp.int32, (BLOCK, 1), 0)
    other = block * BLOCK - HALO + lax.broadcasted_iota(jnp.int32, (1, HALO + BLOCK), 1)
    local_ok = (other >= jnp.maximum(start, own - WINDOW)) & (other <= own)
    lane = lax.broadcasted_iota(jnp.int32, (1, 2 * WINDOW), 1)
    pair_of = lax.shift_right_logical(slot, 1)
    lane_low = lax.bitwise_and(slot, 1) * WINDOW
    prefix_ok = (lane >= lane_low + (own - start)) & (lane < lane_low + WINDOW)
    in_pair = [jnp.broadcast_to(pair_of == pair, (BLOCK, 2 * WINDOW)) for pair in range(pairs)]
    for head in range(heads):
        columns = slice(head * HEAD_SIZE, (head + 1) * HEAD_SIZE)
        query = query_ref[:, columns]
        keys = jnp.concatenate([key_before_ref[:, columns], key_ref[:, columns]], axis=0)
        values = jnp.concatenate([value_before_ref[:, columns], value_ref[:, columns]], axis=0)
        local = lax.dot_general(query, keys, NT, preferred_element_type=jnp.float32)
        local = jnp.where(local_ok, local * inv_scale, -1e30)
        remote = jnp.zeros((BLOCK, 2 * WINDOW), jnp.float32)
        for pair in range(0, pairs, 2):
            wide = jnp.dot(
                query,
                jnp.concatenate([prefix_ref[pair, 0, columns], prefix_ref[pair + 1, 0, columns]], axis=1),
                preferred_element_type=jnp.float32,
            )
            remote = jnp.where(in_pair[pair], wide[:, : 2 * WINDOW], remote)
            remote = jnp.where(in_pair[pair + 1], wide[:, 2 * WINDOW :], remote)
        remote = jnp.where(prefix_ok, remote * inv_scale, -1e30)
        top = jnp.maximum(
            jnp.max(local, axis=1, keepdims=True), jnp.max(remote, axis=1, keepdims=True)
        )
        local = jnp.exp(local - top)
        remote = jnp.exp(remote - top)
        total = jnp.sum(local, axis=1, keepdims=True) + jnp.sum(remote, axis=1, keepdims=True)
        remote = remote.astype(jnp.bfloat16)
        spread = jnp.concatenate(
            [jnp.where(in_pair[pair], remote, jnp.zeros_like(remote)) for pair in range(pairs)], axis=1
        )
        held = jnp.concatenate([prefix_ref[pair, 1, columns] for pair in range(pairs)], axis=1)
        mixed = jnp.dot(local.astype(jnp.bfloat16), values, preferred_element_type=jnp.float32)
        mixed = mixed + lax.dot_general(spread, held, NT, preferred_element_type=jnp.float32)
        mixed_ref[:, columns] = (mixed * (1.0 / total)).astype(jnp.bfloat16)
    projected = jnp.dot(
        mixed_ref[...], weight_ref[...], preferred_element_type=jnp.float32
    ).astype(jnp.bfloat16)
    first = 0
    for out_ref in out_refs:
        span = out_ref.shape[0] // BLOCK

        @pl.when((step >= first) & (step < first + span))
        def _(out_ref=out_ref, first=first):
            rows = pl.multiple_of((step - first) * BLOCK, BLOCK)
            out_ref[pl.ds(rows, BLOCK), :] = projected

        first += span


def attention(order, spans, query, key, value, start, slot, prefix, weight):
    tokens, width = query.shape
    model = weight.shape[1]
    step = BLOCK // HALO
    own = pl.BlockSpec((BLOCK, width), lambda i, order: (order[i], 0))
    before = pl.BlockSpec((HALO, width), lambda i, order: (jnp.maximum(order[i] * step - 1, 0), 0))
    column = pl.BlockSpec((BLOCK, 1), lambda i, order: (order[i], 0))
    return pl.pallas_call(
        attention_kernel,
        grid_spec=pltpu.PrefetchScalarGridSpec(
            num_scalar_prefetch=1,
            grid=(tokens // BLOCK,),
            in_specs=[
                own, before, own, before, own, column, column,
                pl.BlockSpec(prefix.shape, lambda i, order: (0, 0, 0, 0)),
                pl.BlockSpec(weight.shape, lambda i, order: (0, 0)),
            ],
            out_specs=[pl.BlockSpec((span * BLOCK, model), lambda i, order: (0, 0)) for span in spans],
            scratch_shapes=[pltpu.VMEM((BLOCK, width), jnp.bfloat16)],
        ),
        out_shape=[jax.ShapeDtypeStruct((span * BLOCK, model), jnp.bfloat16) for span in spans],
        compiler_params=pltpu.CompilerParams(vmem_limit_bytes=VMEM_LIMIT),
        cost_estimate=pl.CostEstimate(
            flops=2 * tokens * width * (model + 2 * 2 * WINDOW * prefix.shape[0] + 2 * BLOCK),
            bytes_accessed=2 * (prefix.size + weight.size + tokens * model),
            transcendentals=0,
        ),
    )(order, query, key, key, value, value, start, slot, prefix, weight)


def line_gather(block, lines, rows_of_line):
    def hop(array, shift, low, high):
        pairs = []
        for line in range(low, high):
            for side in range(rows_of_line):
                pairs.append((line * rows_of_line + side, (line + shift) * rows_of_line + side))
        return lax.ppermute(array, "req", pairs)

    def swap(array, low, high):
        pairs = []
        for line in range(low, high):
            pairs += [(line * 2, line * 2 + 1), (line * 2 + 1, line * 2)]
        return lax.ppermute(array, "req", pairs)

    below, above = [block], [block]
    other_below = [swap(block, 0, lines)]
    other_above = [other_below[0]]
    for far in range(1, lines):
        below.append(hop(below[-1], 1, far - 1, lines - 1))
        above.append(hop(above[-1], -1, 1, lines - far + 1))
        other_below.append(swap(below[-1], far, lines))
        other_above.append(swap(above[-1], 0, lines - far))
    return (below, above), (other_below, other_above)


def piece_copies(lines, place_ref, pieces, halves, buffers, sems):
    line, side = place_ref[0], place_ref[1]
    jobs = []
    for column in range(2):
        below, above = pieces[column]
        for far in range(lines):
            origin = lax.rem(line - far + lines, lines) * 2 + (side if column == 0 else 1 - side)
            jobs.append((far, below[far], above[(lines - far) % lines], origin))

    def copies(source, origin, number):
        for half, buffer in enumerate(buffers):
            depth = source.shape[-2]
            rows = pl.multiple_of(origin * depth, depth)
            yield pltpu.make_async_copy(
                source.at[half] if halves else source,
                buffer.at[pl.ds(rows, depth), :],
                sems.at[number * len(buffers) + half],
            )

    def start():
        for number, (far, low, high, origin) in enumerate(jobs):
            if far == 0:
                for copy in copies(low, origin, number):
                    copy.start()
                continue

            @pl.when(line >= far)
            def _():
                for copy in copies(low, origin, number):
                    copy.start()

            @pl.when(line < far)
            def _():
                for copy in copies(high, origin, number):
                    copy.start()

    def wait():
        for number, (far, low, high, origin) in enumerate(jobs):
            for copy in copies(low, origin, number):
                copy.wait()

    return start, wait


def split_pieces(lines, refs):
    below, refs = list(refs[:lines]), refs[lines:]
    above, refs = [below[0]] + list(refs[: lines - 1]), refs[lines - 1 :]
    other_below, refs = list(refs[:lines]), refs[lines:]
    other_above, refs = [other_below[0]] + list(refs[: lines - 1]), refs[lines - 1 :]
    return ((below, above), (other_below, other_above)), refs


def join_pieces(pieces):
    (below, above), (other_below, other_above) = pieces
    return below + above[1:] + other_below + other_above[1:]


def hidden_kernel(lines, place_ref, *refs):
    pieces, refs = split_pieces(lines, refs)
    *block_refs, hidden_ref, all_ref, gate_ref, up_ref, sems = refs
    start, wait = piece_copies(lines, place_ref, pieces, True, (gate_ref, up_ref), sems)
    start()
    for number, block_ref in enumerate(block_refs):
        rows = block_ref.shape[0]
        all_ref[number * rows : (number + 1) * rows, :] = block_ref[...]
    wait()
    width = hidden_ref.shape[1]

    def tile(columns):
        gate = jnp.dot(all_ref[...], gate_ref[:, columns], preferred_element_type=jnp.float32)
        up = jnp.dot(all_ref[...], up_ref[:, columns], preferred_element_type=jnp.float32)
        hidden_ref[:, columns] = (gate / (1.0 + jnp.exp(-gate)) * up).astype(jnp.bfloat16)

    whole = width // LANES

    @pl.loop(0, whole)
    def _(step):
        tile(pl.ds(pl.multiple_of(step * LANES, LANES), LANES))

    if width % LANES:
        tile(slice(whole * LANES, width))


def hidden_units(place, lines, pieces, blocks):
    arrays = join_pieces(pieces)
    width = arrays[0].shape[2]
    tokens = sum(block.shape[0] for block in blocks)
    model = blocks[0].shape[1]
    smem = pl.BlockSpec(memory_space=pltpu.SMEM)
    vmem = pl.BlockSpec(memory_space=pltpu.VMEM)
    anywhere = pl.BlockSpec(memory_space=pl.ANY)
    return pl.pallas_call(
        functools.partial(hidden_kernel, lines),
        in_specs=[smem] + [anywhere] * len(arrays) + [vmem] * len(blocks),
        out_specs=vmem,
        out_shape=jax.ShapeDtypeStruct((tokens, width), jnp.bfloat16),
        scratch_shapes=[
            pltpu.VMEM((tokens, model), jnp.bfloat16),
            pltpu.VMEM((model, width), jnp.bfloat16),
            pltpu.VMEM((model, width), jnp.bfloat16),
            pltpu.SemaphoreType.DMA((4 * lines,)),
        ],
        compiler_params=pltpu.CompilerParams(vmem_limit_bytes=VMEM_LIMIT),
        cost_estimate=pl.CostEstimate(
            flops=4 * tokens * model * width, bytes_accessed=4 * model * width, transcendentals=0
        ),
    )(place, *arrays, *blocks)


def down_kernel(lines, place_ref, *refs):
    pieces, refs = split_pieces(lines, refs)
    hidden_ref, own_ref, send_ref, keep_ref, down_ref, sems = refs
    start, wait = piece_copies(lines, place_ref, pieces, False, (down_ref,), sems)
    start()
    wait()
    rows = own_ref.shape[0]

    @pl.loop(0, own_ref.shape[1] // LANES)
    def _(step):
        columns = pl.ds(pl.multiple_of(step * LANES, LANES), LANES)
        part = lax.dot_general(
            hidden_ref[...], down_ref[columns, :], NT, preferred_element_type=jnp.float32
        ).astype(jnp.bfloat16)
        own_ref[:, columns] = part[:rows]
        send_ref[:rows, columns] = part[rows : 2 * rows]
        keep_ref[:, columns] = part[2 * rows : 3 * rows]
        send_ref[rows:, columns] = part[3 * rows :]


def down_sums(place, lines, pieces, hidden):
    arrays = join_pieces(pieces)
    tokens, width = hidden.shape
    model = arrays[0].shape[0] * 2 * lines
    share = tokens // 4
    smem = pl.BlockSpec(memory_space=pltpu.SMEM)
    vmem = pl.BlockSpec(memory_space=pltpu.VMEM)
    anywhere = pl.BlockSpec(memory_space=pl.ANY)
    return pl.pallas_call(
        functools.partial(down_kernel, lines),
        in_specs=[smem] + [anywhere] * len(arrays) + [vmem],
        out_specs=[vmem] * 3,
        out_shape=[
            jax.ShapeDtypeStruct((rows, model), jnp.bfloat16) for rows in (share, 2 * share, share)
        ],
        scratch_shapes=[
            pltpu.VMEM((model, width), jnp.bfloat16),
            pltpu.SemaphoreType.DMA((2 * lines,)),
        ],
        compiler_params=pltpu.CompilerParams(vmem_limit_bytes=VMEM_LIMIT),
        cost_estimate=pl.CostEstimate(
            flops=2 * tokens * model * width, bytes_accessed=2 * model * width, transcendentals=0
        ),
    )(place, *arrays, hidden)


def core_swap(array):
    return lax.ppermute(array, "mdl", [(0, 1), (1, 0), (2, 3), (3, 2)])


def chip_swap(array):
    return lax.ppermute(array, "mdl", [(0, 2), (2, 0), (1, 3), (3, 1)])


def scatter_sum(own, send, keep):
    wide = jnp.float32
    rows = own.shape[0]
    near = core_swap(send)
    far = chip_swap((keep.astype(wide) + near[rows:].astype(wide)).astype(keep.dtype))
    return own.astype(wide) + near[:rows].astype(wide) + far.astype(wide)


def normalise(resid, gain):
    wide = resid.astype(jnp.float32)
    mean_sq = jnp.mean(wide * wide, axis=1, keepdims=True)
    return (wide * lax.rsqrt(mean_sq + 1e-06) * gain.astype(jnp.float32)[None, :]).astype(jnp.bfloat16)


def per_device(
    stream,
    attention_projection_weight,
    head_output_weight,
    adapter_down_maps,
    adapter_up_maps,
    tenant_adapter_scale,
    feedforward_norm_gain,
    feedforward_weight,
    prefix_cache_store,
    token_adapter_index,
    request_token_lengths,
    request_tenant_index,
    last_page_holder,
    holder_page_slot,
    page_filled_rows,
):
    tok_count, model_width = stream.shape
    req_per_dev = request_token_lengths.shape[1]
    rank_total_width = adapter_down_maps.shape[2]
    adapter_number = adapter_up_maps.shape[2] // rank_total_width
    req_devices = lax.axis_size("req")
    req_index = lax.axis_index("req")
    mdl_index = lax.axis_index("mdl")
    row_share = tok_count // lax.axis_size("mdl")
    cap_slots = max(2, (req_per_dev + req_devices - 1) // req_devices + 1)
    cap_slots += cap_slots % 2

    order_ids = jnp.arange(req_per_dev, dtype=jnp.int32)
    owner_table = last_page_holder[:, 0].reshape(req_devices, req_per_dev)
    slot_table = holder_page_slot.reshape(req_devices, req_per_dev)
    offset_table = page_filled_rows.reshape(req_devices, req_per_dev) - WINDOW
    owned = (owner_table == req_index).astype(jnp.int32)
    earlier_one = (order_ids[:, None] > order_ids[None, :]).astype(jnp.int32)
    owned_rank = jnp.sum(owned[:, None, :] * earlier_one[None], axis=2)
    picked = owned[:, None, :] * (
        owned_rank[:, None, :] == jnp.arange(cap_slots, dtype=jnp.int32)[None, :, None]
    ).astype(jnp.int32)
    send_slot = jnp.sum(picked * slot_table[:, None, :], axis=2)
    send_offset = jnp.sum(picked * offset_table[:, None, :], axis=2)
    packed = pack_windows(prefix_cache_store, send_slot, send_offset, cap_slots)
    arrived = lax.all_to_all(packed, "req", split_axis=0, concat_axis=0, tiled=True)

    projected_rows = [
        lax.dot_general(
            stream, attention_projection_weight[k], NT, preferred_element_type=jnp.float32
        )
        for k in range(3)
    ]
    holder_count = adapter_down_maps.shape[0]
    holder_rank_rows = jnp.einsum(
        "qf,kfn->qkn", stream, adapter_down_maps, preferred_element_type=jnp.float32
    )
    held_onehot = (
        token_adapter_index[:, None]
        == (mdl_index * holder_count + jnp.arange(holder_count, dtype=jnp.int32))[None, :]
    )
    rank_part = jnp.sum(holder_rank_rows * held_onehot.astype(jnp.float32)[:, :, None], axis=1)
    rank_feat = lax.psum(rank_part.astype(jnp.bfloat16), "mdl")
    all_onehot = (
        token_adapter_index[:, None] == jnp.arange(adapter_number, dtype=jnp.int32)[None, :]
    )
    broadcast_result = (
        all_onehot.astype(jnp.bfloat16)[:, :, None] * rank_feat[:, None, :]
    ).reshape(tok_count, adapter_number * rank_total_width)
    lora_query = lax.dot_general(
        broadcast_result, adapter_up_maps[0], NT, preferred_element_type=jnp.float32
    )
    lora_value = lax.dot_general(
        broadcast_result, adapter_up_maps[1], NT, preferred_element_type=jnp.float32
    )

    positions = jnp.arange(tok_count, dtype=jnp.int32)
    lengths_row = request_token_lengths[0]
    ends = jnp.sum(
        jnp.where(order_ids[:, None] >= order_ids[None, :], lengths_row[None, :], 0), axis=1
    )
    starts = ends - lengths_row
    member = (positions[:, None] >= starts[None, :]) & (positions[:, None] < ends[None, :])
    member_int = member.astype(jnp.int32)
    start_of = jnp.sum(member_int * starts[None, :], axis=1, keepdims=True)
    my_owner = lax.dynamic_slice_in_dim(owner_table, req_index, 1, 0)[0]
    earlier = (my_owner[:, None] == my_owner[None, :]).astype(jnp.int32) * earlier_one
    slot_in = my_owner * cap_slots + jnp.sum(earlier, axis=1)
    slot_of = jnp.sum(member_int * slot_in[None, :], axis=1, keepdims=True)
    tenant_hot = (
        request_tenant_index[:, None]
        == jnp.arange(tenant_adapter_scale.shape[0], dtype=jnp.int32)[None, :]
    ).astype(jnp.float32)
    request_scale = jnp.sum(tenant_hot * tenant_adapter_scale[None, :], axis=1)
    per_token_scale = jnp.sum(member.astype(jnp.float32) * request_scale[None, :], axis=1)[:, None]
    query_rows = (projected_rows[0] + per_token_scale * lora_query).astype(jnp.bfloat16)
    key_rows = projected_rows[1].astype(jnp.bfloat16)
    value_rows = (projected_rows[2] + per_token_scale * lora_value).astype(jnp.bfloat16)

    prefix = arrived.reshape((-1,) + arrived.shape[2:])
    blocks = tok_count // BLOCK
    rows_held = feedforward_weight.shape[1]
    if lax.axis_size("mdl") == blocks == 4 and req_devices % 2 == 0 and rows_held % 16 == 0:
        lines = req_devices // 2
        gate_up = line_gather(feedforward_weight[:2], lines, 2)
        (below, above), (other_below, other_above) = gate_up
        down_block, below[-1], above[-1] = lax.optimization_barrier(
            (feedforward_weight[2], below[-1], above[-1])
        )
        down = line_gather(down_block, lines, 2)
        place = jnp.stack([req_index // 2, req_index % 2]).astype(jnp.int32)
        early = below[1:3] + above[1:3] + other_below[:2] + other_above[1:2]
        prefix, *early = lax.optimization_barrier([prefix] + early)
        below[1:3], above[1:3] = early[:2], early[2:4]
        other_below[:2], other_above[1:2] = early[4:6], early[6:7]
        order = jnp.stack([mdl_index ^ 1, mdl_index ^ 3, mdl_index ^ 2, mdl_index]).astype(jnp.int32)
        send, keep, own = attention(
            order, (2, 1, 1), query_rows, key_rows, value_rows, start_of, slot_of, prefix,
            head_output_weight,
        )
        stream_mine = lax.dynamic_slice_in_dim(stream, mdl_index * row_share, row_share, 0)
        resid = (stream_mine.astype(jnp.float32) + scatter_sum(own, send, keep)).astype(jnp.bfloat16)
        normed = normalise(resid, feedforward_norm_gain)
        across = chip_swap(normed)
        hidden = hidden_units(
            place, lines, gate_up, [normed, core_swap(normed), across, core_swap(across)]
        )
        own, send, keep = down_sums(place, lines, down, hidden)
        return (resid.astype(jnp.float32) + scatter_sum(own, send, keep)).astype(jnp.bfloat16)

    (attn_part,) = attention(
        jnp.arange(blocks, dtype=jnp.int32), (blocks,), query_rows, key_rows, value_rows, start_of,
        slot_of, prefix, head_output_weight,
    )
    attn_full = lax.psum(attn_part, "mdl").astype(jnp.float32)
    resid = (stream.astype(jnp.float32) + attn_full).astype(jnp.bfloat16)
    normed = normalise(resid, feedforward_norm_gain)
    resid_mine = lax.dynamic_slice_in_dim(resid, mdl_index * row_share, row_share, 0)
    full_mlp = lax.all_gather(feedforward_weight, "req", axis=1, tiled=True)
    gate_part = jnp.dot(normed, full_mlp[0], preferred_element_type=jnp.float32)
    up_part = jnp.dot(normed, full_mlp[1], preferred_element_type=jnp.float32)
    hidden = (jax.nn.silu(gate_part) * up_part).astype(jnp.bfloat16)
    mlp_part = lax.dot_general(
        hidden, full_mlp[2], NT, preferred_element_type=jnp.float32
    ).astype(jnp.bfloat16)
    mlp_mine = lax.psum_scatter(mlp_part, "mdl", scatter_dimension=0, tiled=True)
    return (resid_mine.astype(jnp.float32) + mlp_mine.astype(jnp.float32)).astype(jnp.bfloat16)


def solution(mesh):
    return jax.shard_map(
        per_device,
        mesh=mesh,
        in_specs=(
            P("req", None),
            P(None, "mdl", None),
            P("mdl", None),
            P("mdl", None, None),
            P(None, "mdl", None),
            P(),
            P(),
            P(None, "req", "mdl"),
            P("req", None, "mdl", None),
            P("req"),
            P("req", None),
            P("req"),
            P(),
            P(),
            P(),
        ),
        out_specs=P(("req", "mdl"), None),
        check_vma=False,
    )
```

```python
import functools
import math

import jax
import jax.numpy as jnp
from jax import lax
from jax.experimental import pallas as pl
from jax.experimental.pallas import tpu as pltpu
from jax.sharding import PartitionSpec as P

HEAD_SIZE = 112
WINDOW = 64
BLOCK = 192
HALO = 64
LANES = 256
VMEM_LIMIT = 48 * 1024 * 1024
NT = (((1,), (1,)), ((), ()))


def pack_kernel(cap, table_ref, offset_ref, *refs):
    page_refs, out_ref = refs[:cap], refs[cap]
    dest = pl.program_id(0)
    lane = lax.broadcasted_iota(jnp.int32, out_ref.shape[3:], 1)
    for pair in range(cap // 2):
        first = offset_ref[dest * cap + 2 * pair]
        second = offset_ref[dest * cap + 2 * pair + 1]
        for part in range(2):
            left = page_refs[2 * pair][0, part].astype(jnp.float32)
            right = page_refs[2 * pair + 1][0, part].astype(jnp.float32)
            left = pltpu.roll(left, lax.rem(2 * WINDOW - first, 2 * WINDOW), 1)
            right = pltpu.roll(right, WINDOW - second, 1)
            out_ref[0, pair, part] = jnp.where(lane < WINDOW, left, right).astype(out_ref.dtype)


def pack_windows(pages, table, offsets, cap):
    parts = pages.shape[1:]
    dests = table.shape[0]

    def page_spec(place):
        return pl.BlockSpec(
            (1,) + parts, lambda dest, tbl, off: (tbl[dest * cap + place], 0, 0, 0)
        )

    return pl.pallas_call(
        functools.partial(pack_kernel, cap),
        grid_spec=pltpu.PrefetchScalarGridSpec(
            num_scalar_prefetch=2,
            grid=(dests,),
            in_specs=[page_spec(place) for place in range(cap)],
            out_specs=pl.BlockSpec(
                (1, cap // 2) + parts, lambda dest, tbl, off: (dest, 0, 0, 0, 0)
            ),
        ),
        out_shape=jax.ShapeDtypeStruct((dests, cap // 2) + parts, pages.dtype),
        compiler_params=pltpu.CompilerParams(vmem_limit_bytes=VMEM_LIMIT),
        cost_estimate=pl.CostEstimate(
            flops=0, bytes_accessed=dests * cap * 3 * math.prod(parts), transcendentals=0
        ),
    )(table.reshape(-1), offsets.reshape(-1), *([pages] * cap))


def attention_kernel(
    order_ref, query_ref, key_before_ref, key_ref, value_before_ref, value_ref, start_ref, slot_ref,
    prefix_ref, weight_ref, *out_refs,
):
    *out_refs, mixed_ref = out_refs
    step = pl.program_id(0)
    block = order_ref[step]
    pairs = prefix_ref.shape[0]
    heads = query_ref.shape[1] // HEAD_SIZE
    inv_scale = 1.0 / math.sqrt(HEAD_SIZE)
    start = start_ref[...]
    slot = slot_ref[...]
    own = block * BLOCK + lax.broadcasted_iota(jnp.int32, (BLOCK, 1), 0)
    other = block * BLOCK - HALO + lax.broadcasted_iota(jnp.int32, (1, HALO + BLOCK), 1)
    local_ok = (other >= jnp.maximum(start, own - WINDOW)) & (other <= own)
    lane = lax.broadcasted_iota(jnp.int32, (1, 2 * WINDOW), 1)
    pair_of = lax.shift_right_logical(slot, 1)
    lane_low = lax.bitwise_and(slot, 1) * WINDOW
    prefix_ok = (lane >= lane_low + (own - start)) & (lane < lane_low + WINDOW)
    in_pair = [jnp.broadcast_to(pair_of == pair, (BLOCK, 2 * WINDOW)) for pair in range(pairs)]
    for head in range(heads):
        columns = slice(head * HEAD_SIZE, (head + 1) * HEAD_SIZE)
        query = query_ref[:, columns]
        keys = jnp.concatenate([key_before_ref[:, columns], key_ref[:, columns]], axis=0)
        values = jnp.concatenate([value_before_ref[:, columns], value_ref[:, columns]], axis=0)
        local = lax.dot_general(query, keys, NT, preferred_element_type=jnp.float32)
        local = jnp.where(local_ok, local * inv_scale, -1e30)
        remote = jnp.zeros((BLOCK, 2 * WINDOW), jnp.float32)
        for pair in range(0, pairs, 2):
            wide = jnp.dot(
                query,
                jnp.concatenate([prefix_ref[pair, 0, columns], prefix_ref[pair + 1, 0, columns]], axis=1),
                preferred_element_type=jnp.float32,
            )
            remote = jnp.where(in_pair[pair], wide[:, : 2 * WINDOW], remote)
            remote = jnp.where(in_pair[pair + 1], wide[:, 2 * WINDOW :], remote)
        remote = jnp.where(prefix_ok, remote * inv_scale, -1e30)
        top = jnp.maximum(
            jnp.max(local, axis=1, keepdims=True), jnp.max(remote, axis=1, keepdims=True)
        )
        local = jnp.exp(local - top)
        remote = jnp.exp(remote - top)
        total = jnp.sum(local, axis=1, keepdims=True) + jnp.sum(remote, axis=1, keepdims=True)
        remote = remote.astype(jnp.bfloat16)
        spread = jnp.concatenate(
            [jnp.where(in_pair[pair], remote, jnp.zeros_like(remote)) for pair in range(pairs)], axis=1
        )
        held = jnp.concatenate([prefix_ref[pair, 1, columns] for pair in range(pairs)], axis=1)
        mixed = jnp.dot(local.astype(jnp.bfloat16), values, preferred_element_type=jnp.float32)
        mixed = mixed + lax.dot_general(spread, held, NT, preferred_element_type=jnp.float32)
        mixed_ref[:, columns] = (mixed * (1.0 / total)).astype(jnp.bfloat16)
    projected = jnp.dot(
        mixed_ref[...], weight_ref[...], preferred_element_type=jnp.float32
    ).astype(jnp.bfloat16)
    first = 0
    for out_ref in out_refs:
        span = out_ref.shape[0] // BLOCK

        @pl.when((step >= first) & (step < first + span))
        def _(out_ref=out_ref, first=first):
            rows = pl.multiple_of((step - first) * BLOCK, BLOCK)
            out_ref[pl.ds(rows, BLOCK), :] = projected

        first += span


def attention(order, spans, query, key, value, start, slot, prefix, weight):
    tokens, width = query.shape
    model = weight.shape[1]
    step = BLOCK // HALO
    own = pl.BlockSpec((BLOCK, width), lambda i, order: (order[i], 0))
    before = pl.BlockSpec((HALO, width), lambda i, order: (jnp.maximum(order[i] * step - 1, 0), 0))
    column = pl.BlockSpec((BLOCK, 1), lambda i, order: (order[i], 0))
    return pl.pallas_call(
        attention_kernel,
        grid_spec=pltpu.PrefetchScalarGridSpec(
            num_scalar_prefetch=1,
            grid=(tokens // BLOCK,),
            in_specs=[
                own, before, own, before, own, column, column,
                pl.BlockSpec(prefix.shape, lambda i, order: (0, 0, 0, 0)),
                pl.BlockSpec(weight.shape, lambda i, order: (0, 0)),
            ],
            out_specs=[pl.BlockSpec((span * BLOCK, model), lambda i, order: (0, 0)) for span in spans],
            scratch_shapes=[pltpu.VMEM((BLOCK, width), jnp.bfloat16)],
        ),
        out_shape=[jax.ShapeDtypeStruct((span * BLOCK, model), jnp.bfloat16) for span in spans],
        compiler_params=pltpu.CompilerParams(vmem_limit_bytes=VMEM_LIMIT),
        cost_estimate=pl.CostEstimate(
            flops=2 * tokens * width * (model + 2 * 2 * WINDOW * prefix.shape[0] + 2 * BLOCK),
            bytes_accessed=2 * (prefix.size + weight.size + tokens * model),
            transcendentals=0,
        ),
    )(order, query, key, key, value, value, start, slot, prefix, weight)


def hidden_kernel(*refs):
    *block_refs, gate_ref, up_ref, hidden_ref, all_ref = refs

    @pl.when(pl.program_id(0) == 0)
    def _():
        for number, block_ref in enumerate(block_refs):
            rows = block_ref.shape[0]
            all_ref[number * rows : (number + 1) * rows, :] = block_ref[...]

    gate = jnp.dot(all_ref[...], gate_ref[...], preferred_element_type=jnp.float32)
    up = jnp.dot(all_ref[...], up_ref[...], preferred_element_type=jnp.float32)
    hidden_ref[...] = (gate / (1.0 + jnp.exp(-gate)) * up).astype(jnp.bfloat16)


def hidden_units(blocks, gate, up):
    tokens = sum(block.shape[0] for block in blocks)
    model, width = gate.shape
    columns = pl.BlockSpec((model, LANES), lambda i: (0, i))
    return pl.pallas_call(
        hidden_kernel,
        grid=(pl.cdiv(width, LANES),),
        in_specs=[pl.BlockSpec(block.shape, lambda i: (0, 0)) for block in blocks] + [columns] * 2,
        out_specs=pl.BlockSpec((tokens, LANES), lambda i: (0, i)),
        out_shape=jax.ShapeDtypeStruct((tokens, width), jnp.bfloat16),
        scratch_shapes=[pltpu.VMEM((tokens, model), jnp.bfloat16)],
        compiler_params=pltpu.CompilerParams(vmem_limit_bytes=VMEM_LIMIT),
        cost_estimate=pl.CostEstimate(
            flops=4 * tokens * model * width, bytes_accessed=4 * model * width, transcendentals=0
        ),
    )(*blocks, gate, up)


def down_kernel(hidden_ref, down_ref, own_ref, send_ref, keep_ref):
    rows = own_ref.shape[0]
    part = lax.dot_general(
        hidden_ref[...], down_ref[...], NT, preferred_element_type=jnp.float32
    ).astype(jnp.bfloat16)
    own_ref[...] = part[:rows]
    send_ref[:rows] = part[rows : 2 * rows]
    keep_ref[...] = part[2 * rows : 3 * rows]
    send_ref[rows:] = part[3 * rows :]


def down_sums(hidden, down):
    tokens, width = hidden.shape
    model = down.shape[0]
    share = tokens // 4
    spans = (share, 2 * share, share)
    return pl.pallas_call(
        down_kernel,
        grid=(model // LANES,),
        in_specs=[
            pl.BlockSpec((tokens, width), lambda i: (0, 0)),
            pl.BlockSpec((LANES, width), lambda i: (i, 0)),
        ],
        out_specs=[pl.BlockSpec((rows, LANES), lambda i: (0, i)) for rows in spans],
        out_shape=[jax.ShapeDtypeStruct((rows, model), jnp.bfloat16) for rows in spans],
        compiler_params=pltpu.CompilerParams(vmem_limit_bytes=VMEM_LIMIT),
        cost_estimate=pl.CostEstimate(
            flops=2 * tokens * model * width, bytes_accessed=2 * model * width, transcendentals=0
        ),
    )(hidden, down)


def core_swap(array):
    return lax.ppermute(array, "mdl", [(0, 1), (1, 0), (2, 3), (3, 2)])


def chip_swap(array):
    return lax.ppermute(array, "mdl", [(0, 2), (2, 0), (1, 3), (3, 1)])


def scatter_sum(own, send, keep):
    wide = jnp.float32
    rows = own.shape[0]
    near = core_swap(send)
    far = chip_swap((keep.astype(wide) + near[rows:].astype(wide)).astype(keep.dtype))
    return own.astype(wide) + near[:rows].astype(wide) + far.astype(wide)


def normalise(resid, gain):
    wide = resid.astype(jnp.float32)
    mean_sq = jnp.mean(wide * wide, axis=1, keepdims=True)
    return (wide * lax.rsqrt(mean_sq + 1e-06) * gain.astype(jnp.float32)[None, :]).astype(jnp.bfloat16)


def per_device(
    stream,
    attention_projection_weight,
    head_output_weight,
    adapter_down_maps,
    adapter_up_maps,
    tenant_adapter_scale,
    feedforward_norm_gain,
    feedforward_weight,
    prefix_cache_store,
    token_adapter_index,
    request_token_lengths,
    request_tenant_index,
    last_page_holder,
    holder_page_slot,
    page_filled_rows,
):
    tok_count, model_width = stream.shape
    req_per_dev = request_token_lengths.shape[1]
    rank_total_width = adapter_down_maps.shape[2]
    adapter_number = adapter_up_maps.shape[2] // rank_total_width
    req_devices = lax.axis_size("req")
    req_index = lax.axis_index("req")
    mdl_index = lax.axis_index("mdl")
    row_share = tok_count // lax.axis_size("mdl")
    cap_slots = max(2, (req_per_dev + req_devices - 1) // req_devices + 1)
    cap_slots += cap_slots % 2

    order_ids = jnp.arange(req_per_dev, dtype=jnp.int32)
    owner_table = last_page_holder[:, 0].reshape(req_devices, req_per_dev)
    slot_table = holder_page_slot.reshape(req_devices, req_per_dev)
    offset_table = page_filled_rows.reshape(req_devices, req_per_dev) - WINDOW
    owned = (owner_table == req_index).astype(jnp.int32)
    earlier_one = (order_ids[:, None] > order_ids[None, :]).astype(jnp.int32)
    owned_rank = jnp.sum(owned[:, None, :] * earlier_one[None], axis=2)
    picked = owned[:, None, :] * (
        owned_rank[:, None, :] == jnp.arange(cap_slots, dtype=jnp.int32)[None, :, None]
    ).astype(jnp.int32)
    send_slot = jnp.sum(picked * slot_table[:, None, :], axis=2)
    send_offset = jnp.sum(picked * offset_table[:, None, :], axis=2)
    packed = pack_windows(prefix_cache_store, send_slot, send_offset, cap_slots)
    arrived = lax.all_to_all(packed, "req", split_axis=0, concat_axis=0, tiled=True)

    projected_rows = [
        lax.dot_general(
            stream, attention_projection_weight[k], NT, preferred_element_type=jnp.float32
        )
        for k in range(3)
    ]
    holder_count = adapter_down_maps.shape[0]
    holder_rank_rows = jnp.einsum(
        "qf,kfn->qkn", stream, adapter_down_maps, preferred_element_type=jnp.float32
    )
    held_onehot = (
        token_adapter_index[:, None]
        == (mdl_index * holder_count + jnp.arange(holder_count, dtype=jnp.int32))[None, :]
    )
    rank_part = jnp.sum(holder_rank_rows * held_onehot.astype(jnp.float32)[:, :, None], axis=1)
    rank_feat = lax.psum(rank_part.astype(jnp.bfloat16), "mdl")
    all_onehot = (
        token_adapter_index[:, None] == jnp.arange(adapter_number, dtype=jnp.int32)[None, :]
    )
    broadcast_result = (
        all_onehot.astype(jnp.bfloat16)[:, :, None] * rank_feat[:, None, :]
    ).reshape(tok_count, adapter_number * rank_total_width)
    lora_query = lax.dot_general(
        broadcast_result, adapter_up_maps[0], NT, preferred_element_type=jnp.float32
    )
    lora_value = lax.dot_general(
        broadcast_result, adapter_up_maps[1], NT, preferred_element_type=jnp.float32
    )

    positions = jnp.arange(tok_count, dtype=jnp.int32)
    lengths_row = request_token_lengths[0]
    ends = jnp.sum(
        jnp.where(order_ids[:, None] >= order_ids[None, :], lengths_row[None, :], 0), axis=1
    )
    starts = ends - lengths_row
    member = (positions[:, None] >= starts[None, :]) & (positions[:, None] < ends[None, :])
    member_int = member.astype(jnp.int32)
    start_of = jnp.sum(member_int * starts[None, :], axis=1, keepdims=True)
    my_owner = lax.dynamic_slice_in_dim(owner_table, req_index, 1, 0)[0]
    earlier = (my_owner[:, None] == my_owner[None, :]).astype(jnp.int32) * earlier_one
    slot_in = my_owner * cap_slots + jnp.sum(earlier, axis=1)
    slot_of = jnp.sum(member_int * slot_in[None, :], axis=1, keepdims=True)
    tenant_hot = (
        request_tenant_index[:, None]
        == jnp.arange(tenant_adapter_scale.shape[0], dtype=jnp.int32)[None, :]
    ).astype(jnp.float32)
    request_scale = jnp.sum(tenant_hot * tenant_adapter_scale[None, :], axis=1)
    per_token_scale = jnp.sum(member.astype(jnp.float32) * request_scale[None, :], axis=1)[:, None]
    query_rows = (projected_rows[0] + per_token_scale * lora_query).astype(jnp.bfloat16)
    key_rows = projected_rows[1].astype(jnp.bfloat16)
    value_rows = (projected_rows[2] + per_token_scale * lora_value).astype(jnp.bfloat16)

    prefix = arrived.reshape((-1,) + arrived.shape[2:])
    blocks = tok_count // BLOCK
    if lax.axis_size("mdl") == blocks == 4:
        gate_full = lax.all_gather(feedforward_weight[0], "req", axis=0, tiled=True)
        prefix, gate_full, up_block = lax.optimization_barrier(
            (prefix, gate_full, feedforward_weight[1])
        )
        up_full = lax.all_gather(up_block, "req", axis=0, tiled=True)
        order = jnp.stack([mdl_index ^ 1, mdl_index ^ 3, mdl_index ^ 2, mdl_index]).astype(jnp.int32)
        send, keep, own = attention(
            order, (2, 1, 1), query_rows, key_rows, value_rows, start_of, slot_of, prefix,
            head_output_weight,
        )
        keep, up_full, down_block = lax.optimization_barrier(
            (keep, up_full, feedforward_weight[2])
        )
        stream_mine = lax.dynamic_slice_in_dim(stream, mdl_index * row_share, row_share, 0)
        resid = (stream_mine.astype(jnp.float32) + scatter_sum(own, send, keep)).astype(jnp.bfloat16)
        normed = normalise(resid, feedforward_norm_gain)
        down_full = lax.all_gather(down_block, "req", axis=0, tiled=True)
        across = chip_swap(normed)
        hidden = hidden_units(
            [normed, core_swap(normed), across, core_swap(across)], gate_full, up_full
        )
        own, send, keep = down_sums(hidden, down_full)
        return (resid.astype(jnp.float32) + scatter_sum(own, send, keep)).astype(jnp.bfloat16)

    (attn_part,) = attention(
        jnp.arange(blocks, dtype=jnp.int32), (blocks,), query_rows, key_rows, value_rows, start_of,
        slot_of, prefix, head_output_weight,
    )
    attn_full = lax.psum(attn_part, "mdl").astype(jnp.float32)
    resid = (stream.astype(jnp.float32) + attn_full).astype(jnp.bfloat16)
    normed = normalise(resid, feedforward_norm_gain)
    resid_mine = lax.dynamic_slice_in_dim(resid, mdl_index * row_share, row_share, 0)
    full_mlp = lax.all_gather(feedforward_weight, "req", axis=1, tiled=True)
    gate_part = jnp.dot(normed, full_mlp[0], preferred_element_type=jnp.float32)
    up_part = jnp.dot(normed, full_mlp[1], preferred_element_type=jnp.float32)
    hidden = (jax.nn.silu(gate_part) * up_part).astype(jnp.bfloat16)
    mlp_part = lax.dot_general(
        hidden, full_mlp[2], NT, preferred_element_type=jnp.float32
    ).astype(jnp.bfloat16)
    mlp_mine = lax.psum_scatter(mlp_part, "mdl", scatter_dimension=0, tiled=True)
    return (resid_mine.astype(jnp.float32) + mlp_mine.astype(jnp.float32)).astype(jnp.bfloat16)


def solution(mesh):
    return jax.shard_map(
        per_device,
        mesh=mesh,
        in_specs=(
            P("req", None),
            P(None, "mdl", None),
            P("mdl", None),
            P("mdl", None, None),
            P(None, "mdl", None),
            P(),
            P(),
            P(None, "req", "mdl"),
            P("req", None, "mdl", None),
            P("req"),
            P("req", None),
            P("req"),
            P(),
            P(),
            P(),
        ),
        out_specs=P(("req", "mdl"), None),
        check_vma=False,
    )
```

```python
import functools
import math

import jax
import jax.numpy as jnp
from jax import lax
from jax.experimental import pallas as pl
from jax.experimental.pallas import tpu as pltpu
from jax.sharding import PartitionSpec as P

HEAD_SIZE = 112
WINDOW = 64
BLOCK = 192
HALO = 64
LANES = 256
VMEM_LIMIT = 48 * 1024 * 1024
NT = (((1,), (1,)), ((), ()))


def pack_kernel(cap, table_ref, offset_ref, *refs):
    page_refs, out_ref = refs[:cap], refs[cap]
    dest = pl.program_id(0)
    lane = lax.broadcasted_iota(jnp.int32, out_ref.shape[3:], 1)
    for pair in range(cap // 2):
        first = offset_ref[dest * cap + 2 * pair]
        second = offset_ref[dest * cap + 2 * pair + 1]
        for part in range(2):
            left = page_refs[2 * pair][0, part].astype(jnp.float32)
            right = page_refs[2 * pair + 1][0, part].astype(jnp.float32)
            left = pltpu.roll(left, lax.rem(2 * WINDOW - first, 2 * WINDOW), 1)
            right = pltpu.roll(right, WINDOW - second, 1)
            out_ref[0, pair, part] = jnp.where(lane < WINDOW, left, right).astype(out_ref.dtype)


def pack_windows(pages, table, offsets, cap):
    parts = pages.shape[1:]
    dests = table.shape[0]

    def page_spec(place):
        return pl.BlockSpec(
            (1,) + parts, lambda dest, tbl, off: (tbl[dest * cap + place], 0, 0, 0)
        )

    return pl.pallas_call(
        functools.partial(pack_kernel, cap),
        grid_spec=pltpu.PrefetchScalarGridSpec(
            num_scalar_prefetch=2,
            grid=(dests,),
            in_specs=[page_spec(place) for place in range(cap)],
            out_specs=pl.BlockSpec(
                (1, cap // 2) + parts, lambda dest, tbl, off: (dest, 0, 0, 0, 0)
            ),
        ),
        out_shape=jax.ShapeDtypeStruct((dests, cap // 2) + parts, pages.dtype),
        compiler_params=pltpu.CompilerParams(vmem_limit_bytes=VMEM_LIMIT),
        cost_estimate=pl.CostEstimate(
            flops=0, bytes_accessed=dests * cap * 3 * math.prod(parts), transcendentals=0
        ),
    )(table.reshape(-1), offsets.reshape(-1), *([pages] * cap))


def attention_kernel(
    order_ref, query_ref, key_before_ref, key_ref, value_before_ref, value_ref, start_ref, slot_ref,
    prefix_ref, weight_ref, *out_refs,
):
    *out_refs, mixed_ref = out_refs
    step = pl.program_id(0)
    block = order_ref[step]
    pairs = prefix_ref.shape[0]
    heads = query_ref.shape[1] // HEAD_SIZE
    inv_scale = 1.0 / math.sqrt(HEAD_SIZE)
    start = start_ref[...]
    slot = slot_ref[...]
    own = block * BLOCK + lax.broadcasted_iota(jnp.int32, (BLOCK, 1), 0)
    other = block * BLOCK - HALO + lax.broadcasted_iota(jnp.int32, (1, HALO + BLOCK), 1)
    local_ok = (other >= jnp.maximum(start, own - WINDOW)) & (other <= own)
    lane = lax.broadcasted_iota(jnp.int32, (1, 2 * WINDOW), 1)
    pair_of = lax.shift_right_logical(slot, 1)
    lane_low = lax.bitwise_and(slot, 1) * WINDOW
    prefix_ok = (lane >= lane_low + (own - start)) & (lane < lane_low + WINDOW)
    in_pair = [jnp.broadcast_to(pair_of == pair, (BLOCK, 2 * WINDOW)) for pair in range(pairs)]
    for head in range(heads):
        columns = slice(head * HEAD_SIZE, (head + 1) * HEAD_SIZE)
        query = query_ref[:, columns]
        keys = jnp.concatenate([key_before_ref[:, columns], key_ref[:, columns]], axis=0)
        values = jnp.concatenate([value_before_ref[:, columns], value_ref[:, columns]], axis=0)
        local = lax.dot_general(query, keys, NT, preferred_element_type=jnp.float32)
        local = jnp.where(local_ok, local * inv_scale, -1e30)
        remote = jnp.zeros((BLOCK, 2 * WINDOW), jnp.float32)
        for pair in range(0, pairs, 2):
            wide = jnp.dot(
                query,
                jnp.concatenate([prefix_ref[pair, 0, columns], prefix_ref[pair + 1, 0, columns]], axis=1),
                preferred_element_type=jnp.float32,
            )
            remote = jnp.where(in_pair[pair], wide[:, : 2 * WINDOW], remote)
            remote = jnp.where(in_pair[pair + 1], wide[:, 2 * WINDOW :], remote)
        remote = jnp.where(prefix_ok, remote * inv_scale, -1e30)
        top = jnp.maximum(
            jnp.max(local, axis=1, keepdims=True), jnp.max(remote, axis=1, keepdims=True)
        )
        local = jnp.exp(local - top)
        remote = jnp.exp(remote - top)
        total = jnp.sum(local, axis=1, keepdims=True) + jnp.sum(remote, axis=1, keepdims=True)
        remote = remote.astype(jnp.bfloat16)
        spread = jnp.concatenate(
            [jnp.where(in_pair[pair], remote, jnp.zeros_like(remote)) for pair in range(pairs)], axis=1
        )
        held = jnp.concatenate([prefix_ref[pair, 1, columns] for pair in range(pairs)], axis=1)
        mixed = jnp.dot(local.astype(jnp.bfloat16), values, preferred_element_type=jnp.float32)
        mixed = mixed + lax.dot_general(spread, held, NT, preferred_element_type=jnp.float32)
        mixed_ref[:, columns] = (mixed * (1.0 / total)).astype(jnp.bfloat16)
    projected = jnp.dot(
        mixed_ref[...], weight_ref[...], preferred_element_type=jnp.float32
    ).astype(jnp.bfloat16)
    first = 0
    for out_ref in out_refs:
        span = out_ref.shape[0] // BLOCK

        @pl.when((step >= first) & (step < first + span))
        def _(out_ref=out_ref, first=first):
            rows = pl.multiple_of((step - first) * BLOCK, BLOCK)
            out_ref[pl.ds(rows, BLOCK), :] = projected

        first += span


def attention(order, spans, query, key, value, start, slot, prefix, weight):
    tokens, width = query.shape
    model = weight.shape[1]
    step = BLOCK // HALO
    own = pl.BlockSpec((BLOCK, width), lambda i, order: (order[i], 0))
    before = pl.BlockSpec((HALO, width), lambda i, order: (jnp.maximum(order[i] * step - 1, 0), 0))
    column = pl.BlockSpec((BLOCK, 1), lambda i, order: (order[i], 0))
    return pl.pallas_call(
        attention_kernel,
        grid_spec=pltpu.PrefetchScalarGridSpec(
            num_scalar_prefetch=1,
            grid=(tokens // BLOCK,),
            in_specs=[
                own, before, own, before, own, column, column,
                pl.BlockSpec(prefix.shape, lambda i, order: (0, 0, 0, 0)),
                pl.BlockSpec(weight.shape, lambda i, order: (0, 0)),
            ],
            out_specs=[pl.BlockSpec((span * BLOCK, model), lambda i, order: (0, 0)) for span in spans],
            scratch_shapes=[pltpu.VMEM((BLOCK, width), jnp.bfloat16)],
        ),
        out_shape=[jax.ShapeDtypeStruct((span * BLOCK, model), jnp.bfloat16) for span in spans],
        compiler_params=pltpu.CompilerParams(vmem_limit_bytes=VMEM_LIMIT),
        cost_estimate=pl.CostEstimate(
            flops=2 * tokens * width * (model + 2 * 2 * WINDOW * prefix.shape[0] + 2 * BLOCK),
            bytes_accessed=2 * (prefix.size + weight.size + tokens * model),
            transcendentals=0,
        ),
    )(order, query, key, key, value, value, start, slot, prefix, weight)


def hop(array, shift, low, high):
    pairs = [(2 * line + side, 2 * (line + shift) + side) for line in range(low, high) for side in range(2)]
    return lax.ppermute(array, "req", pairs)


def swap(array, low, high):
    pairs = [(2 * line + side, 2 * line + 1 - side) for line in range(low, high) for side in range(2)]
    return lax.ppermute(array, "req", pairs)


class Gather:
    def __init__(self, block, lines):
        self.lines = lines
        self.below, self.above = [block], [block]
        self.other_below, self.other_above = [], []

    def step(self):
        far = len(self.below)
        self.below.append(hop(self.below[-1], 1, far - 1, self.lines - 1))
        self.above.append(hop(self.above[-1], -1, 1, self.lines - far + 1))

    def share(self):
        far = len(self.other_below)
        self.other_below.append(swap(self.below[far], far, self.lines))
        self.other_above.append(swap(self.above[far], 0, self.lines - far) if far else self.other_below[0])

    def arrays(self):
        return [self.below, self.above, self.other_below, self.other_above]


def tie(gathers, *others):
    lists = [entry for gather in gathers for entry in gather.arrays()]
    flat, others = lax.optimization_barrier((lists, others))
    for entry, new in zip(lists, flat):
        entry[:] = new
    return others


def piece_copies(lines, place_ref, pieces, halves, buffers, sems, tiles):
    line, side = place_ref[0], place_ref[1]
    jobs = []
    for column in range(2):
        below, above = pieces[column]
        for far in range(lines):
            origin = lax.rem(line - far + lines, lines) * 2 + (side if column == 0 else 1 - side)
            jobs.append((far, below[far], above[(lines - far) % lines], origin))

    def copies(source, origin, number, tile):
        for half, buffer in enumerate(buffers):
            depth = source.shape[-2]
            rows = pl.multiple_of(origin * depth, depth)
            yield pltpu.make_async_copy(
                (source.at[half] if halves else source).at[:, tiles[tile]],
                buffer.at[pl.ds(rows, depth), tiles[tile]],
                sems.at[(tile * len(jobs) + number) * len(buffers) + half],
            )

    def start(tile):
        for number, (far, low, high, origin) in enumerate(jobs):
            if far == 0:
                for copy in copies(low, origin, number, tile):
                    copy.start()
                continue

            @pl.when(line >= far)
            def _():
                for copy in copies(low, origin, number, tile):
                    copy.start()

            @pl.when(line < far)
            def _():
                for copy in copies(high, origin, number, tile):
                    copy.start()

    def wait(tile):
        for number, (far, low, high, origin) in enumerate(jobs):
            for copy in copies(low, origin, number, tile):
                copy.wait()

    return start, wait


def column_tiles(width):
    return [slice(first, min(first + LANES, width)) for first in range(0, width, LANES)]


def split_pieces(lines, refs):
    below, refs = list(refs[:lines]), refs[lines:]
    above, refs = [below[0]] + list(refs[: lines - 1]), refs[lines - 1 :]
    other_below, refs = list(refs[:lines]), refs[lines:]
    other_above, refs = [other_below[0]] + list(refs[: lines - 1]), refs[lines - 1 :]
    return ((below, above), (other_below, other_above)), refs


def join_pieces(pieces):
    below, above, other_below, other_above = pieces
    return below + above[1:] + other_below + other_above[1:]


def hidden_kernel(lines, place_ref, *refs):
    pieces, refs = split_pieces(lines, refs)
    *block_refs, hidden_ref, all_ref, gate_ref, up_ref, sems = refs
    tiles = column_tiles(hidden_ref.shape[1])
    start, wait = piece_copies(lines, place_ref, pieces, True, (gate_ref, up_ref), sems, tiles)
    for tile in range(len(tiles)):
        start(tile)
    for number, block_ref in enumerate(block_refs):
        rows = block_ref.shape[0]
        all_ref[number * rows : (number + 1) * rows, :] = block_ref[...]
    for tile, columns in enumerate(tiles):
        wait(tile)
        gate = jnp.dot(all_ref[...], gate_ref[:, columns], preferred_element_type=jnp.float32)
        up = jnp.dot(all_ref[...], up_ref[:, columns], preferred_element_type=jnp.float32)
        hidden_ref[:, columns] = (gate / (1.0 + jnp.exp(-gate)) * up).astype(jnp.bfloat16)


def hidden_units(place, lines, pieces, blocks):
    arrays = join_pieces(pieces)
    width = arrays[0].shape[2]
    tokens = sum(block.shape[0] for block in blocks)
    model = blocks[0].shape[1]
    smem = pl.BlockSpec(memory_space=pltpu.SMEM)
    vmem = pl.BlockSpec(memory_space=pltpu.VMEM)
    anywhere = pl.BlockSpec(memory_space=pl.ANY)
    return pl.pallas_call(
        functools.partial(hidden_kernel, lines),
        in_specs=[smem] + [anywhere] * len(arrays) + [vmem] * len(blocks),
        out_specs=vmem,
        out_shape=jax.ShapeDtypeStruct((tokens, width), jnp.bfloat16),
        scratch_shapes=[
            pltpu.VMEM((tokens, model), jnp.bfloat16),
            pltpu.VMEM((model, width), jnp.bfloat16),
            pltpu.VMEM((model, width), jnp.bfloat16),
            pltpu.SemaphoreType.DMA((4 * lines * len(column_tiles(width)),)),
        ],
        compiler_params=pltpu.CompilerParams(vmem_limit_bytes=VMEM_LIMIT),
        cost_estimate=pl.CostEstimate(
            flops=4 * tokens * model * width, bytes_accessed=4 * model * width, transcendentals=0
        ),
    )(place, *arrays, *blocks)


def down_kernel(lines, place_ref, *refs):
    pieces, refs = split_pieces(lines, refs)
    hidden_ref, own_ref, send_ref, keep_ref, down_ref, sems = refs
    everything = [slice(0, hidden_ref.shape[1])]
    start, wait = piece_copies(lines, place_ref, pieces, False, (down_ref,), sems, everything)
    start(0)
    wait(0)
    rows = own_ref.shape[0]

    @pl.loop(0, own_ref.shape[1] // LANES)
    def _(step):
        columns = pl.ds(pl.multiple_of(step * LANES, LANES), LANES)
        part = lax.dot_general(
            hidden_ref[...], down_ref[columns, :], NT, preferred_element_type=jnp.float32
        ).astype(jnp.bfloat16)
        own_ref[:, columns] = part[:rows]
        send_ref[:rows, columns] = part[rows : 2 * rows]
        keep_ref[:, columns] = part[2 * rows : 3 * rows]
        send_ref[rows:, columns] = part[3 * rows :]


def down_sums(place, lines, pieces, hidden):
    arrays = join_pieces(pieces)
    tokens, width = hidden.shape
    model = arrays[0].shape[0] * 2 * lines
    share = tokens // 4
    smem = pl.BlockSpec(memory_space=pltpu.SMEM)
    vmem = pl.BlockSpec(memory_space=pltpu.VMEM)
    anywhere = pl.BlockSpec(memory_space=pl.ANY)
    return pl.pallas_call(
        functools.partial(down_kernel, lines),
        in_specs=[smem] + [anywhere] * len(arrays) + [vmem],
        out_specs=[vmem] * 3,
        out_shape=[
            jax.ShapeDtypeStruct((rows, model), jnp.bfloat16) for rows in (share, 2 * share, share)
        ],
        scratch_shapes=[
            pltpu.VMEM((model, width), jnp.bfloat16),
            pltpu.SemaphoreType.DMA((2 * lines,)),
        ],
        compiler_params=pltpu.CompilerParams(vmem_limit_bytes=VMEM_LIMIT),
        cost_estimate=pl.CostEstimate(
            flops=2 * tokens * model * width, bytes_accessed=2 * model * width, transcendentals=0
        ),
    )(place, *arrays, hidden)


def core_swap(array):
    return lax.ppermute(array, "mdl", [(0, 1), (1, 0), (2, 3), (3, 2)])


def chip_swap(array):
    return lax.ppermute(array, "mdl", [(0, 2), (2, 0), (1, 3), (3, 1)])


def scatter_sum(own, send, keep):
    wide = jnp.float32
    rows = own.shape[0]
    near = core_swap(send)
    far = chip_swap((keep.astype(wide) + near[rows:].astype(wide)).astype(keep.dtype))
    return own.astype(wide) + near[:rows].astype(wide) + far.astype(wide)


def normalise(resid, gain):
    wide = resid.astype(jnp.float32)
    mean_sq = jnp.mean(wide * wide, axis=1, keepdims=True)
    return (wide * lax.rsqrt(mean_sq + 1e-06) * gain.astype(jnp.float32)[None, :]).astype(jnp.bfloat16)


def per_device(
    stream,
    attention_projection_weight,
    head_output_weight,
    adapter_down_maps,
    adapter_up_maps,
    tenant_adapter_scale,
    feedforward_norm_gain,
    feedforward_weight,
    prefix_cache_store,
    token_adapter_index,
    request_token_lengths,
    request_tenant_index,
    last_page_holder,
    holder_page_slot,
    page_filled_rows,
):
    tok_count, model_width = stream.shape
    req_per_dev = request_token_lengths.shape[1]
    rank_total_width = adapter_down_maps.shape[2]
    adapter_number = adapter_up_maps.shape[2] // rank_total_width
    req_devices = lax.axis_size("req")
    req_index = lax.axis_index("req")
    mdl_index = lax.axis_index("mdl")
    row_share = tok_count // lax.axis_size("mdl")
    cap_slots = max(2, (req_per_dev + req_devices - 1) // req_devices + 1)
    cap_slots += cap_slots % 2

    order_ids = jnp.arange(req_per_dev, dtype=jnp.int32)
    owner_table = last_page_holder[:, 0].reshape(req_devices, req_per_dev)
    slot_table = holder_page_slot.reshape(req_devices, req_per_dev)
    offset_table = page_filled_rows.reshape(req_devices, req_per_dev) - WINDOW
    owned = (owner_table == req_index).astype(jnp.int32)
    earlier_one = (order_ids[:, None] > order_ids[None, :]).astype(jnp.int32)
    owned_rank = jnp.sum(owned[:, None, :] * earlier_one[None], axis=2)
    picked = owned[:, None, :] * (
        owned_rank[:, None, :] == jnp.arange(cap_slots, dtype=jnp.int32)[None, :, None]
    ).astype(jnp.int32)
    send_slot = jnp.sum(picked * slot_table[:, None, :], axis=2)
    send_offset = jnp.sum(picked * offset_table[:, None, :], axis=2)
    packed = pack_windows(prefix_cache_store, send_slot, send_offset, cap_slots)
    lines = req_devices // 2
    chained = (lines, lax.axis_size("mdl"), tok_count // BLOCK) == (4, 4, 4)
    if chained:
        gate_up, down = Gather(feedforward_weight[:2], lines), Gather(feedforward_weight[2], lines)
        gate_up.share()
        gate_up.step()
        (packed,) = tie([gate_up], packed)
        gate_up.step()
        gate_up.share()
        gate_up.step()
        gate_up.share()
    arrived = lax.all_to_all(packed, "req", split_axis=0, concat_axis=0, tiled=True)

    projected_rows = [
        lax.dot_general(
            stream, attention_projection_weight[k], NT, preferred_element_type=jnp.float32
        )
        for k in range(3)
    ]
    holder_count = adapter_down_maps.shape[0]
    holder_rank_rows = jnp.einsum(
        "qf,kfn->qkn", stream, adapter_down_maps, preferred_element_type=jnp.float32
    )
    held_onehot = (
        token_adapter_index[:, None]
        == (mdl_index * holder_count + jnp.arange(holder_count, dtype=jnp.int32))[None, :]
    )
    rank_part = jnp.sum(holder_rank_rows * held_onehot.astype(jnp.float32)[:, :, None], axis=1)
    rank_feat = lax.psum(rank_part.astype(jnp.bfloat16), "mdl")
    all_onehot = (
        token_adapter_index[:, None] == jnp.arange(adapter_number, dtype=jnp.int32)[None, :]
    )
    broadcast_result = (
        all_onehot.astype(jnp.bfloat16)[:, :, None] * rank_feat[:, None, :]
    ).reshape(tok_count, adapter_number * rank_total_width)
    lora_query = lax.dot_general(
        broadcast_result, adapter_up_maps[0], NT, preferred_element_type=jnp.float32
    )
    lora_value = lax.dot_general(
        broadcast_result, adapter_up_maps[1], NT, preferred_element_type=jnp.float32
    )

    positions = jnp.arange(tok_count, dtype=jnp.int32)
    lengths_row = request_token_lengths[0]
    ends = jnp.sum(
        jnp.where(order_ids[:, None] >= order_ids[None, :], lengths_row[None, :], 0), axis=1
    )
    starts = ends - lengths_row
    member = (positions[:, None] >= starts[None, :]) & (positions[:, None] < ends[None, :])
    member_int = member.astype(jnp.int32)
    start_of = jnp.sum(member_int * starts[None, :], axis=1, keepdims=True)
    my_owner = lax.dynamic_slice_in_dim(owner_table, req_index, 1, 0)[0]
    earlier = (my_owner[:, None] == my_owner[None, :]).astype(jnp.int32) * earlier_one
    slot_in = my_owner * cap_slots + jnp.sum(earlier, axis=1)
    slot_of = jnp.sum(member_int * slot_in[None, :], axis=1, keepdims=True)
    tenant_hot = (
        request_tenant_index[:, None]
        == jnp.arange(tenant_adapter_scale.shape[0], dtype=jnp.int32)[None, :]
    ).astype(jnp.float32)
    request_scale = jnp.sum(tenant_hot * tenant_adapter_scale[None, :], axis=1)
    per_token_scale = jnp.sum(member.astype(jnp.float32) * request_scale[None, :], axis=1)[:, None]
    query_rows = (projected_rows[0] + per_token_scale * lora_query).astype(jnp.bfloat16)
    key_rows = projected_rows[1].astype(jnp.bfloat16)
    value_rows = (projected_rows[2] + per_token_scale * lora_value).astype(jnp.bfloat16)

    prefix = arrived.reshape((-1,) + arrived.shape[2:])
    blocks = tok_count // BLOCK
    if chained:
        down.share()
        down.step()
        (prefix,) = tie([gate_up, down], prefix)
        place = jnp.stack([req_index // 2, req_index % 2]).astype(jnp.int32)
        order = jnp.stack([mdl_index ^ 1, mdl_index ^ 3, mdl_index ^ 2, mdl_index]).astype(jnp.int32)
        send, keep, own = attention(
            order, (2, 1, 1), query_rows, key_rows, value_rows, start_of, slot_of, prefix,
            head_output_weight,
        )
        gate_up.share()
        for _ in range(2, lines):
            down.step()
            down.share()
        down.share()
        stream_mine = lax.dynamic_slice_in_dim(stream, mdl_index * row_share, row_share, 0)
        resid = (stream_mine.astype(jnp.float32) + scatter_sum(own, send, keep)).astype(jnp.bfloat16)
        normed = normalise(resid, feedforward_norm_gain)
        across = chip_swap(normed)
        hidden = hidden_units(
            place, lines, gate_up.arrays(), [normed, core_swap(normed), across, core_swap(across)]
        )
        own, send, keep = down_sums(place, lines, down.arrays(), hidden)
        return (resid.astype(jnp.float32) + scatter_sum(own, send, keep)).astype(jnp.bfloat16)

    (attn_part,) = attention(
        jnp.arange(blocks, dtype=jnp.int32), (blocks,), query_rows, key_rows, value_rows, start_of,
        slot_of, prefix, head_output_weight,
    )
    attn_full = lax.psum(attn_part, "mdl").astype(jnp.float32)
    resid = (stream.astype(jnp.float32) + attn_full).astype(jnp.bfloat16)
    normed = normalise(resid, feedforward_norm_gain)
    resid_mine = lax.dynamic_slice_in_dim(resid, mdl_index * row_share, row_share, 0)
    full_mlp = lax.all_gather(feedforward_weight, "req", axis=1, tiled=True)
    gate_part = jnp.dot(normed, full_mlp[0], preferred_element_type=jnp.float32)
    up_part = jnp.dot(normed, full_mlp[1], preferred_element_type=jnp.float32)
    hidden = (jax.nn.silu(gate_part) * up_part).astype(jnp.bfloat16)
    mlp_part = lax.dot_general(
        hidden, full_mlp[2], NT, preferred_element_type=jnp.float32
    ).astype(jnp.bfloat16)
    mlp_mine = lax.psum_scatter(mlp_part, "mdl", scatter_dimension=0, tiled=True)
    return (resid_mine.astype(jnp.float32) + mlp_mine.astype(jnp.float32)).astype(jnp.bfloat16)


def solution(mesh):
    return jax.shard_map(
        per_device,
        mesh=mesh,
        in_specs=(
            P("req", None),
            P(None, "mdl", None),
            P("mdl", None),
            P("mdl", None, None),
            P(None, "mdl", None),
            P(),
            P(),
            P(None, "req", "mdl"),
            P("req", None, "mdl", None),
            P("req"),
            P("req", None),
            P("req"),
            P(),
            P(),
            P(),
        ),
        out_specs=P(("req", "mdl"), None),
        check_vma=False,
    )
```

```python
import functools
import math

import jax
import jax.numpy as jnp
from jax import lax
from jax.experimental import pallas as pl
from jax.experimental.pallas import tpu as pltpu
from jax.sharding import PartitionSpec as P

HEAD_SIZE = 112
WINDOW = 64
BLOCK = 192
HALO = 64
LANES = 256
VMEM_LIMIT = 48 * 1024 * 1024
NT = (((1,), (1,)), ((), ()))


def pack_kernel(cap, table_ref, offset_ref, *refs):
    page_refs, out_ref = refs[:cap], refs[cap]
    dest = pl.program_id(0)
    lane = lax.broadcasted_iota(jnp.int32, out_ref.shape[3:], 1)
    for pair in range(cap // 2):
        first = offset_ref[dest * cap + 2 * pair]
        second = offset_ref[dest * cap + 2 * pair + 1]
        for part in range(2):
            left = page_refs[2 * pair][0, part].astype(jnp.float32)
            right = page_refs[2 * pair + 1][0, part].astype(jnp.float32)
            left = pltpu.roll(left, lax.rem(2 * WINDOW - first, 2 * WINDOW), 1)
            right = pltpu.roll(right, WINDOW - second, 1)
            out_ref[0, pair, part] = jnp.where(lane < WINDOW, left, right).astype(out_ref.dtype)


def pack_windows(pages, table, offsets, cap):
    parts = pages.shape[1:]
    dests = table.shape[0]

    def page_spec(place):
        return pl.BlockSpec(
            (1,) + parts, lambda dest, tbl, off: (tbl[dest * cap + place], 0, 0, 0)
        )

    return pl.pallas_call(
        functools.partial(pack_kernel, cap),
        grid_spec=pltpu.PrefetchScalarGridSpec(
            num_scalar_prefetch=2,
            grid=(dests,),
            in_specs=[page_spec(place) for place in range(cap)],
            out_specs=pl.BlockSpec(
                (1, cap // 2) + parts, lambda dest, tbl, off: (dest, 0, 0, 0, 0)
            ),
        ),
        out_shape=jax.ShapeDtypeStruct((dests, cap // 2) + parts, pages.dtype),
        compiler_params=pltpu.CompilerParams(vmem_limit_bytes=VMEM_LIMIT),
        cost_estimate=pl.CostEstimate(
            flops=0, bytes_accessed=dests * cap * 3 * math.prod(parts), transcendentals=0
        ),
    )(table.reshape(-1), offsets.reshape(-1), *([pages] * cap))


def attention_kernel(
    order_ref, query_ref, key_before_ref, key_ref, value_before_ref, value_ref, start_ref, slot_ref,
    prefix_ref, weight_ref, *out_refs,
):
    *out_refs, mixed_ref = out_refs
    step = pl.program_id(0)
    block = order_ref[step]
    pairs = prefix_ref.shape[0]
    heads = query_ref.shape[1] // HEAD_SIZE
    inv_scale = 1.0 / math.sqrt(HEAD_SIZE)
    start = start_ref[...]
    slot = slot_ref[...]
    own = block * BLOCK + lax.broadcasted_iota(jnp.int32, (BLOCK, 1), 0)
    other = block * BLOCK - HALO + lax.broadcasted_iota(jnp.int32, (1, HALO + BLOCK), 1)
    local_ok = (other >= jnp.maximum(start, own - WINDOW)) & (other <= own)
    lane = lax.broadcasted_iota(jnp.int32, (1, 2 * WINDOW), 1)
    pair_of = lax.shift_right_logical(slot, 1)
    lane_low = lax.bitwise_and(slot, 1) * WINDOW
    prefix_ok = (lane >= lane_low + (own - start)) & (lane < lane_low + WINDOW)
    in_pair = [jnp.broadcast_to(pair_of == pair, (BLOCK, 2 * WINDOW)) for pair in range(pairs)]
    for head in range(heads):
        columns = slice(head * HEAD_SIZE, (head + 1) * HEAD_SIZE)
        query = query_ref[:, columns]
        keys = jnp.concatenate([key_before_ref[:, columns], key_ref[:, columns]], axis=0)
        values = jnp.concatenate([value_before_ref[:, columns], value_ref[:, columns]], axis=0)
        local = lax.dot_general(query, keys, NT, preferred_element_type=jnp.float32)
        local = jnp.where(local_ok, local * inv_scale, -1e30)
        remote = jnp.zeros((BLOCK, 2 * WINDOW), jnp.float32)
        for pair in range(0, pairs, 2):
            wide = jnp.dot(
                query,
                jnp.concatenate([prefix_ref[pair, 0, columns], prefix_ref[pair + 1, 0, columns]], axis=1),
                preferred_element_type=jnp.float32,
            )
            remote = jnp.where(in_pair[pair], wide[:, : 2 * WINDOW], remote)
            remote = jnp.where(in_pair[pair + 1], wide[:, 2 * WINDOW :], remote)
        remote = jnp.where(prefix_ok, remote * inv_scale, -1e30)
        top = jnp.maximum(
            jnp.max(local, axis=1, keepdims=True), jnp.max(remote, axis=1, keepdims=True)
        )
        local = jnp.exp(local - top)
        remote = jnp.exp(remote - top)
        total = jnp.sum(local, axis=1, keepdims=True) + jnp.sum(remote, axis=1, keepdims=True)
        remote = remote.astype(jnp.bfloat16)
        spread = jnp.concatenate(
            [jnp.where(in_pair[pair], remote, jnp.zeros_like(remote)) for pair in range(pairs)], axis=1
        )
        held = jnp.concatenate([prefix_ref[pair, 1, columns] for pair in range(pairs)], axis=1)
        mixed = jnp.dot(local.astype(jnp.bfloat16), values, preferred_element_type=jnp.float32)
        mixed = mixed + lax.dot_general(spread, held, NT, preferred_element_type=jnp.float32)
        mixed_ref[:, columns] = (mixed * (1.0 / total)).astype(jnp.bfloat16)
    projected = jnp.dot(
        mixed_ref[...], weight_ref[...], preferred_element_type=jnp.float32
    ).astype(jnp.bfloat16)
    first = 0
    for out_ref in out_refs:
        span = out_ref.shape[0] // BLOCK

        @pl.when((step >= first) & (step < first + span))
        def _(out_ref=out_ref, first=first):
            rows = pl.multiple_of((step - first) * BLOCK, BLOCK)
            out_ref[pl.ds(rows, BLOCK), :] = projected

        first += span


def attention(order, spans, *, query, key, value, start, slot, prefix, weight):
    tokens, width = order.shape[0] * BLOCK, query.shape[1]
    model = weight.shape[1]
    step = BLOCK // HALO
    own = pl.BlockSpec((BLOCK, width), lambda i, order: (order[i], 0))
    before = pl.BlockSpec((HALO, width), lambda i, order: (jnp.maximum(order[i] * step - 1, 0), 0))
    column = pl.BlockSpec((BLOCK, 1), lambda i, order: (order[i], 0))
    return pl.pallas_call(
        attention_kernel,
        grid_spec=pltpu.PrefetchScalarGridSpec(
            num_scalar_prefetch=1,
            grid=(tokens // BLOCK,),
            in_specs=[
                own, before, own, before, own, column, column,
                pl.BlockSpec(prefix.shape, lambda i, order: (0, 0, 0, 0)),
                pl.BlockSpec(weight.shape, lambda i, order: (0, 0)),
            ],
            out_specs=[pl.BlockSpec((span * BLOCK, model), lambda i, order: (0, 0)) for span in spans],
            scratch_shapes=[pltpu.VMEM((BLOCK, width), jnp.bfloat16)],
        ),
        out_shape=[jax.ShapeDtypeStruct((span * BLOCK, model), jnp.bfloat16) for span in spans],
        compiler_params=pltpu.CompilerParams(vmem_limit_bytes=VMEM_LIMIT),
        cost_estimate=pl.CostEstimate(
            flops=2 * tokens * width * (model + 2 * 2 * WINDOW * prefix.shape[0] + 2 * BLOCK),
            bytes_accessed=2 * (prefix.size + weight.size + tokens * model),
            transcendentals=0,
        ),
    )(order, query, key, key, value, value, start, slot, prefix, weight)


def move(array, line_pairs):
    pairs = [(2 * here + side, 2 * there + side) for here, there in line_pairs for side in range(2)]
    return lax.ppermute(array, "req", pairs)


def swap(array, lines):
    pairs = [(2 * line + side, 2 * line + 1 - side) for line in lines for side in range(2)]
    return lax.ppermute(array, "req", pairs)


class Gather:
    OWN, BELOW, TO_FIRST, ABOVE, TO_LAST, ACROSS, TO_ENDS = range(7)

    def __init__(self, block):
        self.column = {self.OWN: block}
        self.other = {}

    def first(self):
        block = self.column[self.OWN]
        self.column[self.BELOW] = move(block, [(0, 1), (1, 2), (2, 3)])
        self.column[self.ABOVE] = move(block, [(1, 0), (2, 1), (3, 2)])
        self.column[self.ACROSS] = move(block, [(0, 2), (3, 1)])

    def share_own(self):
        self.other[self.OWN] = swap(self.column[self.OWN], range(4))

    def second(self):
        self.column[self.TO_LAST] = move(self.column[self.BELOW], [(2, 3)])
        self.column[self.TO_FIRST] = move(self.column[self.ABOVE], [(1, 0)])
        self.column[self.TO_ENDS] = move(self.column[self.ACROSS], [(2, 3), (1, 0)])

    def share_first(self):
        self.other[self.BELOW] = swap(self.column[self.BELOW], (1, 2, 3))
        self.other[self.ABOVE] = swap(self.column[self.ABOVE], (0, 1, 2))

    def share_second(self):
        self.other[self.TO_LAST] = swap(self.column[self.TO_LAST], (3,))
        self.other[self.TO_FIRST] = swap(self.column[self.TO_FIRST], (0,))
        self.other[self.ACROSS] = swap(self.column[self.ACROSS], (1, 2))

    def last(self, along_lines):
        if along_lines:
            self.other[self.TO_ENDS] = move(self.other[self.ACROSS], [(2, 3), (1, 0)])
        else:
            self.other[self.TO_ENDS] = swap(self.column[self.TO_ENDS], (0, 3))

    def arrays(self):
        return [held[entry] for held in (self.column, self.other) for entry in range(7)]


def tie(gathers, *others):
    held = [entries for gather in gathers for entries in (gather.column, gather.other)]
    flat, others = lax.optimization_barrier((held, others))
    for entries, new in zip(held, flat):
        entries.update(new)
    return others


def piece_copies(place_ref, pieces, halves, buffers, sems, tiles):
    line, side = place_ref[0], place_ref[1]
    jobs = []
    for column in range(2):
        own, below, to_first, above, to_last, across, to_ends = pieces[7 * column : 7 * column + 7]
        at = side if column == 0 else 1 - side
        jobs += [
            (None, own, own, line * 2 + at),
            (line > 0, below, to_first, jnp.where(line > 0, line - 1, 2) * 2 + at),
            (line < 3, above, to_last, jnp.where(line < 3, line + 1, 1) * 2 + at),
            ((line == 1) | (line == 2), across, to_ends, jnp.where(line < 2, 3, 0) * 2 + at),
        ]

    def copies(source, origin, number, tile):
        for half, buffer in enumerate(buffers):
            depth = source.shape[-2]
            rows = pl.multiple_of(origin * depth, depth)
            yield pltpu.make_async_copy(
                (source.at[half] if halves else source).at[:, tiles[tile]],
                buffer.at[pl.ds(rows, depth), tiles[tile]],
                sems.at[(tile * len(jobs) + number) * len(buffers) + half],
            )

    def start(tile):
        for number, (direct, one, two, origin) in enumerate(jobs):
            if direct is None:
                for copy in copies(one, origin, number, tile):
                    copy.start()
                continue

            @pl.when(direct)
            def _():
                for copy in copies(one, origin, number, tile):
                    copy.start()

            @pl.when(jnp.logical_not(direct))
            def _():
                for copy in copies(two, origin, number, tile):
                    copy.start()

    def wait(tile):
        for number, (direct, one, two, origin) in enumerate(jobs):
            for copy in copies(one, origin, number, tile):
                copy.wait()

    return start, wait


def column_tiles(width):
    return [slice(first, min(first + LANES, width)) for first in range(0, width, LANES)]


def hidden_kernel(place_ref, *refs):
    pieces, refs = refs[:14], refs[14:]
    *block_refs, hidden_ref, all_ref, gate_ref, up_ref, sems = refs
    tiles = column_tiles(hidden_ref.shape[1])
    start, wait = piece_copies(place_ref, pieces, True, (gate_ref, up_ref), sems, tiles)
    for tile in range(len(tiles)):
        start(tile)
    for number, block_ref in enumerate(block_refs):
        rows = block_ref.shape[0]
        all_ref[number * rows : (number + 1) * rows, :] = block_ref[...]
    for tile, columns in enumerate(tiles):
        wait(tile)
        gate = jnp.dot(all_ref[...], gate_ref[:, columns], preferred_element_type=jnp.float32)
        up = jnp.dot(all_ref[...], up_ref[:, columns], preferred_element_type=jnp.float32)
        hidden_ref[:, columns] = (gate / (1.0 + jnp.exp(-gate)) * up).astype(jnp.bfloat16)


def hidden_units(place, pieces, blocks):
    width = pieces[0].shape[2]
    tokens = sum(block.shape[0] for block in blocks)
    model = blocks[0].shape[1]
    smem = pl.BlockSpec(memory_space=pltpu.SMEM)
    vmem = pl.BlockSpec(memory_space=pltpu.VMEM)
    anywhere = pl.BlockSpec(memory_space=pl.ANY)
    return pl.pallas_call(
        hidden_kernel,
        in_specs=[smem] + [anywhere] * len(pieces) + [vmem] * len(blocks),
        out_specs=vmem,
        out_shape=jax.ShapeDtypeStruct((tokens, width), jnp.bfloat16),
        scratch_shapes=[
            pltpu.VMEM((tokens, model), jnp.bfloat16),
            pltpu.VMEM((model, width), jnp.bfloat16),
            pltpu.VMEM((model, width), jnp.bfloat16),
            pltpu.SemaphoreType.DMA((16 * len(column_tiles(width)),)),
        ],
        compiler_params=pltpu.CompilerParams(vmem_limit_bytes=VMEM_LIMIT),
        cost_estimate=pl.CostEstimate(
            flops=4 * tokens * model * width, bytes_accessed=4 * model * width, transcendentals=0
        ),
    )(place, *pieces, *blocks)


def down_kernel(place_ref, *refs):
    pieces, refs = refs[:14], refs[14:]
    hidden_ref, keep_ref, send_ref, down_ref, sems = refs
    everything = [slice(0, hidden_ref.shape[1])]
    start, wait = piece_copies(place_ref, pieces, False, (down_ref,), sems, everything)
    start(0)
    wait(0)
    rows = keep_ref.shape[0]

    @pl.loop(0, keep_ref.shape[1] // LANES)
    def _(step):
        columns = pl.ds(pl.multiple_of(step * LANES, LANES), LANES)
        part = lax.dot_general(
            hidden_ref[...], down_ref[columns, :], NT, preferred_element_type=jnp.float32
        ).astype(jnp.bfloat16)
        keep_ref[:, columns] = part[:rows]
        send_ref[:, columns] = part[rows:]


def down_sums(place, pieces, hidden, half):
    tokens, width = hidden.shape
    model = pieces[0].shape[0] * 8
    share = tokens // 4
    smem = pl.BlockSpec(memory_space=pltpu.SMEM)
    vmem = pl.BlockSpec(memory_space=pltpu.VMEM)
    anywhere = pl.BlockSpec(memory_space=pl.ANY)
    return pl.pallas_call(
        down_kernel,
        grid=(1,),
        in_specs=[smem] + [anywhere] * len(pieces) + [pl.BlockSpec((2 * share, width), lambda i: (half, 0))],
        out_specs=[vmem] * 2,
        out_shape=[jax.ShapeDtypeStruct((share, model), jnp.bfloat16)] * 2,
        scratch_shapes=[
            pltpu.VMEM((model, width), jnp.bfloat16),
            pltpu.SemaphoreType.DMA((8,)),
        ],
        compiler_params=pltpu.CompilerParams(vmem_limit_bytes=VMEM_LIMIT),
        cost_estimate=pl.CostEstimate(
            flops=tokens * model * width, bytes_accessed=2 * model * width, transcendentals=0
        ),
    )(place, *pieces, hidden)


def core_swap(array):
    return lax.ppermute(array, "mdl", [(0, 1), (1, 0), (2, 3), (3, 2)])


def chip_swap(array):
    return lax.ppermute(array, "mdl", [(0, 2), (2, 0), (1, 3), (3, 1)])


def sum_on_chip(keep, send):
    wide = jnp.float32
    return (keep.astype(wide) + core_swap(send).astype(wide)).astype(keep.dtype)


def sum_here(keep, send, across):
    wide = jnp.float32
    return keep.astype(wide) + core_swap(send).astype(wide) + across.astype(wide)


def normalise(resid, gain):
    wide = resid.astype(jnp.float32)
    mean_sq = jnp.mean(wide * wide, axis=1, keepdims=True)
    return (wide * lax.rsqrt(mean_sq + 1e-06) * gain.astype(jnp.float32)[None, :]).astype(jnp.bfloat16)


def per_device(
    stream,
    attention_projection_weight,
    head_output_weight,
    adapter_down_maps,
    adapter_up_maps,
    tenant_adapter_scale,
    feedforward_norm_gain,
    feedforward_weight,
    prefix_cache_store,
    token_adapter_index,
    request_token_lengths,
    request_tenant_index,
    last_page_holder,
    holder_page_slot,
    page_filled_rows,
):
    tok_count, model_width = stream.shape
    req_per_dev = request_token_lengths.shape[1]
    rank_total_width = adapter_down_maps.shape[2]
    adapter_number = adapter_up_maps.shape[2] // rank_total_width
    req_devices = lax.axis_size("req")
    req_index = lax.axis_index("req")
    mdl_index = lax.axis_index("mdl")
    row_share = tok_count // lax.axis_size("mdl")
    cap_slots = max(2, (req_per_dev + req_devices - 1) // req_devices + 1)
    cap_slots += cap_slots % 2

    order_ids = jnp.arange(req_per_dev, dtype=jnp.int32)
    owner_table = last_page_holder[:, 0].reshape(req_devices, req_per_dev)
    slot_table = holder_page_slot.reshape(req_devices, req_per_dev)
    offset_table = page_filled_rows.reshape(req_devices, req_per_dev) - WINDOW
    owned = (owner_table == req_index).astype(jnp.int32)
    earlier_one = (order_ids[:, None] > order_ids[None, :]).astype(jnp.int32)
    owned_rank = jnp.sum(owned[:, None, :] * earlier_one[None], axis=2)
    picked = owned[:, None, :] * (
        owned_rank[:, None, :] == jnp.arange(cap_slots, dtype=jnp.int32)[None, :, None]
    ).astype(jnp.int32)
    send_slot = jnp.sum(picked * slot_table[:, None, :], axis=2)
    send_offset = jnp.sum(picked * offset_table[:, None, :], axis=2)
    packed = pack_windows(prefix_cache_store, send_slot, send_offset, cap_slots)
    chained = (req_devices, lax.axis_size("mdl"), tok_count // BLOCK) == (8, 4, 4)
    if chained:
        gate_up, down = Gather(feedforward_weight[:2]), Gather(feedforward_weight[2])
        gate_up.first()
        gate_up.share_own()
        down.share_own()
        (packed,) = tie([gate_up, down], packed)
        gate_up.second()
        gate_up.share_first()
    arrived = lax.all_to_all(packed, "req", split_axis=0, concat_axis=0, tiled=True)

    projected_rows = [
        lax.dot_general(
            stream, attention_projection_weight[k], NT, preferred_element_type=jnp.float32
        )
        for k in range(3)
    ]
    holder_count = adapter_down_maps.shape[0]
    holder_rank_rows = jnp.einsum(
        "qf,kfn->qkn", stream, adapter_down_maps, preferred_element_type=jnp.float32
    )
    held_onehot = (
        token_adapter_index[:, None]
        == (mdl_index * holder_count + jnp.arange(holder_count, dtype=jnp.int32))[None, :]
    )
    rank_part = jnp.sum(holder_rank_rows * held_onehot.astype(jnp.float32)[:, :, None], axis=1)
    rank_feat = lax.psum(rank_part.astype(jnp.bfloat16), "mdl")
    all_onehot = (
        token_adapter_index[:, None] == jnp.arange(adapter_number, dtype=jnp.int32)[None, :]
    )
    broadcast_result = (
        all_onehot.astype(jnp.bfloat16)[:, :, None] * rank_feat[:, None, :]
    ).reshape(tok_count, adapter_number * rank_total_width)
    lora_query = lax.dot_general(
        broadcast_result, adapter_up_maps[0], NT, preferred_element_type=jnp.float32
    )
    lora_value = lax.dot_general(
        broadcast_result, adapter_up_maps[1], NT, preferred_element_type=jnp.float32
    )

    positions = jnp.arange(tok_count, dtype=jnp.int32)
    lengths_row = request_token_lengths[0]
    ends = jnp.sum(
        jnp.where(order_ids[:, None] >= order_ids[None, :], lengths_row[None, :], 0), axis=1
    )
    starts = ends - lengths_row
    member = (positions[:, None] >= starts[None, :]) & (positions[:, None] < ends[None, :])
    member_int = member.astype(jnp.int32)
    start_of = jnp.sum(member_int * starts[None, :], axis=1, keepdims=True)
    my_owner = lax.dynamic_slice_in_dim(owner_table, req_index, 1, 0)[0]
    earlier = (my_owner[:, None] == my_owner[None, :]).astype(jnp.int32) * earlier_one
    slot_in = my_owner * cap_slots + jnp.sum(earlier, axis=1)
    slot_of = jnp.sum(member_int * slot_in[None, :], axis=1, keepdims=True)
    tenant_hot = (
        request_tenant_index[:, None]
        == jnp.arange(tenant_adapter_scale.shape[0], dtype=jnp.int32)[None, :]
    ).astype(jnp.float32)
    request_scale = jnp.sum(tenant_hot * tenant_adapter_scale[None, :], axis=1)
    per_token_scale = jnp.sum(member.astype(jnp.float32) * request_scale[None, :], axis=1)[:, None]
    query_rows = (projected_rows[0] + per_token_scale * lora_query).astype(jnp.bfloat16)
    key_rows = projected_rows[1].astype(jnp.bfloat16)
    value_rows = (projected_rows[2] + per_token_scale * lora_value).astype(jnp.bfloat16)

    prefix = arrived.reshape((-1,) + arrived.shape[2:])
    blocks = tok_count // BLOCK
    attend = functools.partial(
        attention, query=query_rows, key=key_rows, value=value_rows, start=start_of, slot=slot_of,
        weight=head_output_weight,
    )
    if chained:
        (prefix,) = tie([gate_up], prefix)
        place = jnp.stack([req_index // 2, req_index % 2]).astype(jnp.int32)
        far_order = jnp.stack([mdl_index ^ 2, mdl_index ^ 3]).astype(jnp.int32)
        near_order = jnp.stack([mdl_index, mdl_index ^ 1]).astype(jnp.int32)
        gate_up.share_second()
        down.first()
        keep, send = attend(far_order, (1, 1), prefix=prefix)
        prefix, part = lax.optimization_barrier((prefix, sum_on_chip(keep, send)))
        across = chip_swap(part)
        keep, send = attend(near_order, (1, 1), prefix=prefix)
        send, across = lax.optimization_barrier((send, across))
        (keep,) = tie([gate_up, down], keep)
        gate_up.last(True)
        down.second()
        down.share_first()
        down.share_second()
        down.last(False)
        stream_mine = lax.dynamic_slice_in_dim(stream, mdl_index * row_share, row_share, 0)
        resid = (stream_mine.astype(jnp.float32) + sum_here(keep, send, across)).astype(jnp.bfloat16)
        normed = normalise(resid, feedforward_norm_gain)
        across = chip_swap(normed)
        hidden = hidden_units(
            place, gate_up.arrays(), [normed, core_swap(normed), across, core_swap(across)]
        )
        keep, send = down_sums(place, down.arrays(), hidden, 1)
        part, hidden = lax.optimization_barrier((sum_on_chip(keep, send), hidden))
        across = chip_swap(part)
        keep, send = down_sums(place, down.arrays(), hidden, 0)
        send, across = lax.optimization_barrier((send, across))
        return (resid.astype(jnp.float32) + sum_here(keep, send, across)).astype(jnp.bfloat16)

    (attn_part,) = attend(jnp.arange(blocks, dtype=jnp.int32), (blocks,), prefix=prefix)
    attn_full = lax.psum(attn_part, "mdl").astype(jnp.float32)
    resid = (stream.astype(jnp.float32) + attn_full).astype(jnp.bfloat16)
    normed = normalise(resid, feedforward_norm_gain)
    resid_mine = lax.dynamic_slice_in_dim(resid, mdl_index * row_share, row_share, 0)
    full_mlp = lax.all_gather(feedforward_weight, "req", axis=1, tiled=True)
    gate_part = jnp.dot(normed, full_mlp[0], preferred_element_type=jnp.float32)
    up_part = jnp.dot(normed, full_mlp[1], preferred_element_type=jnp.float32)
    hidden = (jax.nn.silu(gate_part) * up_part).astype(jnp.bfloat16)
    mlp_part = lax.dot_general(
        hidden, full_mlp[2], NT, preferred_element_type=jnp.float32
    ).astype(jnp.bfloat16)
    mlp_mine = lax.psum_scatter(mlp_part, "mdl", scatter_dimension=0, tiled=True)
    return (resid_mine.astype(jnp.float32) + mlp_mine.astype(jnp.float32)).astype(jnp.bfloat16)


def solution(mesh):
    return jax.shard_map(
        per_device,
        mesh=mesh,
        in_specs=(
            P("req", None),
            P(None, "mdl", None),
            P("mdl", None),
            P("mdl", None, None),
            P(None, "mdl", None),
            P(),
            P(),
            P(None, "req", "mdl"),
            P("req", None, "mdl", None),
            P("req"),
            P("req", None),
            P("req"),
            P(),
            P(),
            P(),
        ),
        out_specs=P(("req", "mdl"), None),
        check_vma=False,
    )
```

```python
import functools
import math

import jax
import jax.numpy as jnp
from jax import lax
from jax.experimental import pallas as pl
from jax.experimental.pallas import tpu as pltpu
from jax.sharding import PartitionSpec as P

HEAD_SIZE = 112
WINDOW = 64
BLOCK = 192
HALO = 64
LANES = 256
VMEM_LIMIT = 48 * 1024 * 1024
NT = (((1,), (1,)), ((), ()))
SMALL = pl.CostEstimate(flops=0, bytes_accessed=0, transcendentals=0)


def pack_kernel(cap, table_ref, offset_ref, *refs):
    page_refs, out_ref = refs[:cap], refs[cap]
    dest = pl.program_id(0)
    lane = lax.broadcasted_iota(jnp.int32, out_ref.shape[3:], 1)
    for pair in range(cap // 2):
        first = offset_ref[dest * cap + 2 * pair]
        second = offset_ref[dest * cap + 2 * pair + 1]
        for part in range(2):
            left = page_refs[2 * pair][0, part].astype(jnp.float32)
            right = page_refs[2 * pair + 1][0, part].astype(jnp.float32)
            left = pltpu.roll(left, lax.rem(2 * WINDOW - first, 2 * WINDOW), 1)
            right = pltpu.roll(right, WINDOW - second, 1)
            out_ref[0, pair, part] = jnp.where(lane < WINDOW, left, right).astype(out_ref.dtype)


def pack_windows(pages, table, offsets, cap):
    parts = pages.shape[1:]
    dests = table.shape[0]

    def page_spec(place):
        return pl.BlockSpec(
            (1,) + parts, lambda dest, tbl, off: (tbl[dest * cap + place], 0, 0, 0)
        )

    return pl.pallas_call(
        functools.partial(pack_kernel, cap),
        grid_spec=pltpu.PrefetchScalarGridSpec(
            num_scalar_prefetch=2,
            grid=(dests,),
            in_specs=[page_spec(place) for place in range(cap)],
            out_specs=pl.BlockSpec(
                (1, cap // 2) + parts, lambda dest, tbl, off: (dest, 0, 0, 0, 0)
            ),
        ),
        out_shape=jax.ShapeDtypeStruct((dests, cap // 2) + parts, pages.dtype),
        compiler_params=pltpu.CompilerParams(vmem_limit_bytes=VMEM_LIMIT),
        cost_estimate=SMALL,
    )(table.reshape(-1), offsets.reshape(-1), *([pages] * cap))


def attention_kernel(
    order_ref, query_ref, key_before_ref, key_ref, value_before_ref, value_ref, start_ref, slot_ref,
    prefix_ref, weight_ref, *out_refs,
):
    *out_refs, mixed_ref = out_refs
    step = pl.program_id(0)
    block = order_ref[step]
    pairs = prefix_ref.shape[0]
    heads = query_ref.shape[1] // HEAD_SIZE
    inv_scale = 1.0 / math.sqrt(HEAD_SIZE)
    start = start_ref[...]
    slot = slot_ref[...]
    own = block * BLOCK + lax.broadcasted_iota(jnp.int32, (BLOCK, 1), 0)
    other = block * BLOCK - HALO + lax.broadcasted_iota(jnp.int32, (1, HALO + BLOCK), 1)
    local_ok = (other >= jnp.maximum(start, own - WINDOW)) & (other <= own)
    lane = lax.broadcasted_iota(jnp.int32, (1, 2 * WINDOW), 1)
    pair_of = lax.shift_right_logical(slot, 1)
    lane_low = lax.bitwise_and(slot, 1) * WINDOW
    prefix_ok = (lane >= lane_low + (own - start)) & (lane < lane_low + WINDOW)
    in_pair = [jnp.broadcast_to(pair_of == pair, (BLOCK, 2 * WINDOW)) for pair in range(pairs)]
    for head in range(heads):
        columns = slice(head * HEAD_SIZE, (head + 1) * HEAD_SIZE)
        query = query_ref[:, columns]
        keys = jnp.concatenate([key_before_ref[:, columns], key_ref[:, columns]], axis=0)
        values = jnp.concatenate([value_before_ref[:, columns], value_ref[:, columns]], axis=0)
        local = lax.dot_general(query, keys, NT, preferred_element_type=jnp.float32)
        local = jnp.where(local_ok, local * inv_scale, -1e30)
        remote = jnp.zeros((BLOCK, 2 * WINDOW), jnp.float32)
        for pair in range(0, pairs, 2):
            wide = jnp.dot(
                query,
                jnp.concatenate([prefix_ref[pair, 0, columns], prefix_ref[pair + 1, 0, columns]], axis=1),
                preferred_element_type=jnp.float32,
            )
            remote = jnp.where(in_pair[pair], wide[:, : 2 * WINDOW], remote)
            remote = jnp.where(in_pair[pair + 1], wide[:, 2 * WINDOW :], remote)
        remote = jnp.where(prefix_ok, remote * inv_scale, -1e30)
        top = jnp.maximum(
            jnp.max(local, axis=1, keepdims=True), jnp.max(remote, axis=1, keepdims=True)
        )
        local = jnp.exp(local - top)
        remote = jnp.exp(remote - top)
        total = jnp.sum(local, axis=1, keepdims=True) + jnp.sum(remote, axis=1, keepdims=True)
        remote = remote.astype(jnp.bfloat16)
        spread = jnp.concatenate(
            [jnp.where(in_pair[pair], remote, jnp.zeros_like(remote)) for pair in range(pairs)], axis=1
        )
        held = jnp.concatenate([prefix_ref[pair, 1, columns] for pair in range(pairs)], axis=1)
        mixed = jnp.dot(local.astype(jnp.bfloat16), values, preferred_element_type=jnp.float32)
        mixed = mixed + lax.dot_general(spread, held, NT, preferred_element_type=jnp.float32)
        mixed_ref[:, columns] = (mixed * (1.0 / total)).astype(jnp.bfloat16)
    projected = jnp.dot(
        mixed_ref[...], weight_ref[...], preferred_element_type=jnp.float32
    ).astype(jnp.bfloat16)
    first = 0
    for out_ref in out_refs:
        span = out_ref.shape[0] // BLOCK

        @pl.when((step >= first) & (step < first + span))
        def _(out_ref=out_ref, first=first):
            rows = pl.multiple_of((step - first) * BLOCK, BLOCK)
            out_ref[pl.ds(rows, BLOCK), :] = projected

        first += span


def attention(order, spans, query, key, value, start, slot, prefix, weight):
    tokens, width = query.shape
    model = weight.shape[1]
    step = BLOCK // HALO
    own = pl.BlockSpec((BLOCK, width), lambda i, order: (order[i], 0))
    before = pl.BlockSpec((HALO, width), lambda i, order: (jnp.maximum(order[i] * step - 1, 0), 0))
    column = pl.BlockSpec((BLOCK, 1), lambda i, order: (order[i], 0))
    return pl.pallas_call(
        attention_kernel,
        grid_spec=pltpu.PrefetchScalarGridSpec(
            num_scalar_prefetch=1,
            grid=(tokens // BLOCK,),
            in_specs=[
                own, before, own, before, own, column, column,
                pl.BlockSpec(prefix.shape, lambda i, order: (0, 0, 0, 0)),
                pl.BlockSpec(weight.shape, lambda i, order: (0, 0)),
            ],
            out_specs=[pl.BlockSpec((span * BLOCK, model), lambda i, order: (0, 0)) for span in spans],
            scratch_shapes=[pltpu.VMEM((BLOCK, width), jnp.bfloat16)],
        ),
        out_shape=[jax.ShapeDtypeStruct((span * BLOCK, model), jnp.bfloat16) for span in spans],
        compiler_params=pltpu.CompilerParams(vmem_limit_bytes=VMEM_LIMIT),
        cost_estimate=SMALL,
    )(order, query, key, key, value, value, start, slot, prefix, weight)


def hidden_kernel(*refs):
    *block_refs, gate_ref, up_ref, hidden_ref, all_ref = refs

    @pl.when(pl.program_id(0) == 0)
    def _():
        for number, block_ref in enumerate(block_refs):
            rows = block_ref.shape[0]
            all_ref[number * rows : (number + 1) * rows, :] = block_ref[...]

    gate = jnp.dot(all_ref[...], gate_ref[...], preferred_element_type=jnp.float32)
    up = jnp.dot(all_ref[...], up_ref[...], preferred_element_type=jnp.float32)
    hidden_ref[...] = (gate / (1.0 + jnp.exp(-gate)) * up).astype(jnp.bfloat16)


def hidden_units(blocks, gate_up):
    tokens = sum(block.shape[0] for block in blocks)
    _, model, width = gate_up.shape
    columns = [
        pl.BlockSpec((None, model, LANES), functools.partial(lambda part, i: (part, 0, i), part))
        for part in range(2)
    ]
    return pl.pallas_call(
        hidden_kernel,
        grid=(pl.cdiv(width, LANES),),
        in_specs=[pl.BlockSpec(block.shape, lambda i: (0, 0)) for block in blocks] + columns,
        out_specs=pl.BlockSpec((tokens, LANES), lambda i: (0, i)),
        out_shape=jax.ShapeDtypeStruct((tokens, width), jnp.bfloat16),
        scratch_shapes=[pltpu.VMEM((tokens, model), jnp.bfloat16)],
        compiler_params=pltpu.CompilerParams(vmem_limit_bytes=VMEM_LIMIT),
        cost_estimate=SMALL,
    )(*blocks, gate_up, gate_up)


def down_kernel(hidden_ref, down_ref, own_ref, send_ref, keep_ref):
    rows = own_ref.shape[0]
    part = lax.dot_general(
        hidden_ref[...], down_ref[...], NT, preferred_element_type=jnp.float32
    ).astype(jnp.bfloat16)
    own_ref[...] = part[:rows]
    send_ref[:rows] = part[rows : 2 * rows]
    keep_ref[...] = part[2 * rows : 3 * rows]
    send_ref[rows:] = part[3 * rows :]


def down_sums(hidden, down):
    tokens, width = hidden.shape
    model = down.shape[0]
    share = tokens // 4
    spans = (share, 2 * share, share)
    return pl.pallas_call(
        down_kernel,
        grid=(model // LANES,),
        in_specs=[
            pl.BlockSpec((tokens, width), lambda i: (0, 0)),
            pl.BlockSpec((LANES, width), lambda i: (i, 0)),
        ],
        out_specs=[pl.BlockSpec((rows, LANES), lambda i: (0, i)) for rows in spans],
        out_shape=[jax.ShapeDtypeStruct((rows, model), jnp.bfloat16) for rows in spans],
        compiler_params=pltpu.CompilerParams(vmem_limit_bytes=VMEM_LIMIT),
        cost_estimate=SMALL,
    )(hidden, down)


def core_swap(array):
    return lax.ppermute(array, "mdl", [(0, 1), (1, 0), (2, 3), (3, 2)])


def chip_swap(array):
    return lax.ppermute(array, "mdl", [(0, 2), (2, 0), (1, 3), (3, 1)])


def scatter_sum(own, send, keep):
    wide = jnp.float32
    rows = own.shape[0]
    near = core_swap(send)
    far = chip_swap((keep.astype(wide) + near[rows:].astype(wide)).astype(keep.dtype))
    return own.astype(wide) + near[:rows].astype(wide) + far.astype(wide)


def normalise(resid, gain):
    wide = resid.astype(jnp.float32)
    mean_sq = jnp.mean(wide * wide, axis=1, keepdims=True)
    return (wide * lax.rsqrt(mean_sq + 1e-06) * gain.astype(jnp.float32)[None, :]).astype(jnp.bfloat16)


def per_device(
    stream,
    attention_projection_weight,
    head_output_weight,
    adapter_down_maps,
    adapter_up_maps,
    tenant_adapter_scale,
    feedforward_norm_gain,
    feedforward_weight,
    prefix_cache_store,
    token_adapter_index,
    request_token_lengths,
    request_tenant_index,
    last_page_holder,
    holder_page_slot,
    page_filled_rows,
):
    tok_count, model_width = stream.shape
    req_per_dev = request_token_lengths.shape[1]
    rank_total_width = adapter_down_maps.shape[2]
    adapter_number = adapter_up_maps.shape[2] // rank_total_width
    req_devices = lax.axis_size("req")
    req_index = lax.axis_index("req")
    mdl_index = lax.axis_index("mdl")
    row_share = tok_count // lax.axis_size("mdl")
    cap_slots = max(2, (req_per_dev + req_devices - 1) // req_devices + 1)
    cap_slots += cap_slots % 2

    order_ids = jnp.arange(req_per_dev, dtype=jnp.int32)
    owner_table = last_page_holder[:, 0].reshape(req_devices, req_per_dev)
    slot_table = holder_page_slot.reshape(req_devices, req_per_dev)
    offset_table = page_filled_rows.reshape(req_devices, req_per_dev) - WINDOW
    owned = (owner_table == req_index).astype(jnp.int32)
    earlier_one = (order_ids[:, None] > order_ids[None, :]).astype(jnp.int32)
    owned_rank = jnp.sum(owned[:, None, :] * earlier_one[None], axis=2)
    picked = owned[:, None, :] * (
        owned_rank[:, None, :] == jnp.arange(cap_slots, dtype=jnp.int32)[None, :, None]
    ).astype(jnp.int32)
    send_slot = jnp.sum(picked * slot_table[:, None, :], axis=2)
    send_offset = jnp.sum(picked * offset_table[:, None, :], axis=2)
    packed = pack_windows(prefix_cache_store, send_slot, send_offset, cap_slots)
    arrived = lax.all_to_all(packed, "req", split_axis=0, concat_axis=0, tiled=True)

    projected_rows = [
        lax.dot_general(
            stream, attention_projection_weight[k], NT, preferred_element_type=jnp.float32
        )
        for k in range(3)
    ]
    holder_count = adapter_down_maps.shape[0]
    holder_rank_rows = jnp.einsum(
        "qf,kfn->qkn", stream, adapter_down_maps, preferred_element_type=jnp.float32
    )
    held_onehot = (
        token_adapter_index[:, None]
        == (mdl_index * holder_count + jnp.arange(holder_count, dtype=jnp.int32))[None, :]
    )
    rank_part = jnp.sum(holder_rank_rows * held_onehot.astype(jnp.float32)[:, :, None], axis=1)
    rank_feat = lax.psum(rank_part.astype(jnp.bfloat16), "mdl")
    all_onehot = (
        token_adapter_index[:, None] == jnp.arange(adapter_number, dtype=jnp.int32)[None, :]
    )
    broadcast_result = (
        all_onehot.astype(jnp.bfloat16)[:, :, None] * rank_feat[:, None, :]
    ).reshape(tok_count, adapter_number * rank_total_width)
    lora_query = lax.dot_general(
        broadcast_result, adapter_up_maps[0], NT, preferred_element_type=jnp.float32
    )
    lora_value = lax.dot_general(
        broadcast_result, adapter_up_maps[1], NT, preferred_element_type=jnp.float32
    )

    positions = jnp.arange(tok_count, dtype=jnp.int32)
    lengths_row = request_token_lengths[0]
    ends = jnp.sum(
        jnp.where(order_ids[:, None] >= order_ids[None, :], lengths_row[None, :], 0), axis=1
    )
    starts = ends - lengths_row
    member = (positions[:, None] >= starts[None, :]) & (positions[:, None] < ends[None, :])
    member_int = member.astype(jnp.int32)
    start_of = jnp.sum(member_int * starts[None, :], axis=1, keepdims=True)
    my_owner = lax.dynamic_slice_in_dim(owner_table, req_index, 1, 0)[0]
    earlier = (my_owner[:, None] == my_owner[None, :]).astype(jnp.int32) * earlier_one
    slot_in = my_owner * cap_slots + jnp.sum(earlier, axis=1)
    slot_of = jnp.sum(member_int * slot_in[None, :], axis=1, keepdims=True)
    tenant_hot = (
        request_tenant_index[:, None]
        == jnp.arange(tenant_adapter_scale.shape[0], dtype=jnp.int32)[None, :]
    ).astype(jnp.float32)
    request_scale = jnp.sum(tenant_hot * tenant_adapter_scale[None, :], axis=1)
    per_token_scale = jnp.sum(member.astype(jnp.float32) * request_scale[None, :], axis=1)[:, None]
    query_rows = (projected_rows[0] + per_token_scale * lora_query).astype(jnp.bfloat16)
    key_rows = projected_rows[1].astype(jnp.bfloat16)
    value_rows = (projected_rows[2] + per_token_scale * lora_value).astype(jnp.bfloat16)

    prefix = arrived.reshape((-1,) + arrived.shape[2:])
    blocks = tok_count // BLOCK
    if lax.axis_size("mdl") == blocks == 4:
        order = jnp.stack([mdl_index ^ 1, mdl_index ^ 3, mdl_index ^ 2, mdl_index]).astype(jnp.int32)
        send, keep, own = attention(
            order, (2, 1, 1), query_rows, key_rows, value_rows, start_of, slot_of, prefix,
            head_output_weight,
        )
        stream_mine = lax.dynamic_slice_in_dim(stream, mdl_index * row_share, row_share, 0)
        resid = (stream_mine.astype(jnp.float32) + scatter_sum(own, send, keep)).astype(jnp.bfloat16)
        normed = normalise(resid, feedforward_norm_gain)
        gate_up = lax.all_gather(feedforward_weight[:2], "req", axis=1, tiled=True)
        down_full = lax.all_gather(feedforward_weight[2], "req", axis=0, tiled=True)
        across = chip_swap(normed)
        hidden = hidden_units(
            [normed, core_swap(normed), across, core_swap(across)], gate_up
        )
        own, send, keep = down_sums(hidden, down_full)
        return (resid.astype(jnp.float32) + scatter_sum(own, send, keep)).astype(jnp.bfloat16)

    (attn_part,) = attention(
        jnp.arange(blocks, dtype=jnp.int32), (blocks,), query_rows, key_rows, value_rows, start_of,
        slot_of, prefix, head_output_weight,
    )
    attn_full = lax.psum(attn_part, "mdl").astype(jnp.float32)
    resid = (stream.astype(jnp.float32) + attn_full).astype(jnp.bfloat16)
    normed = normalise(resid, feedforward_norm_gain)
    resid_mine = lax.dynamic_slice_in_dim(resid, mdl_index * row_share, row_share, 0)
    full_mlp = lax.all_gather(feedforward_weight, "req", axis=1, tiled=True)
    gate_part = jnp.dot(normed, full_mlp[0], preferred_element_type=jnp.float32)
    up_part = jnp.dot(normed, full_mlp[1], preferred_element_type=jnp.float32)
    hidden = (jax.nn.silu(gate_part) * up_part).astype(jnp.bfloat16)
    mlp_part = lax.dot_general(
        hidden, full_mlp[2], NT, preferred_element_type=jnp.float32
    ).astype(jnp.bfloat16)
    mlp_mine = lax.psum_scatter(mlp_part, "mdl", scatter_dimension=0, tiled=True)
    return (resid_mine.astype(jnp.float32) + mlp_mine.astype(jnp.float32)).astype(jnp.bfloat16)


def solution(mesh):
    return jax.shard_map(
        per_device,
        mesh=mesh,
        in_specs=(
            P("req", None),
            P(None, "mdl", None),
            P("mdl", None),
            P("mdl", None, None),
            P(None, "mdl", None),
            P(),
            P(),
            P(None, "req", "mdl"),
            P("req", None, "mdl", None),
            P("req"),
            P("req", None),
            P("req"),
            P(),
            P(),
            P(),
        ),
        out_specs=P(("req", "mdl"), None),
        check_vma=False,
    )
```

```python
import functools
import math

import jax
import jax.numpy as jnp
from jax import lax
from jax.experimental import pallas as pl
from jax.experimental.pallas import tpu as pltpu
from jax.sharding import PartitionSpec as P

HEAD_SIZE = 112
WINDOW = 64
BLOCK = 192
HALO = 64
LANES = 256
VMEM_LIMIT = 48 * 1024 * 1024
NT = (((1,), (1,)), ((), ()))
SMALL = pl.CostEstimate(flops=0, bytes_accessed=0, transcendentals=0)


def pack_kernel(cap, table_ref, offset_ref, *refs):
    page_refs, out_ref = refs[:cap], refs[cap]
    dest = pl.program_id(0)
    lane = lax.broadcasted_iota(jnp.int32, out_ref.shape[3:], 1)
    for pair in range(cap // 2):
        first = offset_ref[dest * cap + 2 * pair]
        second = offset_ref[dest * cap + 2 * pair + 1]
        for part in range(2):
            left = page_refs[2 * pair][0, part].astype(jnp.float32)
            right = page_refs[2 * pair + 1][0, part].astype(jnp.float32)
            left = pltpu.roll(left, lax.rem(2 * WINDOW - first, 2 * WINDOW), 1)
            right = pltpu.roll(right, WINDOW - second, 1)
            out_ref[0, pair, part] = jnp.where(lane < WINDOW, left, right).astype(out_ref.dtype)


def pack_windows(pages, table, offsets, cap):
    parts = pages.shape[1:]
    dests = table.shape[0]

    def page_spec(place):
        return pl.BlockSpec(
            (1,) + parts, lambda dest, tbl, off: (tbl[dest * cap + place], 0, 0, 0)
        )

    return pl.pallas_call(
        functools.partial(pack_kernel, cap),
        grid_spec=pltpu.PrefetchScalarGridSpec(
            num_scalar_prefetch=2,
            grid=(dests,),
            in_specs=[page_spec(place) for place in range(cap)],
            out_specs=pl.BlockSpec(
                (1, cap // 2) + parts, lambda dest, tbl, off: (dest, 0, 0, 0, 0)
            ),
        ),
        out_shape=jax.ShapeDtypeStruct((dests, cap // 2) + parts, pages.dtype),
        compiler_params=pltpu.CompilerParams(vmem_limit_bytes=VMEM_LIMIT),
        cost_estimate=SMALL,
    )(table.reshape(-1), offsets.reshape(-1), *([pages] * cap))


def attention_kernel(
    order_ref, query_ref, key_before_ref, key_ref, value_before_ref, value_ref, start_ref, slot_ref,
    prefix_ref, weight_ref, *out_refs,
):
    *out_refs, mixed_ref = out_refs
    step = pl.program_id(0)
    block = order_ref[step]
    pairs = prefix_ref.shape[0]
    heads = query_ref.shape[1] // HEAD_SIZE
    inv_scale = 1.0 / math.sqrt(HEAD_SIZE)
    start = start_ref[...]
    slot = slot_ref[...]
    own = block * BLOCK + lax.broadcasted_iota(jnp.int32, (BLOCK, 1), 0)
    other = block * BLOCK - HALO + lax.broadcasted_iota(jnp.int32, (1, HALO + BLOCK), 1)
    local_ok = (other >= jnp.maximum(start, own - WINDOW)) & (other <= own)
    lane = lax.broadcasted_iota(jnp.int32, (1, 2 * WINDOW), 1)
    pair_of = lax.shift_right_logical(slot, 1)
    lane_low = lax.bitwise_and(slot, 1) * WINDOW
    prefix_ok = (lane >= lane_low + (own - start)) & (lane < lane_low + WINDOW)
    in_pair = [jnp.broadcast_to(pair_of == pair, (BLOCK, 2 * WINDOW)) for pair in range(pairs)]
    for head in range(heads):
        columns = slice(head * HEAD_SIZE, (head + 1) * HEAD_SIZE)
        query = query_ref[:, columns]
        keys = jnp.concatenate([key_before_ref[:, columns], key_ref[:, columns]], axis=0)
        values = jnp.concatenate([value_before_ref[:, columns], value_ref[:, columns]], axis=0)
        local = lax.dot_general(query, keys, NT, preferred_element_type=jnp.float32)
        local = jnp.where(local_ok, local * inv_scale, -1e30)
        remote = jnp.zeros((BLOCK, 2 * WINDOW), jnp.float32)
        for pair in range(0, pairs, 2):
            wide = jnp.dot(
                query,
                jnp.concatenate([prefix_ref[pair, 0, columns], prefix_ref[pair + 1, 0, columns]], axis=1),
                preferred_element_type=jnp.float32,
            )
            remote = jnp.where(in_pair[pair], wide[:, : 2 * WINDOW], remote)
            remote = jnp.where(in_pair[pair + 1], wide[:, 2 * WINDOW :], remote)
        remote = jnp.where(prefix_ok, remote * inv_scale, -1e30)
        top = jnp.maximum(
            jnp.max(local, axis=1, keepdims=True), jnp.max(remote, axis=1, keepdims=True)
        )
        local = jnp.exp(local - top)
        remote = jnp.exp(remote - top)
        total = jnp.sum(local, axis=1, keepdims=True) + jnp.sum(remote, axis=1, keepdims=True)
        remote = remote.astype(jnp.bfloat16)
        spread = jnp.concatenate(
            [jnp.where(in_pair[pair], remote, jnp.zeros_like(remote)) for pair in range(pairs)], axis=1
        )
        held = jnp.concatenate([prefix_ref[pair, 1, columns] for pair in range(pairs)], axis=1)
        mixed = jnp.dot(local.astype(jnp.bfloat16), values, preferred_element_type=jnp.float32)
        mixed = mixed + lax.dot_general(spread, held, NT, preferred_element_type=jnp.float32)
        mixed_ref[:, columns] = (mixed * (1.0 / total)).astype(jnp.bfloat16)
    projected = jnp.dot(
        mixed_ref[...], weight_ref[...], preferred_element_type=jnp.float32
    ).astype(jnp.bfloat16)
    first = 0
    for out_ref in out_refs:
        span = out_ref.shape[0] // BLOCK

        @pl.when((step >= first) & (step < first + span))
        def _(out_ref=out_ref, first=first):
            rows = pl.multiple_of((step - first) * BLOCK, BLOCK)
            out_ref[pl.ds(rows, BLOCK), :] = projected

        first += span


def attention(order, spans, query, key, value, start, slot, prefix, weight):
    tokens, width = query.shape
    model = weight.shape[1]
    step = BLOCK // HALO
    own = pl.BlockSpec((BLOCK, width), lambda i, order: (order[i], 0))
    before = pl.BlockSpec((HALO, width), lambda i, order: (jnp.maximum(order[i] * step - 1, 0), 0))
    column = pl.BlockSpec((BLOCK, 1), lambda i, order: (order[i], 0))
    return pl.pallas_call(
        attention_kernel,
        grid_spec=pltpu.PrefetchScalarGridSpec(
            num_scalar_prefetch=1,
            grid=(tokens // BLOCK,),
            in_specs=[
                own, before, own, before, own, column, column,
                pl.BlockSpec(prefix.shape, lambda i, order: (0, 0, 0, 0)),
                pl.BlockSpec(weight.shape, lambda i, order: (0, 0)),
            ],
            out_specs=[pl.BlockSpec((span * BLOCK, model), lambda i, order: (0, 0)) for span in spans],
            scratch_shapes=[pltpu.VMEM((BLOCK, width), jnp.bfloat16)],
        ),
        out_shape=[jax.ShapeDtypeStruct((span * BLOCK, model), jnp.bfloat16) for span in spans],
        compiler_params=pltpu.CompilerParams(vmem_limit_bytes=VMEM_LIMIT),
        cost_estimate=SMALL,
    )(order, query, key, key, value, value, start, slot, prefix, weight)


def ring_place(index, count):
    return jnp.where(index % 2 == 0, index // 2, count - 1 - index // 2)


def ring_index(place, count):
    place = (place + count) % count
    return jnp.where(place < count // 2, 2 * place, 2 * (count - 1 - place) + 1)


class Ring:
    def __init__(self, block, count):
        cycle = list(range(0, count, 2)) + list(range(count - 1, 0, -2))
        self.ahead = [(cycle[at], cycle[(at + 1) % count]) for at in range(count)]
        self.back = [(there, here) for here, there in self.ahead]
        self.forward, self.backward, self.half = [block], [block], block.shape[0] // 2

    def step(self):
        self.forward.append(lax.ppermute(self.forward[-1], "req", self.ahead))
        self.backward.append(lax.ppermute(self.backward[-1], "req", self.back))

    def last(self):
        self.forward.append(lax.ppermute(self.forward[-1][: self.half], "req", self.ahead))
        self.backward.append(lax.ppermute(self.backward[-1][self.half :], "req", self.back))

    def tie(self, *others):
        self.forward[-1], self.backward[-1], *others = lax.optimization_barrier(
            (self.forward[-1], self.backward[-1], *others)
        )
        return others

    def arrays(self):
        return self.forward + self.backward[1:]

    def origins(self, index, count):
        place = ring_place(index, count)
        steps = list(range(count // 2 + 1))
        steps = [-step for step in steps] + steps[1:]
        return jnp.stack([ring_index(place + step, count) for step in steps]).astype(jnp.int32)


def hidden_kernel(pieces, origin_ref, *refs):
    piece_refs, refs = refs[:pieces], refs[pieces:]
    *block_refs, hidden_ref, all_ref, gate_ref, up_ref, sems = refs
    buffers = gate_ref, up_ref
    depth, width = piece_refs[0].shape[1:]
    chunks = [slice(0, LANES), slice(LANES, width)]
    copies = [[], []]
    for number, piece_ref in enumerate(piece_refs):
        rows = pl.ds(pl.multiple_of(origin_ref[number] * depth, 16), depth)
        for part in range(piece_ref.shape[0]):
            buffer = buffers[part] if piece_ref.shape[0] == 2 else buffers[number // (pieces // 2 + 1)]
            for chunk, columns in enumerate(chunks):
                copies[chunk].append(
                    pltpu.make_async_copy(
                        piece_ref.at[part, :, columns],
                        buffer.at[rows, columns],
                        sems.at[chunk, 2 * number + part],
                    )
                )
    for chunk in copies:
        for copy in chunk:
            copy.start()
    for number, block_ref in enumerate(block_refs):
        rows = block_ref.shape[0]
        all_ref[number * rows : (number + 1) * rows, :] = block_ref[...]
    for first in range(0, width, LANES):
        columns = slice(first, min(first + LANES, width))
        if first in (0, LANES):
            for copy in copies[first // LANES]:
                copy.wait()
        gate = jnp.dot(all_ref[...], gate_ref[:, columns], preferred_element_type=jnp.float32)
        up = jnp.dot(all_ref[...], up_ref[:, columns], preferred_element_type=jnp.float32)
        hidden_ref[:, columns] = (gate / (1.0 + jnp.exp(-gate)) * up).astype(jnp.bfloat16)


def hidden_units(origins, pieces, blocks):
    width = pieces[0].shape[2]
    tokens = sum(block.shape[0] for block in blocks)
    model = blocks[0].shape[1]
    smem = pl.BlockSpec(memory_space=pltpu.SMEM)
    vmem = pl.BlockSpec(memory_space=pltpu.VMEM)
    anywhere = pl.BlockSpec(memory_space=pl.ANY)
    return pl.pallas_call(
        functools.partial(hidden_kernel, len(pieces)),
        in_specs=[smem] + [anywhere] * len(pieces) + [vmem] * len(blocks),
        out_specs=vmem,
        out_shape=jax.ShapeDtypeStruct((tokens, width), jnp.bfloat16),
        scratch_shapes=[
            pltpu.VMEM((tokens, model), jnp.bfloat16),
            pltpu.VMEM((model, width), jnp.bfloat16),
            pltpu.VMEM((model, width), jnp.bfloat16),
            pltpu.SemaphoreType.DMA((2, 2 * len(pieces))),
        ],
        compiler_params=pltpu.CompilerParams(vmem_limit_bytes=VMEM_LIMIT),
        cost_estimate=SMALL,
    )(origins, *pieces, *blocks)


def down_kernel(pieces, origin_ref, *refs):
    piece_refs, refs = refs[:pieces], refs[pieces:]
    hidden_ref, own_ref, send_ref, keep_ref, down_ref, sems = refs
    depth = piece_refs[0].shape[0]
    copies = []
    for number, piece_ref in enumerate(piece_refs):
        first = origin_ref[number] * depth
        if number == pieces - 1:
            first = first + depth - piece_ref.shape[0]
        rows = pl.ds(pl.multiple_of(first, 16), piece_ref.shape[0])
        copies.append(pltpu.make_async_copy(piece_ref, down_ref.at[rows, :], sems.at[number]))
    for copy in copies:
        copy.start()
    for copy in copies:
        copy.wait()
    rows = own_ref.shape[0]

    @pl.loop(0, own_ref.shape[1] // LANES)
    def _(step):
        columns = pl.ds(pl.multiple_of(step * LANES, LANES), LANES)
        part = lax.dot_general(
            hidden_ref[...], down_ref[columns, :], NT, preferred_element_type=jnp.float32
        ).astype(jnp.bfloat16)
        own_ref[:, columns] = part[:rows]
        send_ref[:rows, columns] = part[rows : 2 * rows]
        keep_ref[:, columns] = part[2 * rows : 3 * rows]
        send_ref[rows:, columns] = part[3 * rows :]


def down_sums(origins, pieces, hidden, model):
    tokens, width = hidden.shape
    share = tokens // 4
    smem = pl.BlockSpec(memory_space=pltpu.SMEM)
    vmem = pl.BlockSpec(memory_space=pltpu.VMEM)
    anywhere = pl.BlockSpec(memory_space=pl.ANY)
    return pl.pallas_call(
        functools.partial(down_kernel, len(pieces)),
        in_specs=[smem] + [anywhere] * len(pieces) + [vmem],
        out_specs=[vmem] * 3,
        out_shape=[
            jax.ShapeDtypeStruct((rows, model), jnp.bfloat16) for rows in (share, 2 * share, share)
        ],
        scratch_shapes=[
            pltpu.VMEM((model, width), jnp.bfloat16),
            pltpu.SemaphoreType.DMA((len(pieces),)),
        ],
        compiler_params=pltpu.CompilerParams(vmem_limit_bytes=VMEM_LIMIT),
        cost_estimate=SMALL,
    )(origins, *pieces, hidden)


def core_swap(array):
    return lax.ppermute(array, "mdl", [(0, 1), (1, 0), (2, 3), (3, 2)])


def chip_swap(array):
    return lax.ppermute(array, "mdl", [(0, 2), (2, 0), (1, 3), (3, 1)])


def scatter_sum(own, send, keep):
    wide = jnp.float32
    rows = own.shape[0]
    near = core_swap(send)
    far = chip_swap((keep.astype(wide) + near[rows:].astype(wide)).astype(keep.dtype))
    return own.astype(wide) + near[:rows].astype(wide) + far.astype(wide)


def normalise(resid, gain):
    wide = resid.astype(jnp.float32)
    mean_sq = jnp.mean(wide * wide, axis=1, keepdims=True)
    return (wide * lax.rsqrt(mean_sq + 1e-06) * gain.astype(jnp.float32)[None, :]).astype(jnp.bfloat16)


def per_device(
    stream,
    attention_projection_weight,
    head_output_weight,
    adapter_down_maps,
    adapter_up_maps,
    tenant_adapter_scale,
    feedforward_norm_gain,
    feedforward_weight,
    prefix_cache_store,
    token_adapter_index,
    request_token_lengths,
    request_tenant_index,
    last_page_holder,
    holder_page_slot,
    page_filled_rows,
):
    tok_count, model_width = stream.shape
    req_per_dev = request_token_lengths.shape[1]
    rank_total_width = adapter_down_maps.shape[2]
    adapter_number = adapter_up_maps.shape[2] // rank_total_width
    req_devices = lax.axis_size("req")
    req_index = lax.axis_index("req")
    mdl_index = lax.axis_index("mdl")
    row_share = tok_count // lax.axis_size("mdl")
    cap_slots = max(2, (req_per_dev + req_devices - 1) // req_devices + 1)
    cap_slots += cap_slots % 2

    order_ids = jnp.arange(req_per_dev, dtype=jnp.int32)
    owner_table = last_page_holder[:, 0].reshape(req_devices, req_per_dev)
    slot_table = holder_page_slot.reshape(req_devices, req_per_dev)
    offset_table = page_filled_rows.reshape(req_devices, req_per_dev) - WINDOW
    owned = (owner_table == req_index).astype(jnp.int32)
    earlier_one = (order_ids[:, None] > order_ids[None, :]).astype(jnp.int32)
    owned_rank = jnp.sum(owned[:, None, :] * earlier_one[None], axis=2)
    picked = owned[:, None, :] * (
        owned_rank[:, None, :] == jnp.arange(cap_slots, dtype=jnp.int32)[None, :, None]
    ).astype(jnp.int32)
    send_slot = jnp.sum(picked * slot_table[:, None, :], axis=2)
    send_offset = jnp.sum(picked * offset_table[:, None, :], axis=2)
    packed = pack_windows(prefix_cache_store, send_slot, send_offset, cap_slots)
    rows_held = feedforward_weight.shape[1]
    ringed = (lax.axis_size("mdl"), tok_count // BLOCK, req_devices % 2, rows_held % 32) == (4, 4, 0, 0)
    if ringed:
        gate_up = Ring(feedforward_weight[:2], req_devices)
        gate_up.step()
        gate_up.step()
    arrived = lax.all_to_all(packed, "req", split_axis=0, concat_axis=0, tiled=True)

    projected_rows = [
        lax.dot_general(
            stream, attention_projection_weight[k], NT, preferred_element_type=jnp.float32
        )
        for k in range(3)
    ]
    holder_count = adapter_down_maps.shape[0]
    holder_rank_rows = jnp.einsum(
        "qf,kfn->qkn", stream, adapter_down_maps, preferred_element_type=jnp.float32
    )
    held_onehot = (
        token_adapter_index[:, None]
        == (mdl_index * holder_count + jnp.arange(holder_count, dtype=jnp.int32))[None, :]
    )
    rank_part = jnp.sum(holder_rank_rows * held_onehot.astype(jnp.float32)[:, :, None], axis=1)
    rank_feat = lax.psum(rank_part.astype(jnp.bfloat16), "mdl")
    all_onehot = (
        token_adapter_index[:, None] == jnp.arange(adapter_number, dtype=jnp.int32)[None, :]
    )
    broadcast_result = (
        all_onehot.astype(jnp.bfloat16)[:, :, None] * rank_feat[:, None, :]
    ).reshape(tok_count, adapter_number * rank_total_width)
    lora_query = lax.dot_general(
        broadcast_result, adapter_up_maps[0], NT, preferred_element_type=jnp.float32
    )
    lora_value = lax.dot_general(
        broadcast_result, adapter_up_maps[1], NT, preferred_element_type=jnp.float32
    )

    positions = jnp.arange(tok_count, dtype=jnp.int32)
    lengths_row = request_token_lengths[0]
    ends = jnp.sum(
        jnp.where(order_ids[:, None] >= order_ids[None, :], lengths_row[None, :], 0), axis=1
    )
    starts = ends - lengths_row
    member = (positions[:, None] >= starts[None, :]) & (positions[:, None] < ends[None, :])
    member_int = member.astype(jnp.int32)
    start_of = jnp.sum(member_int * starts[None, :], axis=1, keepdims=True)
    my_owner = lax.dynamic_slice_in_dim(owner_table, req_index, 1, 0)[0]
    earlier = (my_owner[:, None] == my_owner[None, :]).astype(jnp.int32) * earlier_one
    slot_in = my_owner * cap_slots + jnp.sum(earlier, axis=1)
    slot_of = jnp.sum(member_int * slot_in[None, :], axis=1, keepdims=True)
    tenant_hot = (
        request_tenant_index[:, None]
        == jnp.arange(tenant_adapter_scale.shape[0], dtype=jnp.int32)[None, :]
    ).astype(jnp.float32)
    request_scale = jnp.sum(tenant_hot * tenant_adapter_scale[None, :], axis=1)
    per_token_scale = jnp.sum(member.astype(jnp.float32) * request_scale[None, :], axis=1)[:, None]
    query_rows = (projected_rows[0] + per_token_scale * lora_query).astype(jnp.bfloat16)
    key_rows = projected_rows[1].astype(jnp.bfloat16)
    value_rows = (projected_rows[2] + per_token_scale * lora_value).astype(jnp.bfloat16)

    prefix = arrived.reshape((-1,) + arrived.shape[2:])
    blocks = tok_count // BLOCK
    if ringed:
        (prefix,) = gate_up.tie(prefix)
        for _ in range(3, req_devices // 2):
            gate_up.step()
        origins = gate_up.origins(req_index, req_devices)
        order = jnp.stack([mdl_index ^ 1, mdl_index ^ 3, mdl_index ^ 2, mdl_index]).astype(jnp.int32)
        send, keep, own = attention(
            order, (2, 1, 1), query_rows, key_rows, value_rows, start_of, slot_of, prefix,
            head_output_weight,
        )
        (send,) = gate_up.tie(send)
        gate_up.last()
        (down_block,) = gate_up.tie(feedforward_weight[2])
        down = Ring(down_block, req_devices)
        for _ in range(1, req_devices // 2):
            down.step()
        down.last()
        stream_mine = lax.dynamic_slice_in_dim(stream, mdl_index * row_share, row_share, 0)
        resid = (stream_mine.astype(jnp.float32) + scatter_sum(own, send, keep)).astype(jnp.bfloat16)
        normed = normalise(resid, feedforward_norm_gain)
        across = chip_swap(normed)
        hidden = hidden_units(
            origins, gate_up.arrays(), [normed, core_swap(normed), across, core_swap(across)]
        )
        own, send, keep = down_sums(origins, down.arrays(), hidden, model_width)
        return (resid.astype(jnp.float32) + scatter_sum(own, send, keep)).astype(jnp.bfloat16)

    (attn_part,) = attention(
        jnp.arange(blocks, dtype=jnp.int32), (blocks,), query_rows, key_rows, value_rows, start_of,
        slot_of, prefix, head_output_weight,
    )
    attn_full = lax.psum(attn_part, "mdl").astype(jnp.float32)
    resid = (stream.astype(jnp.float32) + attn_full).astype(jnp.bfloat16)
    normed = normalise(resid, feedforward_norm_gain)
    resid_mine = lax.dynamic_slice_in_dim(resid, mdl_index * row_share, row_share, 0)
    full_mlp = lax.all_gather(feedforward_weight, "req", axis=1, tiled=True)
    gate_part = jnp.dot(normed, full_mlp[0], preferred_element_type=jnp.float32)
    up_part = jnp.dot(normed, full_mlp[1], preferred_element_type=jnp.float32)
    hidden = (jax.nn.silu(gate_part) * up_part).astype(jnp.bfloat16)
    mlp_part = lax.dot_general(
        hidden, full_mlp[2], NT, preferred_element_type=jnp.float32
    ).astype(jnp.bfloat16)
    mlp_mine = lax.psum_scatter(mlp_part, "mdl", scatter_dimension=0, tiled=True)
    return (resid_mine.astype(jnp.float32) + mlp_mine.astype(jnp.float32)).astype(jnp.bfloat16)


def solution(mesh):
    return jax.shard_map(
        per_device,
        mesh=mesh,
        in_specs=(
            P("req", None),
            P(None, "mdl", None),
            P("mdl", None),
            P("mdl", None, None),
            P(None, "mdl", None),
            P(),
            P(),
            P(None, "req", "mdl"),
            P("req", None, "mdl", None),
            P("req"),
            P("req", None),
            P("req"),
            P(),
            P(),
            P(),
        ),
        out_specs=P(("req", "mdl"), None),
        check_vma=False,
    )
```

```python
import functools
import math

import jax
import jax.numpy as jnp
from jax import lax
from jax.experimental import pallas as pl
from jax.experimental.pallas import tpu as pltpu
from jax.sharding import PartitionSpec as P

HEAD_SIZE = 112
WINDOW = 64
BLOCK = 192
HALO = 64
LANES = 256
VMEM_LIMIT = 48 * 1024 * 1024
NT = (((1,), (1,)), ((), ()))
SMALL = pl.CostEstimate(flops=0, bytes_accessed=0, transcendentals=0)


def pack_kernel(cap, table_ref, offset_ref, *refs):
    page_refs, out_ref = refs[:cap], refs[cap]
    dest = pl.program_id(0)
    lane = lax.broadcasted_iota(jnp.int32, out_ref.shape[3:], 1)
    for pair in range(cap // 2):
        first = offset_ref[dest * cap + 2 * pair]
        second = offset_ref[dest * cap + 2 * pair + 1]
        for part in range(2):
            left = page_refs[2 * pair][0, part].astype(jnp.float32)
            right = page_refs[2 * pair + 1][0, part].astype(jnp.float32)
            left = pltpu.roll(left, lax.rem(2 * WINDOW - first, 2 * WINDOW), 1)
            right = pltpu.roll(right, WINDOW - second, 1)
            out_ref[0, pair, part] = jnp.where(lane < WINDOW, left, right).astype(out_ref.dtype)


def pack_windows(pages, table, offsets, cap):
    parts = pages.shape[1:]
    dests = table.shape[0]

    def page_spec(place):
        return pl.BlockSpec(
            (1,) + parts, lambda dest, tbl, off: (tbl[dest * cap + place], 0, 0, 0)
        )

    return pl.pallas_call(
        functools.partial(pack_kernel, cap),
        grid_spec=pltpu.PrefetchScalarGridSpec(
            num_scalar_prefetch=2,
            grid=(dests,),
            in_specs=[page_spec(place) for place in range(cap)],
            out_specs=pl.BlockSpec(
                (1, cap // 2) + parts, lambda dest, tbl, off: (dest, 0, 0, 0, 0)
            ),
        ),
        out_shape=jax.ShapeDtypeStruct((dests, cap // 2) + parts, pages.dtype),
        compiler_params=pltpu.CompilerParams(vmem_limit_bytes=VMEM_LIMIT),
        cost_estimate=SMALL,
    )(table.reshape(-1), offsets.reshape(-1), *([pages] * cap))


def attention_kernel(
    order_ref, query_ref, key_before_ref, key_ref, value_before_ref, value_ref, start_ref, slot_ref,
    prefix_ref, weight_ref, *out_refs,
):
    *out_refs, mixed_ref = out_refs
    step = pl.program_id(0)
    block = order_ref[step]
    pairs = prefix_ref.shape[0]
    heads = query_ref.shape[1] // HEAD_SIZE
    inv_scale = 1.0 / math.sqrt(HEAD_SIZE)
    start = start_ref[...]
    slot = slot_ref[...]
    own = block * BLOCK + lax.broadcasted_iota(jnp.int32, (BLOCK, 1), 0)
    other = block * BLOCK - HALO + lax.broadcasted_iota(jnp.int32, (1, HALO + BLOCK), 1)
    local_ok = (other >= jnp.maximum(start, own - WINDOW)) & (other <= own)
    lane = lax.broadcasted_iota(jnp.int32, (1, 2 * WINDOW), 1)
    pair_of = lax.shift_right_logical(slot, 1)
    lane_low = lax.bitwise_and(slot, 1) * WINDOW
    prefix_ok = (lane >= lane_low + (own - start)) & (lane < lane_low + WINDOW)
    in_pair = [jnp.broadcast_to(pair_of == pair, (BLOCK, 2 * WINDOW)) for pair in range(pairs)]
    for head in range(heads):
        columns = slice(head * HEAD_SIZE, (head + 1) * HEAD_SIZE)
        query = query_ref[:, columns]
        keys = jnp.concatenate([key_before_ref[:, columns], key_ref[:, columns]], axis=0)
        values = jnp.concatenate([value_before_ref[:, columns], value_ref[:, columns]], axis=0)
        local = lax.dot_general(query, keys, NT, preferred_element_type=jnp.float32)
        local = jnp.where(local_ok, local * inv_scale, -1e30)
        remote = jnp.zeros((BLOCK, 2 * WINDOW), jnp.float32)
        for pair in range(0, pairs, 2):
            wide = jnp.dot(
                query,
                jnp.concatenate([prefix_ref[pair, 0, columns], prefix_ref[pair + 1, 0, columns]], axis=1),
                preferred_element_type=jnp.float32,
            )
            remote = jnp.where(in_pair[pair], wide[:, : 2 * WINDOW], remote)
            remote = jnp.where(in_pair[pair + 1], wide[:, 2 * WINDOW :], remote)
        remote = jnp.where(prefix_ok, remote * inv_scale, -1e30)
        top = jnp.maximum(
            jnp.max(local, axis=1, keepdims=True), jnp.max(remote, axis=1, keepdims=True)
        )
        local = jnp.exp(local - top)
        remote = jnp.exp(remote - top)
        total = jnp.sum(local, axis=1, keepdims=True) + jnp.sum(remote, axis=1, keepdims=True)
        remote = remote.astype(jnp.bfloat16)
        spread = jnp.concatenate(
            [jnp.where(in_pair[pair], remote, jnp.zeros_like(remote)) for pair in range(pairs)], axis=1
        )
        held = jnp.concatenate([prefix_ref[pair, 1, columns] for pair in range(pairs)], axis=1)
        mixed = jnp.dot(local.astype(jnp.bfloat16), values, preferred_element_type=jnp.float32)
        mixed = mixed + lax.dot_general(spread, held, NT, preferred_element_type=jnp.float32)
        mixed_ref[:, columns] = (mixed * (1.0 / total)).astype(jnp.bfloat16)
    projected = jnp.dot(
        mixed_ref[...], weight_ref[...], preferred_element_type=jnp.float32
    ).astype(jnp.bfloat16)
    first = 0
    for out_ref in out_refs:
        span = out_ref.shape[0] // BLOCK

        @pl.when((step >= first) & (step < first + span))
        def _(out_ref=out_ref, first=first):
            rows = pl.multiple_of((step - first) * BLOCK, BLOCK)
            out_ref[pl.ds(rows, BLOCK), :] = projected

        first += span


def attention(order, spans, query, key, value, start, slot, prefix, weight):
    tokens, width = query.shape
    model = weight.shape[1]
    step = BLOCK // HALO
    own = pl.BlockSpec((BLOCK, width), lambda i, order: (order[i], 0))
    before = pl.BlockSpec((HALO, width), lambda i, order: (jnp.maximum(order[i] * step - 1, 0), 0))
    column = pl.BlockSpec((BLOCK, 1), lambda i, order: (order[i], 0))
    return pl.pallas_call(
        attention_kernel,
        grid_spec=pltpu.PrefetchScalarGridSpec(
            num_scalar_prefetch=1,
            grid=(tokens // BLOCK,),
            in_specs=[
                own, before, own, before, own, column, column,
                pl.BlockSpec(prefix.shape, lambda i, order: (0, 0, 0, 0)),
                pl.BlockSpec(weight.shape, lambda i, order: (0, 0)),
            ],
            out_specs=[pl.BlockSpec((span * BLOCK, model), lambda i, order: (0, 0)) for span in spans],
            scratch_shapes=[pltpu.VMEM((BLOCK, width), jnp.bfloat16)],
        ),
        out_shape=[jax.ShapeDtypeStruct((span * BLOCK, model), jnp.bfloat16) for span in spans],
        compiler_params=pltpu.CompilerParams(vmem_limit_bytes=VMEM_LIMIT),
        cost_estimate=SMALL,
    )(order, query, key, key, value, value, start, slot, prefix, weight)


def ring_place(index, count):
    return jnp.where(index % 2 == 0, index // 2, count - 1 - index // 2)


def ring_index(place, count):
    place = (place + count) % count
    return jnp.where(place < count // 2, 2 * place, 2 * (count - 1 - place) + 1)


class Ring:
    def __init__(self, block, count):
        cycle = list(range(0, count, 2)) + list(range(count - 1, 0, -2))
        self.ahead = [(cycle[at], cycle[(at + 1) % count]) for at in range(count)]
        self.back = [(there, here) for here, there in self.ahead]
        self.forward, self.backward, self.half = [block], [block], block.shape[0] // 2

    def step(self):
        self.forward.append(lax.ppermute(self.forward[-1], "req", self.ahead))
        self.backward.append(lax.ppermute(self.backward[-1], "req", self.back))

    def last(self):
        self.forward.append(lax.ppermute(self.forward[-1][: self.half], "req", self.ahead))
        self.backward.append(lax.ppermute(self.backward[-1][self.half :], "req", self.back))

    def tie(self, *others):
        self.forward[-1], self.backward[-1], *others = lax.optimization_barrier(
            (self.forward[-1], self.backward[-1], *others)
        )
        return others

    def arrays(self):
        return self.forward + self.backward[1:]

    def origins(self, index, count):
        place = ring_place(index, count)
        steps = list(range(count // 2 + 1))
        steps = [-step for step in steps] + steps[1:]
        return jnp.stack([ring_index(place + step, count) for step in steps]).astype(jnp.int32)


def hidden_kernel(pieces, origin_ref, *refs):
    piece_refs, refs = refs[:pieces], refs[pieces:]
    *block_refs, hidden_ref, all_ref, gate_ref, up_ref, sems = refs
    buffers = gate_ref, up_ref
    depth, width = piece_refs[0].shape[1:]
    chunks = [slice(0, LANES), slice(LANES, width)]
    copies = [[], []]
    for number, piece_ref in enumerate(piece_refs):
        rows = pl.ds(pl.multiple_of(origin_ref[number] * depth, 16), depth)
        for part in range(piece_ref.shape[0]):
            buffer = buffers[part] if piece_ref.shape[0] == 2 else buffers[number // (pieces // 2 + 1)]
            for chunk, columns in enumerate(chunks):
                copies[chunk].append(
                    pltpu.make_async_copy(
                        piece_ref.at[part, :, columns],
                        buffer.at[rows, columns],
                        sems.at[chunk, 2 * number + part],
                    )
                )
    for chunk in copies:
        for copy in chunk:
            copy.start()
    for number, block_ref in enumerate(block_refs):
        rows = block_ref.shape[0]
        all_ref[number * rows : (number + 1) * rows, :] = block_ref[...]
    for first in range(0, width, LANES):
        columns = slice(first, min(first + LANES, width))
        if first in (0, LANES):
            for copy in copies[first // LANES]:
                copy.wait()
        gate = jnp.dot(all_ref[...], gate_ref[:, columns], preferred_element_type=jnp.float32)
        up = jnp.dot(all_ref[...], up_ref[:, columns], preferred_element_type=jnp.float32)
        hidden_ref[:, columns] = (gate / (1.0 + jnp.exp(-gate)) * up).astype(jnp.bfloat16)


def hidden_units(origins, pieces, blocks):
    width = pieces[0].shape[2]
    tokens = sum(block.shape[0] for block in blocks)
    model = blocks[0].shape[1]
    smem = pl.BlockSpec(memory_space=pltpu.SMEM)
    vmem = pl.BlockSpec(memory_space=pltpu.VMEM)
    anywhere = pl.BlockSpec(memory_space=pl.ANY)
    return pl.pallas_call(
        functools.partial(hidden_kernel, len(pieces)),
        in_specs=[smem] + [anywhere] * len(pieces) + [vmem] * len(blocks),
        out_specs=vmem,
        out_shape=jax.ShapeDtypeStruct((tokens, width), jnp.bfloat16),
        scratch_shapes=[
            pltpu.VMEM((tokens, model), jnp.bfloat16),
            pltpu.VMEM((model, width), jnp.bfloat16),
            pltpu.VMEM((model, width), jnp.bfloat16),
            pltpu.SemaphoreType.DMA((2, 2 * len(pieces))),
        ],
        compiler_params=pltpu.CompilerParams(vmem_limit_bytes=VMEM_LIMIT),
        cost_estimate=SMALL,
    )(origins, *pieces, *blocks)


def down_kernel(pieces, hidden_ref, *refs):
    piece_refs, out_refs = refs[:pieces], refs[pieces:]
    hidden = hidden_ref[...]
    blocks = [piece_ref[...] for piece_ref in piece_refs]
    depth = blocks[0].shape[0]
    if blocks[-1].shape[0] < depth:
        blocks[-2:] = [jnp.concatenate(blocks[-2:], axis=0)]
    for number, block in enumerate(blocks):
        columns = slice(number * depth, (number + 1) * depth)
        part = lax.dot_general(hidden, block, NT, preferred_element_type=jnp.float32)
        first = 0
        for out_ref in out_refs:
            rows = out_ref.shape[0]
            out_ref[:, columns] = part[first : first + rows].astype(out_ref.dtype)
            first += rows


def down_sums(pieces, hidden):
    tokens = hidden.shape[0]
    columns = sum(piece.shape[0] for piece in pieces)
    vmem = pl.BlockSpec(memory_space=pltpu.VMEM)
    return pl.pallas_call(
        functools.partial(down_kernel, len(pieces)),
        in_specs=[vmem] * (1 + len(pieces)),
        out_specs=[vmem] * 4,
        out_shape=[jax.ShapeDtypeStruct((tokens // 4, columns), jnp.bfloat16)] * 4,
        compiler_params=pltpu.CompilerParams(vmem_limit_bytes=VMEM_LIMIT),
        cost_estimate=SMALL,
    )(hidden, *pieces)


def place_kernel(groups, depth, origin_ref, resid_ref, *refs):
    term_refs, (out_ref, sum_ref) = refs[:-2], refs[-2:]
    rows, model = out_ref.shape
    sum_ref[...] = jnp.zeros_like(sum_ref)
    number, span = 0, 3 * 128
    for count, parts in groups:
        terms, term_refs = term_refs[:parts], term_refs[parts:]
        total = sum(term_ref[...].astype(jnp.float32) for term_ref in terms)
        for entry in range(count):
            first = origin_ref[number] * depth
            block = total[:, entry * depth : (entry + 1) * depth]
            block = jnp.concatenate([block, jnp.zeros((rows, span - depth), jnp.float32)], axis=1)
            block = pltpu.roll(block, lax.rem(first, 128), 1)
            lanes = pl.ds(pl.multiple_of(lax.div(first, 128) * 128, 128), span)
            sum_ref[:, lanes] += block
            number += 1
    out_ref[...] = (resid_ref[...].astype(jnp.float32) + sum_ref[:, :model]).astype(out_ref.dtype)


def place_and_add(origins, resid, groups, depth):
    sizes = [(terms[0].shape[1] // depth, len(terms)) for terms in groups]
    smem = pl.BlockSpec(memory_space=pltpu.SMEM)
    vmem = pl.BlockSpec(memory_space=pltpu.VMEM)
    terms = [term for group in groups for term in group]
    rows, model = resid.shape
    return pl.pallas_call(
        functools.partial(place_kernel, sizes, depth),
        in_specs=[smem] + [vmem] * (1 + len(terms)),
        out_specs=vmem,
        out_shape=jax.ShapeDtypeStruct(resid.shape, resid.dtype),
        scratch_shapes=[pltpu.VMEM((rows, model + 128), jnp.float32)],
        compiler_params=pltpu.CompilerParams(vmem_limit_bytes=VMEM_LIMIT),
        cost_estimate=SMALL,
    )(origins, resid, *terms)


def core_swap(array):
    return lax.ppermute(array, "mdl", [(0, 1), (1, 0), (2, 3), (3, 2)])


def chip_swap(array):
    return lax.ppermute(array, "mdl", [(0, 2), (2, 0), (1, 3), (3, 1)])


def sum_on_chip(keep, send):
    wide = jnp.float32
    return (keep.astype(wide) + core_swap(send).astype(wide)).astype(keep.dtype)


def sum_here(own, other, across):
    wide = jnp.float32
    return own.astype(wide) + core_swap(other).astype(wide) + across.astype(wide)


def scatter_sum(own, send, keep):
    wide = jnp.float32
    rows = own.shape[0]
    near = core_swap(send)
    far = chip_swap((keep.astype(wide) + near[rows:].astype(wide)).astype(keep.dtype))
    return own.astype(wide) + near[:rows].astype(wide) + far.astype(wide)


def normalise(resid, gain):
    wide = resid.astype(jnp.float32)
    mean_sq = jnp.mean(wide * wide, axis=1, keepdims=True)
    return (wide * lax.rsqrt(mean_sq + 1e-06) * gain.astype(jnp.float32)[None, :]).astype(jnp.bfloat16)


def per_device(
    stream,
    attention_projection_weight,
    head_output_weight,
    adapter_down_maps,
    adapter_up_maps,
    tenant_adapter_scale,
    feedforward_norm_gain,
    feedforward_weight,
    prefix_cache_store,
    token_adapter_index,
    request_token_lengths,
    request_tenant_index,
    last_page_holder,
    holder_page_slot,
    page_filled_rows,
):
    tok_count, model_width = stream.shape
    req_per_dev = request_token_lengths.shape[1]
    rank_total_width = adapter_down_maps.shape[2]
    adapter_number = adapter_up_maps.shape[2] // rank_total_width
    req_devices = lax.axis_size("req")
    req_index = lax.axis_index("req")
    mdl_index = lax.axis_index("mdl")
    row_share = tok_count // lax.axis_size("mdl")
    cap_slots = max(2, (req_per_dev + req_devices - 1) // req_devices + 1)
    cap_slots += cap_slots % 2

    order_ids = jnp.arange(req_per_dev, dtype=jnp.int32)
    owner_table = last_page_holder[:, 0].reshape(req_devices, req_per_dev)
    slot_table = holder_page_slot.reshape(req_devices, req_per_dev)
    offset_table = page_filled_rows.reshape(req_devices, req_per_dev) - WINDOW
    owned = (owner_table == req_index).astype(jnp.int32)
    earlier_one = (order_ids[:, None] > order_ids[None, :]).astype(jnp.int32)
    owned_rank = jnp.sum(owned[:, None, :] * earlier_one[None], axis=2)
    picked = owned[:, None, :] * (
        owned_rank[:, None, :] == jnp.arange(cap_slots, dtype=jnp.int32)[None, :, None]
    ).astype(jnp.int32)
    send_slot = jnp.sum(picked * slot_table[:, None, :], axis=2)
    send_offset = jnp.sum(picked * offset_table[:, None, :], axis=2)
    packed = pack_windows(prefix_cache_store, send_slot, send_offset, cap_slots)
    rows_held = feedforward_weight.shape[1]
    ringed = (lax.axis_size("mdl"), tok_count // BLOCK, req_devices % 2, rows_held % 32) == (4, 4, 0, 0)
    if ringed:
        gate_up = Ring(feedforward_weight[:2], req_devices)
        gate_up.step()
        (packed,) = gate_up.tie(packed)
        gate_up.step()
    arrived = lax.all_to_all(packed, "req", split_axis=0, concat_axis=0, tiled=True)

    projected_rows = [
        lax.dot_general(
            stream, attention_projection_weight[k], NT, preferred_element_type=jnp.float32
        )
        for k in range(3)
    ]
    holder_count = adapter_down_maps.shape[0]
    holder_rank_rows = jnp.einsum(
        "qf,kfn->qkn", stream, adapter_down_maps, preferred_element_type=jnp.float32
    )
    held_onehot = (
        token_adapter_index[:, None]
        == (mdl_index * holder_count + jnp.arange(holder_count, dtype=jnp.int32))[None, :]
    )
    rank_part = jnp.sum(holder_rank_rows * held_onehot.astype(jnp.float32)[:, :, None], axis=1)
    rank_feat = lax.psum(rank_part.astype(jnp.bfloat16), "mdl")
    all_onehot = (
        token_adapter_index[:, None] == jnp.arange(adapter_number, dtype=jnp.int32)[None, :]
    )
    broadcast_result = (
        all_onehot.astype(jnp.bfloat16)[:, :, None] * rank_feat[:, None, :]
    ).reshape(tok_count, adapter_number * rank_total_width)
    lora_query = lax.dot_general(
        broadcast_result, adapter_up_maps[0], NT, preferred_element_type=jnp.float32
    )
    lora_value = lax.dot_general(
        broadcast_result, adapter_up_maps[1], NT, preferred_element_type=jnp.float32
    )

    positions = jnp.arange(tok_count, dtype=jnp.int32)
    lengths_row = request_token_lengths[0]
    ends = jnp.sum(
        jnp.where(order_ids[:, None] >= order_ids[None, :], lengths_row[None, :], 0), axis=1
    )
    starts = ends - lengths_row
    member = (positions[:, None] >= starts[None, :]) & (positions[:, None] < ends[None, :])
    member_int = member.astype(jnp.int32)
    start_of = jnp.sum(member_int * starts[None, :], axis=1, keepdims=True)
    my_owner = lax.dynamic_slice_in_dim(owner_table, req_index, 1, 0)[0]
    earlier = (my_owner[:, None] == my_owner[None, :]).astype(jnp.int32) * earlier_one
    slot_in = my_owner * cap_slots + jnp.sum(earlier, axis=1)
    slot_of = jnp.sum(member_int * slot_in[None, :], axis=1, keepdims=True)
    tenant_hot = (
        request_tenant_index[:, None]
        == jnp.arange(tenant_adapter_scale.shape[0], dtype=jnp.int32)[None, :]
    ).astype(jnp.float32)
    request_scale = jnp.sum(tenant_hot * tenant_adapter_scale[None, :], axis=1)
    per_token_scale = jnp.sum(member.astype(jnp.float32) * request_scale[None, :], axis=1)[:, None]
    query_rows = (projected_rows[0] + per_token_scale * lora_query).astype(jnp.bfloat16)
    key_rows = projected_rows[1].astype(jnp.bfloat16)
    value_rows = (projected_rows[2] + per_token_scale * lora_value).astype(jnp.bfloat16)

    prefix = arrived.reshape((-1,) + arrived.shape[2:])
    blocks = tok_count // BLOCK
    if ringed:
        prefix, query_rows, key_rows, value_rows = gate_up.tie(
            prefix, query_rows, key_rows, value_rows
        )
        for _ in range(3, req_devices // 2):
            gate_up.step()
        origins = gate_up.origins(req_index, req_devices)
        order = jnp.stack([mdl_index ^ 1, mdl_index ^ 3, mdl_index ^ 2, mdl_index]).astype(jnp.int32)
        send, keep, own = attention(
            order, (2, 1, 1), query_rows, key_rows, value_rows, start_of, slot_of, prefix,
            head_output_weight,
        )
        (send,) = gate_up.tie(send)
        gate_up.last()
        (down_block,) = gate_up.tie(feedforward_weight[2])
        down = Ring(down_block, req_devices)
        for _ in range(1, req_devices // 2):
            down.step()
        down.last()
        stream_mine = lax.dynamic_slice_in_dim(stream, mdl_index * row_share, row_share, 0)
        resid = (stream_mine.astype(jnp.float32) + scatter_sum(own, send, keep)).astype(jnp.bfloat16)
        normed = normalise(resid, feedforward_norm_gain)
        across = chip_swap(normed)
        hidden = hidden_units(
            origins, gate_up.arrays(), [normed, core_swap(normed), across, core_swap(across)]
        )
        early, late = 2, req_devices // 2
        forward, backward = down.forward, down.backward
        early_pieces = forward[: early + 1] + backward[1 : early + 1]
        late_pieces = forward[early + 1 : late] + backward[early + 1 : late] + [forward[late], backward[late]]
        hold = list(range(early + 1)) + [late + 1 + k for k in range(early)]
        hold += list(range(early + 1, late)) + [late + 1 + k for k in range(early, late - 1)] + [late]
        own, other, keep, send = down_sums(early_pieces, hidden)
        send, *late_pieces = lax.optimization_barrier([send] + late_pieces)
        part, hidden = lax.optimization_barrier((sum_on_chip(keep, send), hidden))
        early_sum = sum_here(own, other, chip_swap(part))
        own, other, keep, send = down_sums(late_pieces, hidden)
        part, early_sum = lax.optimization_barrier((sum_on_chip(keep, send), early_sum))
        groups = [early_sum], [own, core_swap(other), chip_swap(part)]
        return place_and_add(origins[jnp.array(hold)], resid, groups, rows_held)

    (attn_part,) = attention(
        jnp.arange(blocks, dtype=jnp.int32), (blocks,), query_rows, key_rows, value_rows, start_of,
        slot_of, prefix, head_output_weight,
    )
    attn_full = lax.psum(attn_part, "mdl").astype(jnp.float32)
    resid = (stream.astype(jnp.float32) + attn_full).astype(jnp.bfloat16)
    normed = normalise(resid, feedforward_norm_gain)
    resid_mine = lax.dynamic_slice_in_dim(resid, mdl_index * row_share, row_share, 0)
    full_mlp = lax.all_gather(feedforward_weight, "req", axis=1, tiled=True)
    gate_part = jnp.dot(normed, full_mlp[0], preferred_element_type=jnp.float32)
    up_part = jnp.dot(normed, full_mlp[1], preferred_element_type=jnp.float32)
    hidden = (jax.nn.silu(gate_part) * up_part).astype(jnp.bfloat16)
    mlp_part = lax.dot_general(
        hidden, full_mlp[2], NT, preferred_element_type=jnp.float32
    ).astype(jnp.bfloat16)
    mlp_mine = lax.psum_scatter(mlp_part, "mdl", scatter_dimension=0, tiled=True)
    return (resid_mine.astype(jnp.float32) + mlp_mine.astype(jnp.float32)).astype(jnp.bfloat16)


def solution(mesh):
    return jax.shard_map(
        per_device,
        mesh=mesh,
        in_specs=(
            P("req", None),
            P(None, "mdl", None),
            P("mdl", None),
            P("mdl", None, None),
            P(None, "mdl", None),
            P(),
            P(),
            P(None, "req", "mdl"),
            P("req", None, "mdl", None),
            P("req"),
            P("req", None),
            P("req"),
            P(),
            P(),
            P(),
        ),
        out_specs=P(("req", "mdl"), None),
        check_vma=False,
    )
```

```python
import functools
import math

import jax
import jax.numpy as jnp
from jax import lax
from jax.experimental import pallas as pl
from jax.experimental.pallas import tpu as pltpu
from jax.sharding import PartitionSpec as P

HEAD_SIZE = 112
WINDOW = 64
BLOCK = 192
HALO = 64
LANES = 256
VMEM_LIMIT = 48 * 1024 * 1024
NT = (((1,), (1,)), ((), ()))
SMALL = pl.CostEstimate(flops=0, bytes_accessed=0, transcendentals=0)


def pack_kernel(cap, table_ref, offset_ref, *refs):
    page_refs, out_ref = refs[:cap], refs[cap]
    dest = pl.program_id(0)
    lane = lax.broadcasted_iota(jnp.int32, out_ref.shape[3:], 1)
    for pair in range(cap // 2):
        first = offset_ref[dest * cap + 2 * pair]
        second = offset_ref[dest * cap + 2 * pair + 1]
        for part in range(2):
            left = page_refs[2 * pair][0, part].astype(jnp.float32)
            right = page_refs[2 * pair + 1][0, part].astype(jnp.float32)
            left = pltpu.roll(left, lax.rem(2 * WINDOW - first, 2 * WINDOW), 1)
            right = pltpu.roll(right, WINDOW - second, 1)
            out_ref[0, pair, part] = jnp.where(lane < WINDOW, left, right).astype(out_ref.dtype)


def pack_windows(pages, table, offsets, cap):
    parts = pages.shape[1:]
    dests = table.shape[0]

    def page_spec(place):
        return pl.BlockSpec(
            (1,) + parts, lambda dest, tbl, off: (tbl[dest * cap + place], 0, 0, 0)
        )

    return pl.pallas_call(
        functools.partial(pack_kernel, cap),
        grid_spec=pltpu.PrefetchScalarGridSpec(
            num_scalar_prefetch=2,
            grid=(dests,),
            in_specs=[page_spec(place) for place in range(cap)],
            out_specs=pl.BlockSpec(
                (1, cap // 2) + parts, lambda dest, tbl, off: (dest, 0, 0, 0, 0)
            ),
        ),
        out_shape=jax.ShapeDtypeStruct((dests, cap // 2) + parts, pages.dtype),
        compiler_params=pltpu.CompilerParams(vmem_limit_bytes=VMEM_LIMIT),
        cost_estimate=SMALL,
    )(table.reshape(-1), offsets.reshape(-1), *([pages] * cap))


def attention_kernel(
    order_ref, query_ref, key_before_ref, key_ref, value_before_ref, value_ref, start_ref, slot_ref,
    prefix_ref, weight_ref, *out_refs,
):
    *out_refs, mixed_ref = out_refs
    step = pl.program_id(0)
    block = order_ref[step]
    pairs = prefix_ref.shape[0]
    heads = query_ref.shape[1] // HEAD_SIZE
    inv_scale = 1.0 / math.sqrt(HEAD_SIZE)
    start = start_ref[...]
    slot = slot_ref[...]
    own = block * BLOCK + lax.broadcasted_iota(jnp.int32, (BLOCK, 1), 0)
    other = block * BLOCK - HALO + lax.broadcasted_iota(jnp.int32, (1, HALO + BLOCK), 1)
    local_ok = (other >= jnp.maximum(start, own - WINDOW)) & (other <= own)
    lane = lax.broadcasted_iota(jnp.int32, (1, 2 * WINDOW), 1)
    pair_of = lax.shift_right_logical(slot, 1)
    lane_low = lax.bitwise_and(slot, 1) * WINDOW
    prefix_ok = (lane >= lane_low + (own - start)) & (lane < lane_low + WINDOW)
    in_pair = [jnp.broadcast_to(pair_of == pair, (BLOCK, 2 * WINDOW)) for pair in range(pairs)]
    for head in range(heads):
        columns = slice(head * HEAD_SIZE, (head + 1) * HEAD_SIZE)
        query = query_ref[:, columns]
        keys = jnp.concatenate([key_before_ref[:, columns], key_ref[:, columns]], axis=0)
        values = jnp.concatenate([value_before_ref[:, columns], value_ref[:, columns]], axis=0)
        local = lax.dot_general(query, keys, NT, preferred_element_type=jnp.float32)
        local = jnp.where(local_ok, local * inv_scale, -1e30)
        remote = jnp.zeros((BLOCK, 2 * WINDOW), jnp.float32)
        for pair in range(0, pairs, 2):
            wide = jnp.dot(
                query,
                jnp.concatenate([prefix_ref[pair, 0, columns], prefix_ref[pair + 1, 0, columns]], axis=1),
                preferred_element_type=jnp.float32,
            )
            remote = jnp.where(in_pair[pair], wide[:, : 2 * WINDOW], remote)
            remote = jnp.where(in_pair[pair + 1], wide[:, 2 * WINDOW :], remote)
        remote = jnp.where(prefix_ok, remote * inv_scale, -1e30)
        top = jnp.maximum(
            jnp.max(local, axis=1, keepdims=True), jnp.max(remote, axis=1, keepdims=True)
        )
        local = jnp.exp(local - top)
        remote = jnp.exp(remote - top)
        total = jnp.sum(local, axis=1, keepdims=True) + jnp.sum(remote, axis=1, keepdims=True)
        remote = remote.astype(jnp.bfloat16)
        spread = jnp.concatenate(
            [jnp.where(in_pair[pair], remote, jnp.zeros_like(remote)) for pair in range(pairs)], axis=1
        )
        held = jnp.concatenate([prefix_ref[pair, 1, columns] for pair in range(pairs)], axis=1)
        mixed = jnp.dot(local.astype(jnp.bfloat16), values, preferred_element_type=jnp.float32)
        mixed = mixed + lax.dot_general(spread, held, NT, preferred_element_type=jnp.float32)
        mixed_ref[:, columns] = (mixed * (1.0 / total)).astype(jnp.bfloat16)
    projected = jnp.dot(
        mixed_ref[...], weight_ref[...], preferred_element_type=jnp.float32
    ).astype(jnp.bfloat16)
    first = 0
    for out_ref in out_refs:
        span = out_ref.shape[0] // BLOCK

        @pl.when((step >= first) & (step < first + span))
        def _(out_ref=out_ref, first=first):
            rows = pl.multiple_of((step - first) * BLOCK, BLOCK)
            out_ref[pl.ds(rows, BLOCK), :] = projected

        first += span


def attention(order, spans, query, key, value, start, slot, prefix, weight):
    tokens, width = query.shape
    model = weight.shape[1]
    step = BLOCK // HALO
    own = pl.BlockSpec((BLOCK, width), lambda i, order: (order[i], 0))
    before = pl.BlockSpec((HALO, width), lambda i, order: (jnp.maximum(order[i] * step - 1, 0), 0))
    column = pl.BlockSpec((BLOCK, 1), lambda i, order: (order[i], 0))
    return pl.pallas_call(
        attention_kernel,
        grid_spec=pltpu.PrefetchScalarGridSpec(
            num_scalar_prefetch=1,
            grid=(tokens // BLOCK,),
            in_specs=[
                own, before, own, before, own, column, column,
                pl.BlockSpec(prefix.shape, lambda i, order: (0, 0, 0, 0)),
                pl.BlockSpec(weight.shape, lambda i, order: (0, 0)),
            ],
            out_specs=[pl.BlockSpec((span * BLOCK, model), lambda i, order: (0, 0)) for span in spans],
            scratch_shapes=[pltpu.VMEM((BLOCK, width), jnp.bfloat16)],
        ),
        out_shape=[jax.ShapeDtypeStruct((span * BLOCK, model), jnp.bfloat16) for span in spans],
        compiler_params=pltpu.CompilerParams(vmem_limit_bytes=VMEM_LIMIT),
        cost_estimate=SMALL,
    )(order, query, key, key, value, value, start, slot, prefix, weight)


def ring_place(index, count):
    return jnp.where(index % 2 == 0, index // 2, count - 1 - index // 2)


def ring_index(place, count):
    place = (place + count) % count
    return jnp.where(place < count // 2, 2 * place, 2 * (count - 1 - place) + 1)


class Ring:
    def __init__(self, block, count):
        cycle = list(range(0, count, 2)) + list(range(count - 1, 0, -2))
        self.pairs = [(cycle[at], cycle[(at + 1) % count]) for at in range(count)]
        self.forward, self.backward = [block], [block]

    def step_forward(self, rows=slice(None)):
        self.forward.append(lax.ppermute(self.forward[-1][rows], "req", self.pairs))

    def step_backward(self, rows=slice(None)):
        pairs = [(there, here) for here, there in self.pairs]
        self.backward.append(lax.ppermute(self.backward[-1][rows], "req", pairs))


def step(*rings):
    for ring in rings:
        ring.step_forward()
        ring.step_backward()


def tie(rings, *others):
    last = [side[-1] for ring in rings for side in (ring.forward, ring.backward)]
    last, others = lax.optimization_barrier((last, others))
    for ring in rings:
        ring.forward[-1], ring.backward[-1], *last = last
    return others


def ring_origins(index, count, steps):
    place = ring_place(index, count)
    return jnp.stack([ring_index(place + step, count) for step in steps]).astype(jnp.int32)


def hidden_kernel(pieces, origin_ref, *refs):
    gate_refs, up_refs, refs = refs[:pieces], refs[pieces : 2 * pieces], refs[2 * pieces :]
    *block_refs, hidden_ref, all_ref, gate_ref, up_ref, sems = refs
    depth, width = gate_refs[0].shape
    chunks = [slice(0, LANES), slice(LANES, width)]
    copies = [[], []]
    for part, (piece_refs, buffer) in enumerate([(gate_refs, gate_ref), (up_refs, up_ref)]):
        for number, piece_ref in enumerate(piece_refs):
            rows = pl.ds(pl.multiple_of(origin_ref[part * pieces + number] * depth, 16), depth)
            for chunk, columns in enumerate(chunks):
                copies[chunk].append(
                    pltpu.make_async_copy(
                        piece_ref.at[:, columns],
                        buffer.at[rows, columns],
                        sems.at[chunk, part * pieces + number],
                    )
                )
    for chunk in copies:
        for copy in chunk:
            copy.start()
    for number, block_ref in enumerate(block_refs):
        rows = block_ref.shape[0]
        all_ref[number * rows : (number + 1) * rows, :] = block_ref[...]
    for first in range(0, width, LANES):
        columns = slice(first, min(first + LANES, width))
        if first in (0, LANES):
            for copy in copies[first // LANES]:
                copy.wait()
        gate = jnp.dot(all_ref[...], gate_ref[:, columns], preferred_element_type=jnp.float32)
        up = jnp.dot(all_ref[...], up_ref[:, columns], preferred_element_type=jnp.float32)
        hidden_ref[:, columns] = (gate / (1.0 + jnp.exp(-gate)) * up).astype(jnp.bfloat16)


def hidden_units(origins, gate_pieces, up_pieces, blocks):
    width = gate_pieces[0].shape[1]
    tokens = sum(block.shape[0] for block in blocks)
    model = blocks[0].shape[1]
    count = len(gate_pieces)
    pieces = gate_pieces + up_pieces
    smem = pl.BlockSpec(memory_space=pltpu.SMEM)
    vmem = pl.BlockSpec(memory_space=pltpu.VMEM)
    anywhere = pl.BlockSpec(memory_space=pl.ANY)
    return pl.pallas_call(
        functools.partial(hidden_kernel, count),
        in_specs=[smem] + [anywhere] * len(pieces) + [vmem] * len(blocks),
        out_specs=vmem,
        out_shape=jax.ShapeDtypeStruct((tokens, width), jnp.bfloat16),
        scratch_shapes=[
            pltpu.VMEM((tokens, model), jnp.bfloat16),
            pltpu.VMEM((model, width), jnp.bfloat16),
            pltpu.VMEM((model, width), jnp.bfloat16),
            pltpu.SemaphoreType.DMA((2, len(pieces))),
        ],
        compiler_params=pltpu.CompilerParams(vmem_limit_bytes=VMEM_LIMIT),
        cost_estimate=SMALL,
    )(origins, *pieces, *blocks)


def down_kernel(pieces, hidden_ref, *refs):
    piece_refs, out_refs = refs[:pieces], refs[pieces:]
    hidden = hidden_ref[...]
    blocks = [piece_ref[...] for piece_ref in piece_refs]
    depth = blocks[0].shape[0]
    if blocks[-1].shape[0] < depth:
        blocks[-2:] = [jnp.concatenate(blocks[-2:], axis=0)]
    for number, block in enumerate(blocks):
        columns = slice(number * depth, (number + 1) * depth)
        part = lax.dot_general(hidden, block, NT, preferred_element_type=jnp.float32)
        first = 0
        for out_ref in out_refs:
            rows = out_ref.shape[0]
            out_ref[:, columns] = part[first : first + rows].astype(out_ref.dtype)
            first += rows


def down_sums(pieces, hidden):
    tokens = hidden.shape[0]
    columns = sum(piece.shape[0] for piece in pieces)
    vmem = pl.BlockSpec(memory_space=pltpu.VMEM)
    return pl.pallas_call(
        functools.partial(down_kernel, len(pieces)),
        in_specs=[vmem] * (1 + len(pieces)),
        out_specs=[vmem] * 4,
        out_shape=[jax.ShapeDtypeStruct((tokens // 4, columns), jnp.bfloat16)] * 4,
        compiler_params=pltpu.CompilerParams(vmem_limit_bytes=VMEM_LIMIT),
        cost_estimate=SMALL,
    )(hidden, *pieces)


def place_kernel(groups, depth, origin_ref, resid_ref, *refs):
    term_refs, (out_ref, sum_ref) = refs[:-2], refs[-2:]
    rows, model = out_ref.shape
    sum_ref[...] = jnp.zeros_like(sum_ref)
    number, span = 0, 3 * 128
    for count, parts in groups:
        terms, term_refs = term_refs[:parts], term_refs[parts:]
        total = sum(term_ref[...].astype(jnp.float32) for term_ref in terms)
        for entry in range(count):
            first = origin_ref[number] * depth
            block = total[:, entry * depth : (entry + 1) * depth]
            block = jnp.concatenate([block, jnp.zeros((rows, span - depth), jnp.float32)], axis=1)
            block = pltpu.roll(block, lax.rem(first, 128), 1)
            lanes = pl.ds(pl.multiple_of(lax.div(first, 128) * 128, 128), span)
            sum_ref[:, lanes] += block
            number += 1
    out_ref[...] = (resid_ref[...].astype(jnp.float32) + sum_ref[:, :model]).astype(out_ref.dtype)


def place_and_add(origins, resid, groups, depth):
    sizes = [(terms[0].shape[1] // depth, len(terms)) for terms in groups]
    smem = pl.BlockSpec(memory_space=pltpu.SMEM)
    vmem = pl.BlockSpec(memory_space=pltpu.VMEM)
    terms = [term for group in groups for term in group]
    rows, model = resid.shape
    return pl.pallas_call(
        functools.partial(place_kernel, sizes, depth),
        in_specs=[smem] + [vmem] * (1 + len(terms)),
        out_specs=vmem,
        out_shape=jax.ShapeDtypeStruct(resid.shape, resid.dtype),
        scratch_shapes=[pltpu.VMEM((rows, model + 128), jnp.float32)],
        compiler_params=pltpu.CompilerParams(vmem_limit_bytes=VMEM_LIMIT),
        cost_estimate=SMALL,
    )(origins, resid, *terms)


def core_swap(array):
    return lax.ppermute(array, "mdl", [(0, 1), (1, 0), (2, 3), (3, 2)])


def chip_swap(array):
    return lax.ppermute(array, "mdl", [(0, 2), (2, 0), (1, 3), (3, 1)])


def sum_on_chip(keep, send):
    wide = jnp.float32
    return (keep.astype(wide) + core_swap(send).astype(wide)).astype(keep.dtype)


def sum_here(own, other, across):
    wide = jnp.float32
    return own.astype(wide) + core_swap(other).astype(wide) + across.astype(wide)


def scatter_sum(own, send, keep):
    wide = jnp.float32
    rows = own.shape[0]
    near = core_swap(send)
    far = chip_swap((keep.astype(wide) + near[rows:].astype(wide)).astype(keep.dtype))
    return own.astype(wide) + near[:rows].astype(wide) + far.astype(wide)


def normalise(resid, gain):
    wide = resid.astype(jnp.float32)
    mean_sq = jnp.mean(wide * wide, axis=1, keepdims=True)
    return (wide * lax.rsqrt(mean_sq + 1e-06) * gain.astype(jnp.float32)[None, :]).astype(jnp.bfloat16)


def per_device(
    stream,
    attention_projection_weight,
    head_output_weight,
    adapter_down_maps,
    adapter_up_maps,
    tenant_adapter_scale,
    feedforward_norm_gain,
    feedforward_weight,
    prefix_cache_store,
    token_adapter_index,
    request_token_lengths,
    request_tenant_index,
    last_page_holder,
    holder_page_slot,
    page_filled_rows,
):
    tok_count, model_width = stream.shape
    req_per_dev = request_token_lengths.shape[1]
    rank_total_width = adapter_down_maps.shape[2]
    adapter_number = adapter_up_maps.shape[2] // rank_total_width
    req_devices = lax.axis_size("req")
    req_index = lax.axis_index("req")
    mdl_index = lax.axis_index("mdl")
    row_share = tok_count // lax.axis_size("mdl")
    cap_slots = max(2, (req_per_dev + req_devices - 1) // req_devices + 1)
    cap_slots += cap_slots % 2

    order_ids = jnp.arange(req_per_dev, dtype=jnp.int32)
    owner_table = last_page_holder[:, 0].reshape(req_devices, req_per_dev)
    slot_table = holder_page_slot.reshape(req_devices, req_per_dev)
    offset_table = page_filled_rows.reshape(req_devices, req_per_dev) - WINDOW
    owned = (owner_table == req_index).astype(jnp.int32)
    earlier_one = (order_ids[:, None] > order_ids[None, :]).astype(jnp.int32)
    owned_rank = jnp.sum(owned[:, None, :] * earlier_one[None], axis=2)
    picked = owned[:, None, :] * (
        owned_rank[:, None, :] == jnp.arange(cap_slots, dtype=jnp.int32)[None, :, None]
    ).astype(jnp.int32)
    send_slot = jnp.sum(picked * slot_table[:, None, :], axis=2)
    send_offset = jnp.sum(picked * offset_table[:, None, :], axis=2)
    packed = pack_windows(prefix_cache_store, send_slot, send_offset, cap_slots)
    rows_held = feedforward_weight.shape[1]
    ringed = (lax.axis_size("mdl"), tok_count // BLOCK, req_devices, rows_held % 32) == (4, 4, 8, 0)
    if ringed:
        half = req_devices // 2
        near_steps = [-k for k in range(3)] + [1, 2]
        far_steps = [sign * k for k in range(3, half) for sign in (-1, 1)] + [half]
        gate_steps = [-k for k in range(half + 1)] + list(range(1, half))
        up_steps = [-k for k in range(half)] + list(range(1, half + 1))
        origins = ring_origins(req_index, req_devices, gate_steps + up_steps)
        down_origins = ring_origins(req_index, req_devices, near_steps + far_steps)
        gate, up = Ring(feedforward_weight[0], req_devices), Ring(feedforward_weight[1], req_devices)
        step(gate, up)
        (packed,) = tie([gate, up], packed)
        step(gate, up)
    arrived = lax.all_to_all(packed, "req", split_axis=0, concat_axis=0, tiled=True)

    projected_rows = [
        lax.dot_general(
            stream, attention_projection_weight[k], NT, preferred_element_type=jnp.float32
        )
        for k in range(3)
    ]
    holder_count = adapter_down_maps.shape[0]
    holder_rank_rows = jnp.einsum(
        "qf,kfn->qkn", stream, adapter_down_maps, preferred_element_type=jnp.float32
    )
    held_onehot = (
        token_adapter_index[:, None]
        == (mdl_index * holder_count + jnp.arange(holder_count, dtype=jnp.int32))[None, :]
    )
    rank_part = jnp.sum(holder_rank_rows * held_onehot.astype(jnp.float32)[:, :, None], axis=1)
    rank_feat = lax.psum(rank_part.astype(jnp.bfloat16), "mdl")
    all_onehot = (
        token_adapter_index[:, None] == jnp.arange(adapter_number, dtype=jnp.int32)[None, :]
    )
    broadcast_result = (
        all_onehot.astype(jnp.bfloat16)[:, :, None] * rank_feat[:, None, :]
    ).reshape(tok_count, adapter_number * rank_total_width)
    lora_query = lax.dot_general(
        broadcast_result, adapter_up_maps[0], NT, preferred_element_type=jnp.float32
    )
    lora_value = lax.dot_general(
        broadcast_result, adapter_up_maps[1], NT, preferred_element_type=jnp.float32
    )

    positions = jnp.arange(tok_count, dtype=jnp.int32)
    lengths_row = request_token_lengths[0]
    ends = jnp.sum(
        jnp.where(order_ids[:, None] >= order_ids[None, :], lengths_row[None, :], 0), axis=1
    )
    starts = ends - lengths_row
    member = (positions[:, None] >= starts[None, :]) & (positions[:, None] < ends[None, :])
    member_int = member.astype(jnp.int32)
    start_of = jnp.sum(member_int * starts[None, :], axis=1, keepdims=True)
    my_owner = lax.dynamic_slice_in_dim(owner_table, req_index, 1, 0)[0]
    earlier = (my_owner[:, None] == my_owner[None, :]).astype(jnp.int32) * earlier_one
    slot_in = my_owner * cap_slots + jnp.sum(earlier, axis=1)
    slot_of = jnp.sum(member_int * slot_in[None, :], axis=1, keepdims=True)
    tenant_hot = (
        request_tenant_index[:, None]
        == jnp.arange(tenant_adapter_scale.shape[0], dtype=jnp.int32)[None, :]
    ).astype(jnp.float32)
    request_scale = jnp.sum(tenant_hot * tenant_adapter_scale[None, :], axis=1)
    per_token_scale = jnp.sum(member.astype(jnp.float32) * request_scale[None, :], axis=1)[:, None]
    query_rows = (projected_rows[0] + per_token_scale * lora_query).astype(jnp.bfloat16)
    key_rows = projected_rows[1].astype(jnp.bfloat16)
    value_rows = (projected_rows[2] + per_token_scale * lora_value).astype(jnp.bfloat16)

    prefix = arrived.reshape((-1,) + arrived.shape[2:])
    blocks = tok_count // BLOCK
    if ringed:
        prefix, query_rows, key_rows, value_rows = tie(
            [gate, up], prefix, query_rows, key_rows, value_rows
        )
        step(gate, up)
        order = jnp.stack([mdl_index ^ 1, mdl_index ^ 3, mdl_index ^ 2, mdl_index]).astype(jnp.int32)
        send, keep, own = attention(
            order, (2, 1, 1), query_rows, key_rows, value_rows, start_of, slot_of, prefix,
            head_output_weight,
        )
        (send,) = tie([gate, up], send)
        gate.step_forward()
        up.step_backward()
        (down_block,) = tie([gate, up], feedforward_weight[2])
        down = Ring(down_block, req_devices)
        for _ in range(1, half):
            step(down)
        stream_mine = lax.dynamic_slice_in_dim(stream, mdl_index * row_share, row_share, 0)
        resid = (stream_mine.astype(jnp.float32) + scatter_sum(own, send, keep)).astype(jnp.bfloat16)
        normed = normalise(resid, feedforward_norm_gain)
        across = chip_swap(normed)
        hidden = hidden_units(
            origins, gate.forward + gate.backward[1:], up.forward + up.backward[1:],
            [normed, core_swap(normed), across, core_swap(across)],
        )
        (hidden,) = tie([down], hidden)
        near_pieces = down.forward[:3] + down.backward[1:3]
        far_pieces = [side[k] for k in range(3, half) for side in (down.forward, down.backward)]
        down.step_forward(slice(0, rows_held // 2))
        down.step_backward(slice(rows_held // 2, rows_held))
        far_pieces += [down.forward[-1], down.backward[-1]]
        own, other, keep, send = down_sums(near_pieces, hidden)
        part, hidden = lax.optimization_barrier((sum_on_chip(keep, send), hidden))
        across = chip_swap(part)
        near_terms = own, other
        own, other, keep, send = down_sums(far_pieces, hidden)
        send, across = lax.optimization_barrier((send, across))
        near_sum = sum_here(*near_terms, across)
        part, near_sum = lax.optimization_barrier((sum_on_chip(keep, send), near_sum))
        groups = [near_sum], [own, core_swap(other), chip_swap(part)]
        return place_and_add(down_origins, resid, groups, rows_held)

    (attn_part,) = attention(
        jnp.arange(blocks, dtype=jnp.int32), (blocks,), query_rows, key_rows, value_rows, start_of,
        slot_of, prefix, head_output_weight,
    )
    attn_full = lax.psum(attn_part, "mdl").astype(jnp.float32)
    resid = (stream.astype(jnp.float32) + attn_full).astype(jnp.bfloat16)
    normed = normalise(resid, feedforward_norm_gain)
    resid_mine = lax.dynamic_slice_in_dim(resid, mdl_index * row_share, row_share, 0)
    full_mlp = lax.all_gather(feedforward_weight, "req", axis=1, tiled=True)
    gate_part = jnp.dot(normed, full_mlp[0], preferred_element_type=jnp.float32)
    up_part = jnp.dot(normed, full_mlp[1], preferred_element_type=jnp.float32)
    hidden = (jax.nn.silu(gate_part) * up_part).astype(jnp.bfloat16)
    mlp_part = lax.dot_general(
        hidden, full_mlp[2], NT, preferred_element_type=jnp.float32
    ).astype(jnp.bfloat16)
    mlp_mine = lax.psum_scatter(mlp_part, "mdl", scatter_dimension=0, tiled=True)
    return (resid_mine.astype(jnp.float32) + mlp_mine.astype(jnp.float32)).astype(jnp.bfloat16)


def solution(mesh):
    return jax.shard_map(
        per_device,
        mesh=mesh,
        in_specs=(
            P("req", None),
            P(None, "mdl", None),
            P("mdl", None),
            P("mdl", None, None),
            P(None, "mdl", None),
            P(),
            P(),
            P(None, "req", "mdl"),
            P("req", None, "mdl", None),
            P("req"),
            P("req", None),
            P("req"),
            P(),
            P(),
            P(),
        ),
        out_specs=P(("req", "mdl"), None),
        check_vma=False,
    )
```

```python
import functools
import math

import jax
import jax.numpy as jnp
from jax import lax
from jax.experimental import pallas as pl
from jax.experimental.pallas import tpu as pltpu
from jax.sharding import PartitionSpec as P

HEAD_SIZE = 112
WINDOW = 64
BLOCK = 192
HALO = 64
LANES = 256
VMEM_LIMIT = 48 * 1024 * 1024
NT = (((1,), (1,)), ((), ()))
SMALL = pl.CostEstimate(flops=0, bytes_accessed=0, transcendentals=0)


def pack_kernel(cap, table_ref, offset_ref, *refs):
    page_refs, out_ref = refs[:cap], refs[cap]
    dest = pl.program_id(0)
    lane = lax.broadcasted_iota(jnp.int32, out_ref.shape[3:], 1)
    for pair in range(cap // 2):
        first = offset_ref[dest * cap + 2 * pair]
        second = offset_ref[dest * cap + 2 * pair + 1]
        for part in range(2):
            left = page_refs[2 * pair][0, part].astype(jnp.float32)
            right = page_refs[2 * pair + 1][0, part].astype(jnp.float32)
            left = pltpu.roll(left, lax.rem(2 * WINDOW - first, 2 * WINDOW), 1)
            right = pltpu.roll(right, WINDOW - second, 1)
            out_ref[0, pair, part] = jnp.where(lane < WINDOW, left, right).astype(out_ref.dtype)


def pack_windows(pages, table, offsets, cap):
    parts = pages.shape[1:]
    dests = table.shape[0]

    def page_spec(place):
        return pl.BlockSpec(
            (1,) + parts, lambda dest, tbl, off: (tbl[dest * cap + place], 0, 0, 0)
        )

    return pl.pallas_call(
        functools.partial(pack_kernel, cap),
        grid_spec=pltpu.PrefetchScalarGridSpec(
            num_scalar_prefetch=2,
            grid=(dests,),
            in_specs=[page_spec(place) for place in range(cap)],
            out_specs=pl.BlockSpec(
                (1, cap // 2) + parts, lambda dest, tbl, off: (dest, 0, 0, 0, 0)
            ),
        ),
        out_shape=jax.ShapeDtypeStruct((dests, cap // 2) + parts, pages.dtype),
        compiler_params=pltpu.CompilerParams(vmem_limit_bytes=VMEM_LIMIT),
        cost_estimate=SMALL,
    )(table.reshape(-1), offsets.reshape(-1), *([pages] * cap))


def attention_kernel(
    query_ref, key_before_ref, key_ref, value_before_ref, value_ref, start_ref, slot_ref, prefix_ref,
    out_ref, mixed_ref,
):
    block = pl.program_id(0)
    pairs = prefix_ref.shape[0]
    heads = query_ref.shape[1] // HEAD_SIZE
    inv_scale = 1.0 / math.sqrt(HEAD_SIZE)
    start = start_ref[...]
    slot = slot_ref[...]
    own = block * BLOCK + lax.broadcasted_iota(jnp.int32, (BLOCK, 1), 0)
    other = block * BLOCK - HALO + lax.broadcasted_iota(jnp.int32, (1, HALO + BLOCK), 1)
    local_ok = (other >= jnp.maximum(start, own - WINDOW)) & (other <= own)
    lane = lax.broadcasted_iota(jnp.int32, (1, 2 * WINDOW), 1)
    pair_of = lax.shift_right_logical(slot, 1)
    lane_low = lax.bitwise_and(slot, 1) * WINDOW
    prefix_ok = (lane >= lane_low + (own - start)) & (lane < lane_low + WINDOW)
    in_pair = [jnp.broadcast_to(pair_of == pair, (BLOCK, 2 * WINDOW)) for pair in range(pairs)]
    for head in range(heads):
        columns = slice(head * HEAD_SIZE, (head + 1) * HEAD_SIZE)
        query = query_ref[:, columns]
        keys = jnp.concatenate([key_before_ref[:, columns], key_ref[:, columns]], axis=0)
        values = jnp.concatenate([value_before_ref[:, columns], value_ref[:, columns]], axis=0)
        local = lax.dot_general(query, keys, NT, preferred_element_type=jnp.float32)
        local = jnp.where(local_ok, local * inv_scale, -1e30)
        remote = jnp.zeros((BLOCK, 2 * WINDOW), jnp.float32)
        for pair in range(0, pairs, 2):
            wide = jnp.dot(
                query,
                jnp.concatenate([prefix_ref[pair, 0, columns], prefix_ref[pair + 1, 0, columns]], axis=1),
                preferred_element_type=jnp.float32,
            )
            remote = jnp.where(in_pair[pair], wide[:, : 2 * WINDOW], remote)
            remote = jnp.where(in_pair[pair + 1], wide[:, 2 * WINDOW :], remote)
        remote = jnp.where(prefix_ok, remote * inv_scale, -1e30)
        top = jnp.maximum(
            jnp.max(local, axis=1, keepdims=True), jnp.max(remote, axis=1, keepdims=True)
        )
        local = jnp.exp(local - top)
        remote = jnp.exp(remote - top)
        total = jnp.sum(local, axis=1, keepdims=True) + jnp.sum(remote, axis=1, keepdims=True)
        remote = remote.astype(jnp.bfloat16)
        spread = jnp.concatenate(
            [jnp.where(in_pair[pair], remote, jnp.zeros_like(remote)) for pair in range(pairs)], axis=1
        )
        held = jnp.concatenate([prefix_ref[pair, 1, columns] for pair in range(pairs)], axis=1)
        mixed = jnp.dot(local.astype(jnp.bfloat16), values, preferred_element_type=jnp.float32)
        mixed = mixed + lax.dot_general(spread, held, NT, preferred_element_type=jnp.float32)
        mixed_ref[:, columns] = (mixed * (1.0 / total)).astype(jnp.bfloat16)
    width = mixed_ref.shape[1]
    for number in range(out_ref.shape[1] // width):

        @pl.when(block == number)
        def _(number=number):
            out_ref[:, number * width : (number + 1) * width] = mixed_ref[...]


def attention(query, key, value, start, slot, prefix):
    tokens, width = query.shape
    step = BLOCK // HALO
    own = pl.BlockSpec((BLOCK, width), lambda i: (i, 0))
    before = pl.BlockSpec((HALO, width), lambda i: (jnp.maximum(i * step - 1, 0), 0))
    column = pl.BlockSpec((BLOCK, 1), lambda i: (i, 0))
    wide = BLOCK, width * (tokens // BLOCK)
    return pl.pallas_call(
        attention_kernel,
        grid=(tokens // BLOCK,),
        in_specs=[
            own, before, own, before, own, column, column,
            pl.BlockSpec(prefix.shape, lambda i: (0, 0, 0, 0)),
        ],
        out_specs=pl.BlockSpec(wide, lambda i: (0, 0)),
        out_shape=jax.ShapeDtypeStruct(wide, jnp.bfloat16),
        scratch_shapes=[pltpu.VMEM((BLOCK, width), jnp.bfloat16)],
        compiler_params=pltpu.CompilerParams(vmem_limit_bytes=VMEM_LIMIT),
        cost_estimate=SMALL,
    )(query, key, key, value, value, start, slot, prefix)


def project_kernel(place_ref, *refs):
    mixed_refs, weight_refs, (stream_ref, gain_ref, normed_ref, resid_ref) = refs[:4], refs[4:8], refs[8:]
    rows = mixed_refs[0].shape[0]
    gain = gain_ref[...].astype(jnp.float32)
    for block in range(4):
        width = weight_refs[0].shape[0]
        columns = slice(block * width, (block + 1) * width)
        attn = sum(
            jnp.dot(mixed_ref[:, columns], weight_ref[...], preferred_element_type=jnp.float32)
            for mixed_ref, weight_ref in zip(mixed_refs, weight_refs)
        )
        resid = stream_ref[block * rows : (block + 1) * rows, :].astype(jnp.float32) + attn
        resid = resid.astype(resid_ref.dtype)

        @pl.when(place_ref[0] == block)
        def _():
            resid_ref[...] = resid

        wide = resid.astype(jnp.float32)
        mean_sq = jnp.mean(wide * wide, axis=1, keepdims=True)
        first = pl.multiple_of(jnp.bitwise_xor(place_ref[0], block) * rows, rows)
        normed_ref[pl.ds(first, rows), :] = (
            wide * lax.rsqrt(mean_sq + 1e-06) * gain
        ).astype(normed_ref.dtype)


def project_and_normalise(place, mixed, weights, stream, gain):
    tokens, model = stream.shape
    smem = pl.BlockSpec(memory_space=pltpu.SMEM)
    vmem = pl.BlockSpec(memory_space=pltpu.VMEM)
    return pl.pallas_call(
        project_kernel,
        in_specs=[smem] + [vmem] * 10,
        out_specs=[vmem] * 2,
        out_shape=[
            jax.ShapeDtypeStruct((tokens, model), stream.dtype),
            jax.ShapeDtypeStruct((tokens // 4, model), stream.dtype),
        ],
        compiler_params=pltpu.CompilerParams(vmem_limit_bytes=VMEM_LIMIT),
        cost_estimate=SMALL,
    )(place, *mixed, *weights, stream, gain)


def ring_place(index, count):
    return jnp.where(index % 2 == 0, index // 2, count - 1 - index // 2)


def ring_index(place, count):
    place = (place + count) % count
    return jnp.where(place < count // 2, 2 * place, 2 * (count - 1 - place) + 1)


class Ring:
    def __init__(self, block, count):
        cycle = list(range(0, count, 2)) + list(range(count - 1, 0, -2))
        self.pairs = [(cycle[at], cycle[(at + 1) % count]) for at in range(count)]
        self.forward, self.backward = [block], [block]

    def step_forward(self, rows=slice(None)):
        self.forward.append(lax.ppermute(self.forward[-1][rows], "req", self.pairs))

    def step_backward(self, rows=slice(None)):
        pairs = [(there, here) for here, there in self.pairs]
        self.backward.append(lax.ppermute(self.backward[-1][rows], "req", pairs))


def step(*rings):
    for ring in rings:
        ring.step_forward()
        ring.step_backward()


def tie(rings, *others):
    last = [side[-1] for ring in rings for side in (ring.forward, ring.backward)]
    last, others = lax.optimization_barrier((last, others))
    for ring in rings:
        ring.forward[-1], ring.backward[-1], *last = last
    return others


def ring_origins(index, count, steps):
    place = ring_place(index, count)
    return jnp.stack([ring_index(place + step, count) for step in steps]).astype(jnp.int32)


def hidden_kernel(pieces, origin_ref, *refs):
    gate_refs, up_refs, refs = refs[:pieces], refs[pieces : 2 * pieces], refs[2 * pieces :]
    normed_ref, hidden_ref, gate_ref, up_ref, sems = refs
    depth, width = gate_refs[0].shape
    chunks = [slice(0, LANES), slice(LANES, width)]
    copies = [[], []]
    for part, (piece_refs, buffer) in enumerate([(gate_refs, gate_ref), (up_refs, up_ref)]):
        for number, piece_ref in enumerate(piece_refs):
            rows = pl.ds(pl.multiple_of(origin_ref[part * pieces + number] * depth, 16), depth)
            for chunk, columns in enumerate(chunks):
                copies[chunk].append(
                    pltpu.make_async_copy(
                        piece_ref.at[:, columns],
                        buffer.at[rows, columns],
                        sems.at[chunk, part * pieces + number],
                    )
                )
    for chunk in copies:
        for copy in chunk:
            copy.start()
    for first in range(0, width, LANES):
        columns = slice(first, min(first + LANES, width))
        if first in (0, LANES):
            for copy in copies[first // LANES]:
                copy.wait()
        gate = jnp.dot(normed_ref[...], gate_ref[:, columns], preferred_element_type=jnp.float32)
        up = jnp.dot(normed_ref[...], up_ref[:, columns], preferred_element_type=jnp.float32)
        hidden_ref[:, columns] = (gate / (1.0 + jnp.exp(-gate)) * up).astype(jnp.bfloat16)


def hidden_units(origins, gate_pieces, up_pieces, normed):
    width = gate_pieces[0].shape[1]
    tokens, model = normed.shape
    count = len(gate_pieces)
    pieces = gate_pieces + up_pieces
    smem = pl.BlockSpec(memory_space=pltpu.SMEM)
    vmem = pl.BlockSpec(memory_space=pltpu.VMEM)
    anywhere = pl.BlockSpec(memory_space=pl.ANY)
    return pl.pallas_call(
        functools.partial(hidden_kernel, count),
        in_specs=[smem] + [anywhere] * len(pieces) + [vmem],
        out_specs=vmem,
        out_shape=jax.ShapeDtypeStruct((tokens, width), jnp.bfloat16),
        scratch_shapes=[
            pltpu.VMEM((model, width), jnp.bfloat16),
            pltpu.VMEM((model, width), jnp.bfloat16),
            pltpu.SemaphoreType.DMA((2, len(pieces))),
        ],
        compiler_params=pltpu.CompilerParams(vmem_limit_bytes=VMEM_LIMIT),
        cost_estimate=SMALL,
    )(origins, *pieces, normed)


def down_kernel(pieces, hidden_ref, *refs):
    piece_refs, out_refs = refs[:pieces], refs[pieces:]
    hidden = hidden_ref[...]
    blocks = [piece_ref[...] for piece_ref in piece_refs]
    depth = blocks[0].shape[0]
    if blocks[-1].shape[0] < depth:
        blocks[-2:] = [jnp.concatenate(blocks[-2:], axis=0)]
    for number, block in enumerate(blocks):
        columns = slice(number * depth, (number + 1) * depth)
        part = lax.dot_general(hidden, block, NT, preferred_element_type=jnp.float32)
        first = 0
        for out_ref in out_refs:
            rows = out_ref.shape[0]
            out_ref[:, columns] = part[first : first + rows].astype(out_ref.dtype)
            first += rows


def down_sums(pieces, hidden):
    tokens = hidden.shape[0]
    columns = sum(piece.shape[0] for piece in pieces)
    vmem = pl.BlockSpec(memory_space=pltpu.VMEM)
    return pl.pallas_call(
        functools.partial(down_kernel, len(pieces)),
        in_specs=[vmem] * (1 + len(pieces)),
        out_specs=[vmem] * 4,
        out_shape=[jax.ShapeDtypeStruct((tokens // 4, columns), jnp.bfloat16)] * 4,
        compiler_params=pltpu.CompilerParams(vmem_limit_bytes=VMEM_LIMIT),
        cost_estimate=SMALL,
    )(hidden, *pieces)


def place_kernel(groups, depth, origin_ref, resid_ref, *refs):
    term_refs, (out_ref, sum_ref) = refs[:-2], refs[-2:]
    rows, model = out_ref.shape
    sum_ref[...] = jnp.zeros_like(sum_ref)
    number, span = 0, 3 * 128
    for count, parts in groups:
        terms, term_refs = term_refs[:parts], term_refs[parts:]
        total = sum(term_ref[...].astype(jnp.float32) for term_ref in terms)
        for entry in range(count):
            first = origin_ref[number] * depth
            block = total[:, entry * depth : (entry + 1) * depth]
            block = jnp.concatenate([block, jnp.zeros((rows, span - depth), jnp.float32)], axis=1)
            block = pltpu.roll(block, lax.rem(first, 128), 1)
            lanes = pl.ds(pl.multiple_of(lax.div(first, 128) * 128, 128), span)
            sum_ref[:, lanes] += block
            number += 1
    out_ref[...] = (resid_ref[...].astype(jnp.float32) + sum_ref[:, :model]).astype(out_ref.dtype)


def place_and_add(origins, resid, groups, depth):
    sizes = [(terms[0].shape[1] // depth, len(terms)) for terms in groups]
    smem = pl.BlockSpec(memory_space=pltpu.SMEM)
    vmem = pl.BlockSpec(memory_space=pltpu.VMEM)
    terms = [term for group in groups for term in group]
    rows, model = resid.shape
    return pl.pallas_call(
        functools.partial(place_kernel, sizes, depth),
        in_specs=[smem] + [vmem] * (1 + len(terms)),
        out_specs=vmem,
        out_shape=jax.ShapeDtypeStruct(resid.shape, resid.dtype),
        scratch_shapes=[pltpu.VMEM((rows, model + 128), jnp.float32)],
        compiler_params=pltpu.CompilerParams(vmem_limit_bytes=VMEM_LIMIT),
        cost_estimate=SMALL,
    )(origins, resid, *terms)


def core_swap(array):
    return lax.ppermute(array, "mdl", [(0, 1), (1, 0), (2, 3), (3, 2)])


def chip_swap(array):
    return lax.ppermute(array, "mdl", [(0, 2), (2, 0), (1, 3), (3, 1)])


def gather_model(array):
    far = chip_swap(array)
    return [array, core_swap(array), far, core_swap(far)]


def sum_on_chip(keep, send):
    wide = jnp.float32
    return (keep.astype(wide) + core_swap(send).astype(wide)).astype(keep.dtype)


def sum_here(own, other, across):
    wide = jnp.float32
    return own.astype(wide) + core_swap(other).astype(wide) + across.astype(wide)


def normalise(resid, gain):
    wide = resid.astype(jnp.float32)
    mean_sq = jnp.mean(wide * wide, axis=1, keepdims=True)
    return (wide * lax.rsqrt(mean_sq + 1e-06) * gain.astype(jnp.float32)[None, :]).astype(jnp.bfloat16)


def per_device(
    stream,
    attention_projection_weight,
    head_output_weight,
    adapter_down_maps,
    adapter_up_maps,
    tenant_adapter_scale,
    feedforward_norm_gain,
    feedforward_weight,
    prefix_cache_store,
    token_adapter_index,
    request_token_lengths,
    request_tenant_index,
    last_page_holder,
    holder_page_slot,
    page_filled_rows,
):
    tok_count, model_width = stream.shape
    req_per_dev = request_token_lengths.shape[1]
    rank_total_width = adapter_down_maps.shape[2]
    adapter_number = adapter_up_maps.shape[2] // rank_total_width
    req_devices = lax.axis_size("req")
    req_index = lax.axis_index("req")
    mdl_index = lax.axis_index("mdl")
    row_share = tok_count // lax.axis_size("mdl")
    cap_slots = max(2, (req_per_dev + req_devices - 1) // req_devices + 1)
    cap_slots += cap_slots % 2

    order_ids = jnp.arange(req_per_dev, dtype=jnp.int32)
    owner_table = last_page_holder[:, 0].reshape(req_devices, req_per_dev)
    slot_table = holder_page_slot.reshape(req_devices, req_per_dev)
    offset_table = page_filled_rows.reshape(req_devices, req_per_dev) - WINDOW
    owned = (owner_table == req_index).astype(jnp.int32)
    earlier_one = (order_ids[:, None] > order_ids[None, :]).astype(jnp.int32)
    owned_rank = jnp.sum(owned[:, None, :] * earlier_one[None], axis=2)
    picked = owned[:, None, :] * (
        owned_rank[:, None, :] == jnp.arange(cap_slots, dtype=jnp.int32)[None, :, None]
    ).astype(jnp.int32)
    send_slot = jnp.sum(picked * slot_table[:, None, :], axis=2)
    send_offset = jnp.sum(picked * offset_table[:, None, :], axis=2)
    packed = pack_windows(prefix_cache_store, send_slot, send_offset, cap_slots)
    rows_held = feedforward_weight.shape[1]
    ringed = (lax.axis_size("mdl"), tok_count // BLOCK, req_devices, rows_held % 32) == (4, 4, 8, 0)
    if ringed:
        half = req_devices // 2
        near_steps = [-k for k in range(3)] + [1, 2]
        far_steps = [sign * k for k in range(3, half) for sign in (-1, 1)] + [half]
        gate_steps = [-k for k in range(half + 1)] + list(range(1, half))
        up_steps = [-k for k in range(half)] + list(range(1, half + 1))
        origins = ring_origins(req_index, req_devices, gate_steps + up_steps)
        down_origins = ring_origins(req_index, req_devices, near_steps + far_steps)
        gate, up = Ring(feedforward_weight[0], req_devices), Ring(feedforward_weight[1], req_devices)
        step(gate, up)
        (packed,) = tie([gate, up], packed)
        step(gate, up)
    arrived = lax.all_to_all(packed, "req", split_axis=0, concat_axis=0, tiled=True)

    projected_rows = [
        lax.dot_general(
            stream, attention_projection_weight[k], NT, preferred_element_type=jnp.float32
        )
        for k in range(3)
    ]
    holder_count = adapter_down_maps.shape[0]
    holder_rank_rows = jnp.einsum(
        "qf,kfn->qkn", stream, adapter_down_maps, preferred_element_type=jnp.float32
    )
    held_onehot = (
        token_adapter_index[:, None]
        == (mdl_index * holder_count + jnp.arange(holder_count, dtype=jnp.int32))[None, :]
    )
    rank_part = jnp.sum(holder_rank_rows * held_onehot.astype(jnp.float32)[:, :, None], axis=1)
    rank_feat = lax.psum(rank_part.astype(jnp.bfloat16), "mdl")
    all_onehot = (
        token_adapter_index[:, None] == jnp.arange(adapter_number, dtype=jnp.int32)[None, :]
    )
    broadcast_result = (
        all_onehot.astype(jnp.bfloat16)[:, :, None] * rank_feat[:, None, :]
    ).reshape(tok_count, adapter_number * rank_total_width)
    lora_query = lax.dot_general(
        broadcast_result, adapter_up_maps[0], NT, preferred_element_type=jnp.float32
    )
    lora_value = lax.dot_general(
        broadcast_result, adapter_up_maps[1], NT, preferred_element_type=jnp.float32
    )

    positions = jnp.arange(tok_count, dtype=jnp.int32)
    lengths_row = request_token_lengths[0]
    ends = jnp.sum(
        jnp.where(order_ids[:, None] >= order_ids[None, :], lengths_row[None, :], 0), axis=1
    )
    starts = ends - lengths_row
    member = (positions[:, None] >= starts[None, :]) & (positions[:, None] < ends[None, :])
    member_int = member.astype(jnp.int32)
    start_of = jnp.sum(member_int * starts[None, :], axis=1, keepdims=True)
    my_owner = lax.dynamic_slice_in_dim(owner_table, req_index, 1, 0)[0]
    earlier = (my_owner[:, None] == my_owner[None, :]).astype(jnp.int32) * earlier_one
    slot_in = my_owner * cap_slots + jnp.sum(earlier, axis=1)
    slot_of = jnp.sum(member_int * slot_in[None, :], axis=1, keepdims=True)
    tenant_hot = (
        request_tenant_index[:, None]
        == jnp.arange(tenant_adapter_scale.shape[0], dtype=jnp.int32)[None, :]
    ).astype(jnp.float32)
    request_scale = jnp.sum(tenant_hot * tenant_adapter_scale[None, :], axis=1)
    per_token_scale = jnp.sum(member.astype(jnp.float32) * request_scale[None, :], axis=1)[:, None]
    query_rows = (projected_rows[0] + per_token_scale * lora_query).astype(jnp.bfloat16)
    key_rows = projected_rows[1].astype(jnp.bfloat16)
    value_rows = (projected_rows[2] + per_token_scale * lora_value).astype(jnp.bfloat16)

    prefix = arrived.reshape((-1,) + arrived.shape[2:])
    blocks = tok_count // BLOCK
    if ringed:
        prefix, query_rows, key_rows, value_rows, *weights = tie(
            [gate, up], prefix, query_rows, key_rows, value_rows, *gather_model(head_output_weight)
        )
        step(gate, up)
        mixed = attention(query_rows, key_rows, value_rows, start_of, slot_of, prefix)
        (mixed,) = tie([gate, up], mixed)
        gate.step_forward()
        up.step_backward()
        (down_block,) = tie([gate, up], feedforward_weight[2])
        down = Ring(down_block, req_devices)
        step(down)
        normed, resid = project_and_normalise(
            mdl_index.reshape(1).astype(jnp.int32), gather_model(mixed), weights, stream,
            feedforward_norm_gain.reshape(1, model_width),
        )
        (normed,) = tie([down], normed)
        step(down)
        hidden = hidden_units(
            origins, gate.forward + gate.backward[1:], up.forward + up.backward[1:], normed
        )
        (hidden,) = tie([down], hidden)
        for _ in range(3, half):
            step(down)
        near_pieces = down.forward[:3] + down.backward[1:3]
        far_pieces = [side[k] for k in range(3, half) for side in (down.forward, down.backward)]
        down.step_forward(slice(0, rows_held // 2))
        down.step_backward(slice(rows_held // 2, rows_held))
        far_pieces += [down.forward[-1], down.backward[-1]]
        own, other, keep, send = down_sums(near_pieces, hidden)
        part, hidden = lax.optimization_barrier((sum_on_chip(keep, send), hidden))
        across = chip_swap(part)
        near_terms = own, other
        own, other, keep, send = down_sums(far_pieces, hidden)
        send, across = lax.optimization_barrier((send, across))
        near_sum = sum_here(*near_terms, across)
        part, near_sum = lax.optimization_barrier((sum_on_chip(keep, send), near_sum))
        groups = [near_sum], [own, core_swap(other), chip_swap(part)]
        return place_and_add(down_origins, resid, groups, rows_held)

    mixed = attention(query_rows, key_rows, value_rows, start_of, slot_of, prefix)
    mixed = jnp.concatenate(jnp.split(mixed, blocks, axis=1), axis=0)
    attn_part = jnp.dot(mixed, head_output_weight, preferred_element_type=jnp.float32).astype(jnp.bfloat16)
    attn_full = lax.psum(attn_part, "mdl").astype(jnp.float32)
    resid = (stream.astype(jnp.float32) + attn_full).astype(jnp.bfloat16)
    normed = normalise(resid, feedforward_norm_gain)
    resid_mine = lax.dynamic_slice_in_dim(resid, mdl_index * row_share, row_share, 0)
    full_mlp = lax.all_gather(feedforward_weight, "req", axis=1, tiled=True)
    gate_part = jnp.dot(normed, full_mlp[0], preferred_element_type=jnp.float32)
    up_part = jnp.dot(normed, full_mlp[1], preferred_element_type=jnp.float32)
    hidden = (jax.nn.silu(gate_part) * up_part).astype(jnp.bfloat16)
    mlp_part = lax.dot_general(
        hidden, full_mlp[2], NT, preferred_element_type=jnp.float32
    ).astype(jnp.bfloat16)
    mlp_mine = lax.psum_scatter(mlp_part, "mdl", scatter_dimension=0, tiled=True)
    return (resid_mine.astype(jnp.float32) + mlp_mine.astype(jnp.float32)).astype(jnp.bfloat16)


def solution(mesh):
    return jax.shard_map(
        per_device,
        mesh=mesh,
        in_specs=(
            P("req", None),
            P(None, "mdl", None),
            P("mdl", None),
            P("mdl", None, None),
            P(None, "mdl", None),
            P(),
            P(),
            P(None, "req", "mdl"),
            P("req", None, "mdl", None),
            P("req"),
            P("req", None),
            P("req"),
            P(),
            P(),
            P(),
        ),
        out_specs=P(("req", "mdl"), None),
        check_vma=False,
    )
```

```python
import functools
import math

import jax
import jax.numpy as jnp
from jax import lax
from jax.experimental import pallas as pl
from jax.experimental.pallas import tpu as pltpu
from jax.sharding import PartitionSpec as P

HEAD_SIZE = 112
WINDOW = 64
BLOCK = 192
HALO = 64
LANES = 256
VMEM_LIMIT = 48 * 1024 * 1024
NT = (((1,), (1,)), ((), ()))
SMALL = pl.CostEstimate(flops=0, bytes_accessed=0, transcendentals=0)


def pack_kernel(cap, table_ref, offset_ref, *refs):
    page_refs, out_ref = refs[:cap], refs[cap]
    dest = pl.program_id(0)
    lane = lax.broadcasted_iota(jnp.int32, out_ref.shape[3:], 1)
    for pair in range(cap // 2):
        first = offset_ref[dest * cap + 2 * pair]
        second = offset_ref[dest * cap + 2 * pair + 1]
        for part in range(2):
            left = page_refs[2 * pair][0, part].astype(jnp.float32)
            right = page_refs[2 * pair + 1][0, part].astype(jnp.float32)
            left = pltpu.roll(left, lax.rem(2 * WINDOW - first, 2 * WINDOW), 1)
            right = pltpu.roll(right, WINDOW - second, 1)
            out_ref[0, pair, part] = jnp.where(lane < WINDOW, left, right).astype(out_ref.dtype)


def pack_windows(pages, table, offsets, cap):
    parts = pages.shape[1:]
    dests = table.shape[0]

    def page_spec(place):
        return pl.BlockSpec(
            (1,) + parts, lambda dest, tbl, off: (tbl[dest * cap + place], 0, 0, 0)
        )

    return pl.pallas_call(
        functools.partial(pack_kernel, cap),
        grid_spec=pltpu.PrefetchScalarGridSpec(
            num_scalar_prefetch=2,
            grid=(dests,),
            in_specs=[page_spec(place) for place in range(cap)],
            out_specs=pl.BlockSpec(
                (1, cap // 2) + parts, lambda dest, tbl, off: (dest, 0, 0, 0, 0)
            ),
        ),
        out_shape=jax.ShapeDtypeStruct((dests, cap // 2) + parts, pages.dtype),
        compiler_params=pltpu.CompilerParams(vmem_limit_bytes=VMEM_LIMIT),
        cost_estimate=SMALL,
    )(table.reshape(-1), offsets.reshape(-1), *([pages] * cap))


def attention_kernel(
    query_ref, key_before_ref, key_ref, value_before_ref, value_ref, start_ref, slot_ref, prefix_ref,
    out_ref, mixed_ref,
):
    block = pl.program_id(0)
    pairs = prefix_ref.shape[0]
    heads = query_ref.shape[1] // HEAD_SIZE
    inv_scale = 1.0 / math.sqrt(HEAD_SIZE)
    start = start_ref[...]
    slot = slot_ref[...]
    own = block * BLOCK + lax.broadcasted_iota(jnp.int32, (BLOCK, 1), 0)
    other = block * BLOCK - HALO + lax.broadcasted_iota(jnp.int32, (1, HALO + BLOCK), 1)
    local_ok = (other >= jnp.maximum(start, own - WINDOW)) & (other <= own)
    lane = lax.broadcasted_iota(jnp.int32, (1, 2 * WINDOW), 1)
    pair_of = lax.shift_right_logical(slot, 1)
    lane_low = lax.bitwise_and(slot, 1) * WINDOW
    prefix_ok = (lane >= lane_low + (own - start)) & (lane < lane_low + WINDOW)
    in_pair = [jnp.broadcast_to(pair_of == pair, (BLOCK, 2 * WINDOW)) for pair in range(pairs)]
    for head in range(heads):
        columns = slice(head * HEAD_SIZE, (head + 1) * HEAD_SIZE)
        query = query_ref[:, columns]
        keys = jnp.concatenate([key_before_ref[:, columns], key_ref[:, columns]], axis=0)
        values = jnp.concatenate([value_before_ref[:, columns], value_ref[:, columns]], axis=0)
        local = lax.dot_general(query, keys, NT, preferred_element_type=jnp.float32)
        local = jnp.where(local_ok, local * inv_scale, -1e30)
        remote = jnp.zeros((BLOCK, 2 * WINDOW), jnp.float32)
        for pair in range(0, pairs, 2):
            wide = jnp.dot(
                query,
                jnp.concatenate([prefix_ref[pair, 0, columns], prefix_ref[pair + 1, 0, columns]], axis=1),
                preferred_element_type=jnp.float32,
            )
            remote = jnp.where(in_pair[pair], wide[:, : 2 * WINDOW], remote)
            remote = jnp.where(in_pair[pair + 1], wide[:, 2 * WINDOW :], remote)
        remote = jnp.where(prefix_ok, remote * inv_scale, -1e30)
        top = jnp.maximum(
            jnp.max(local, axis=1, keepdims=True), jnp.max(remote, axis=1, keepdims=True)
        )
        local = jnp.exp(local - top)
        remote = jnp.exp(remote - top)
        total = jnp.sum(local, axis=1, keepdims=True) + jnp.sum(remote, axis=1, keepdims=True)
        remote = remote.astype(jnp.bfloat16)
        spread = jnp.concatenate(
            [jnp.where(in_pair[pair], remote, jnp.zeros_like(remote)) for pair in range(pairs)], axis=1
        )
        held = jnp.concatenate([prefix_ref[pair, 1, columns] for pair in range(pairs)], axis=1)
        mixed = jnp.dot(local.astype(jnp.bfloat16), values, preferred_element_type=jnp.float32)
        mixed = mixed + lax.dot_general(spread, held, NT, preferred_element_type=jnp.float32)
        mixed_ref[:, columns] = (mixed * (1.0 / total)).astype(jnp.bfloat16)
    width = mixed_ref.shape[1]
    for number in range(out_ref.shape[1] // width):

        @pl.when(block == number)
        def _(number=number):
            out_ref[:, number * width : (number + 1) * width] = mixed_ref[...]


def attention(query, key, value, start, slot, prefix):
    tokens, width = query.shape
    step = BLOCK // HALO
    own = pl.BlockSpec((BLOCK, width), lambda i: (i, 0))
    before = pl.BlockSpec((HALO, width), lambda i: (jnp.maximum(i * step - 1, 0), 0))
    column = pl.BlockSpec((BLOCK, 1), lambda i: (i, 0))
    wide = BLOCK, width * (tokens // BLOCK)
    return pl.pallas_call(
        attention_kernel,
        grid=(tokens // BLOCK,),
        in_specs=[
            own, before, own, before, own, column, column,
            pl.BlockSpec(prefix.shape, lambda i: (0, 0, 0, 0)),
        ],
        out_specs=pl.BlockSpec(wide, lambda i: (0, 0)),
        out_shape=jax.ShapeDtypeStruct(wide, jnp.bfloat16),
        scratch_shapes=[pltpu.VMEM((BLOCK, width), jnp.bfloat16)],
        compiler_params=pltpu.CompilerParams(vmem_limit_bytes=VMEM_LIMIT),
        cost_estimate=SMALL,
    )(query, key, key, value, value, start, slot, prefix)


def project_kernel(place_ref, *refs):
    mixed_refs, weight_refs, refs = refs[:4], refs[4:8], refs[8:]
    stream_ref, gain_ref, normed_ref, mine_ref, mixed_all_ref, resid_ref = refs
    share, (tokens, model) = mine_ref.shape[0], resid_ref.shape
    width = weight_refs[0].shape[0]
    for number, mixed_ref in enumerate(mixed_refs):
        for block in range(4):
            mixed_all_ref[number, block * share : (block + 1) * share, :] = (
                mixed_ref[:, block * width : (block + 1) * width]
            )
    squares = jnp.zeros((tokens, 128), jnp.float32)
    for first in range(0, model, LANES):
        columns = slice(first, first + LANES)
        attn = sum(
            jnp.dot(mixed_all_ref[number], weight_ref[:, columns], preferred_element_type=jnp.float32)
            for number, weight_ref in enumerate(weight_refs)
        )
        resid = (stream_ref[:, columns].astype(jnp.float32) + attn).astype(resid_ref.dtype)
        resid_ref[:, columns] = resid
        wide = resid.astype(jnp.float32)
        for part in range(0, LANES, 128):
            squares = squares + wide[:, part : part + 128] * wide[:, part : part + 128]
    scale = lax.rsqrt(jnp.sum(squares, axis=1, keepdims=True) * (1.0 / model) + 1e-06)
    gain = gain_ref[...].astype(jnp.float32)
    own = pl.multiple_of(place_ref[0] * share, share)
    mine_ref[...] = resid_ref[pl.ds(own, share), :]
    for block in range(4):
        rows = slice(block * share, (block + 1) * share)
        first = pl.multiple_of(jnp.bitwise_xor(place_ref[0], block) * share, share)
        normed_ref[pl.ds(first, share), :] = (
            resid_ref[rows, :].astype(jnp.float32) * scale[rows] * gain
        ).astype(normed_ref.dtype)


def project_and_normalise(place, mixed, weights, stream, gain):
    tokens, model = stream.shape
    smem = pl.BlockSpec(memory_space=pltpu.SMEM)
    vmem = pl.BlockSpec(memory_space=pltpu.VMEM)
    return pl.pallas_call(
        project_kernel,
        in_specs=[smem] + [vmem] * 10,
        out_specs=[vmem] * 2,
        out_shape=[
            jax.ShapeDtypeStruct((tokens, model), stream.dtype),
            jax.ShapeDtypeStruct((tokens // 4, model), stream.dtype),
        ],
        scratch_shapes=[
            pltpu.VMEM((4, tokens, weights[0].shape[0]), jnp.bfloat16),
            pltpu.VMEM((tokens, model), jnp.bfloat16),
        ],
        compiler_params=pltpu.CompilerParams(vmem_limit_bytes=VMEM_LIMIT),
        cost_estimate=SMALL,
    )(place, *mixed, *weights, stream, gain)


def ring_place(index, count):
    return jnp.where(index % 2 == 0, index // 2, count - 1 - index // 2)


def ring_index(place, count):
    place = (place + count) % count
    return jnp.where(place < count // 2, 2 * place, 2 * (count - 1 - place) + 1)


class Ring:
    def __init__(self, block, count):
        cycle = list(range(0, count, 2)) + list(range(count - 1, 0, -2))
        self.pairs = [(cycle[at], cycle[(at + 1) % count]) for at in range(count)]
        self.forward, self.backward = [block], [block]

    def step_forward(self, rows=slice(None)):
        self.forward.append(lax.ppermute(self.forward[-1][rows], "req", self.pairs))

    def step_backward(self, rows=slice(None)):
        pairs = [(there, here) for here, there in self.pairs]
        self.backward.append(lax.ppermute(self.backward[-1][rows], "req", pairs))


def step(*rings):
    for ring in rings:
        ring.step_forward()
        ring.step_backward()


def tie(rings, *others):
    last = [side[-1] for ring in rings for side in (ring.forward, ring.backward)]
    last, others = lax.optimization_barrier((last, others))
    for ring in rings:
        ring.forward[-1], ring.backward[-1], *last = last
    return others


def ring_origins(index, count, steps):
    place = ring_place(index, count)
    return jnp.stack([ring_index(place + step, count) for step in steps]).astype(jnp.int32)


def hidden_kernel(pieces, origin_ref, *refs):
    gate_refs, up_refs, refs = refs[:pieces], refs[pieces : 2 * pieces], refs[2 * pieces :]
    normed_ref, hidden_ref, gate_ref, up_ref, sems = refs
    depth, width = gate_refs[0].shape
    chunks = [slice(0, LANES), slice(LANES, width)]
    copies = [[], []]
    for part, (piece_refs, buffer) in enumerate([(gate_refs, gate_ref), (up_refs, up_ref)]):
        for number, piece_ref in enumerate(piece_refs):
            rows = pl.ds(pl.multiple_of(origin_ref[part * pieces + number] * depth, 16), depth)
            for chunk, columns in enumerate(chunks):
                copies[chunk].append(
                    pltpu.make_async_copy(
                        piece_ref.at[:, columns],
                        buffer.at[rows, columns],
                        sems.at[chunk, part * pieces + number],
                    )
                )
    for chunk in copies:
        for copy in chunk:
            copy.start()
    for first in range(0, width, LANES):
        columns = slice(first, min(first + LANES, width))
        if first in (0, LANES):
            for copy in copies[first // LANES]:
                copy.wait()
        gate = jnp.dot(normed_ref[...], gate_ref[:, columns], preferred_element_type=jnp.float32)
        up = jnp.dot(normed_ref[...], up_ref[:, columns], preferred_element_type=jnp.float32)
        hidden_ref[:, columns] = (gate / (1.0 + jnp.exp(-gate)) * up).astype(jnp.bfloat16)


def hidden_units(origins, gate_pieces, up_pieces, normed):
    width = gate_pieces[0].shape[1]
    tokens, model = normed.shape
    count = len(gate_pieces)
    pieces = gate_pieces + up_pieces
    smem = pl.BlockSpec(memory_space=pltpu.SMEM)
    vmem = pl.BlockSpec(memory_space=pltpu.VMEM)
    anywhere = pl.BlockSpec(memory_space=pl.ANY)
    return pl.pallas_call(
        functools.partial(hidden_kernel, count),
        in_specs=[smem] + [anywhere] * len(pieces) + [vmem],
        out_specs=vmem,
        out_shape=jax.ShapeDtypeStruct((tokens, width), jnp.bfloat16),
        scratch_shapes=[
            pltpu.VMEM((model, width), jnp.bfloat16),
            pltpu.VMEM((model, width), jnp.bfloat16),
            pltpu.SemaphoreType.DMA((2, len(pieces))),
        ],
        compiler_params=pltpu.CompilerParams(vmem_limit_bytes=VMEM_LIMIT),
        cost_estimate=SMALL,
    )(origins, *pieces, normed)


def down_kernel(pieces, hidden_ref, *refs):
    piece_refs, out_refs = refs[:pieces], refs[pieces:]
    hidden = hidden_ref[...]
    blocks = [piece_ref[...] for piece_ref in piece_refs]
    depth = blocks[0].shape[0]
    if blocks[-1].shape[0] < depth:
        blocks[-2:] = [jnp.concatenate(blocks[-2:], axis=0)]
    for number, block in enumerate(blocks):
        columns = slice(number * depth, (number + 1) * depth)
        part = lax.dot_general(hidden, block, NT, preferred_element_type=jnp.float32)
        first = 0
        for out_ref in out_refs:
            rows = out_ref.shape[0]
            out_ref[:, columns] = part[first : first + rows].astype(out_ref.dtype)
            first += rows


def down_sums(pieces, hidden, cost=SMALL):
    tokens = hidden.shape[0]
    columns = sum(piece.shape[0] for piece in pieces)
    vmem = pl.BlockSpec(memory_space=pltpu.VMEM)
    return pl.pallas_call(
        functools.partial(down_kernel, len(pieces)),
        in_specs=[vmem] * (1 + len(pieces)),
        out_specs=[vmem] * 4,
        out_shape=[jax.ShapeDtypeStruct((tokens // 4, columns), jnp.bfloat16)] * 4,
        compiler_params=pltpu.CompilerParams(vmem_limit_bytes=VMEM_LIMIT),
        cost_estimate=cost,
    )(hidden, *pieces)


def place_kernel(groups, depth, origin_ref, resid_ref, *refs):
    term_refs, (out_ref, sum_ref) = refs[:-2], refs[-2:]
    rows, model = out_ref.shape
    sum_ref[...] = jnp.zeros_like(sum_ref)
    number, span = 0, 3 * 128
    for count, parts in groups:
        terms, term_refs = term_refs[:parts], term_refs[parts:]
        total = sum(term_ref[...].astype(jnp.float32) for term_ref in terms)
        for entry in range(count):
            first = origin_ref[number] * depth
            block = total[:, entry * depth : (entry + 1) * depth]
            block = jnp.concatenate([block, jnp.zeros((rows, span - depth), jnp.float32)], axis=1)
            block = pltpu.roll(block, lax.rem(first, 128), 1)
            lanes = pl.ds(pl.multiple_of(lax.div(first, 128) * 128, 128), span)
            sum_ref[:, lanes] += block
            number += 1
    out_ref[...] = (resid_ref[...].astype(jnp.float32) + sum_ref[:, :model]).astype(out_ref.dtype)


def place_and_add(origins, resid, groups, depth):
    sizes = [(terms[0].shape[1] // depth, len(terms)) for terms in groups]
    smem = pl.BlockSpec(memory_space=pltpu.SMEM)
    vmem = pl.BlockSpec(memory_space=pltpu.VMEM)
    terms = [term for group in groups for term in group]
    rows, model = resid.shape
    return pl.pallas_call(
        functools.partial(place_kernel, sizes, depth),
        in_specs=[smem] + [vmem] * (1 + len(terms)),
        out_specs=vmem,
        out_shape=jax.ShapeDtypeStruct(resid.shape, resid.dtype),
        scratch_shapes=[pltpu.VMEM((rows, model + 128), jnp.float32)],
        compiler_params=pltpu.CompilerParams(vmem_limit_bytes=VMEM_LIMIT),
        cost_estimate=SMALL,
    )(origins, resid, *terms)


def core_swap(array):
    return lax.ppermute(array, "mdl", [(0, 1), (1, 0), (2, 3), (3, 2)])


def chip_swap(array):
    return lax.ppermute(array, "mdl", [(0, 2), (2, 0), (1, 3), (3, 1)])


def gather_model(array):
    far = chip_swap(array)
    return [array, core_swap(array), far, core_swap(far)]


def sum_on_chip(keep, send):
    wide = jnp.float32
    return (keep.astype(wide) + core_swap(send).astype(wide)).astype(keep.dtype)


def sum_here(own, other, across):
    wide = jnp.float32
    return own.astype(wide) + core_swap(other).astype(wide) + across.astype(wide)


def normalise(resid, gain):
    wide = resid.astype(jnp.float32)
    mean_sq = jnp.mean(wide * wide, axis=1, keepdims=True)
    return (wide * lax.rsqrt(mean_sq + 1e-06) * gain.astype(jnp.float32)[None, :]).astype(jnp.bfloat16)


def per_device(
    stream,
    attention_projection_weight,
    head_output_weight,
    adapter_down_maps,
    adapter_up_maps,
    tenant_adapter_scale,
    feedforward_norm_gain,
    feedforward_weight,
    prefix_cache_store,
    token_adapter_index,
    request_token_lengths,
    request_tenant_index,
    last_page_holder,
    holder_page_slot,
    page_filled_rows,
):
    tok_count, model_width = stream.shape
    req_per_dev = request_token_lengths.shape[1]
    rank_total_width = adapter_down_maps.shape[2]
    adapter_number = adapter_up_maps.shape[2] // rank_total_width
    req_devices = lax.axis_size("req")
    req_index = lax.axis_index("req")
    mdl_index = lax.axis_index("mdl")
    row_share = tok_count // lax.axis_size("mdl")
    cap_slots = max(2, (req_per_dev + req_devices - 1) // req_devices + 1)
    cap_slots += cap_slots % 2

    order_ids = jnp.arange(req_per_dev, dtype=jnp.int32)
    owner_table = last_page_holder[:, 0].reshape(req_devices, req_per_dev)
    slot_table = holder_page_slot.reshape(req_devices, req_per_dev)
    offset_table = page_filled_rows.reshape(req_devices, req_per_dev) - WINDOW
    owned = (owner_table == req_index).astype(jnp.int32)
    earlier_one = (order_ids[:, None] > order_ids[None, :]).astype(jnp.int32)
    owned_rank = jnp.sum(owned[:, None, :] * earlier_one[None], axis=2)
    picked = owned[:, None, :] * (
        owned_rank[:, None, :] == jnp.arange(cap_slots, dtype=jnp.int32)[None, :, None]
    ).astype(jnp.int32)
    send_slot = jnp.sum(picked * slot_table[:, None, :], axis=2)
    send_offset = jnp.sum(picked * offset_table[:, None, :], axis=2)
    packed = pack_windows(prefix_cache_store, send_slot, send_offset, cap_slots)
    rows_held = feedforward_weight.shape[1]
    ringed = (lax.axis_size("mdl"), tok_count // BLOCK, req_devices, rows_held % 32) == (4, 4, 8, 0)
    if ringed:
        half = req_devices // 2
        near_steps = [-k for k in range(3)] + [1, 2]
        far_steps = [sign * k for k in range(3, half) for sign in (-1, 1)] + [half]
        gate_steps = [-k for k in range(half + 1)] + list(range(1, half))
        up_steps = [-k for k in range(half)] + list(range(1, half + 1))
        origins = ring_origins(req_index, req_devices, gate_steps + up_steps)
        down_origins = ring_origins(req_index, req_devices, near_steps + far_steps)
        gate, up = Ring(feedforward_weight[0], req_devices), Ring(feedforward_weight[1], req_devices)
        step(gate, up)
        (packed,) = tie([gate, up], packed)
        step(gate, up)
    arrived = lax.all_to_all(packed, "req", split_axis=0, concat_axis=0, tiled=True)

    projected_rows = [
        lax.dot_general(
            stream, attention_projection_weight[k], NT, preferred_element_type=jnp.float32
        )
        for k in range(3)
    ]
    holder_count = adapter_down_maps.shape[0]
    holder_rank_rows = jnp.einsum(
        "qf,kfn->qkn", stream, adapter_down_maps, preferred_element_type=jnp.float32
    )
    held_onehot = (
        token_adapter_index[:, None]
        == (mdl_index * holder_count + jnp.arange(holder_count, dtype=jnp.int32))[None, :]
    )
    rank_part = jnp.sum(holder_rank_rows * held_onehot.astype(jnp.float32)[:, :, None], axis=1)
    rank_feat = lax.psum(rank_part.astype(jnp.bfloat16), "mdl")
    all_onehot = (
        token_adapter_index[:, None] == jnp.arange(adapter_number, dtype=jnp.int32)[None, :]
    )
    broadcast_result = (
        all_onehot.astype(jnp.bfloat16)[:, :, None] * rank_feat[:, None, :]
    ).reshape(tok_count, adapter_number * rank_total_width)
    lora_query = lax.dot_general(
        broadcast_result, adapter_up_maps[0], NT, preferred_element_type=jnp.float32
    )
    lora_value = lax.dot_general(
        broadcast_result, adapter_up_maps[1], NT, preferred_element_type=jnp.float32
    )

    positions = jnp.arange(tok_count, dtype=jnp.int32)
    lengths_row = request_token_lengths[0]
    ends = jnp.sum(
        jnp.where(order_ids[:, None] >= order_ids[None, :], lengths_row[None, :], 0), axis=1
    )
    starts = ends - lengths_row
    member = (positions[:, None] >= starts[None, :]) & (positions[:, None] < ends[None, :])
    member_int = member.astype(jnp.int32)
    start_of = jnp.sum(member_int * starts[None, :], axis=1, keepdims=True)
    my_owner = lax.dynamic_slice_in_dim(owner_table, req_index, 1, 0)[0]
    earlier = (my_owner[:, None] == my_owner[None, :]).astype(jnp.int32) * earlier_one
    slot_in = my_owner * cap_slots + jnp.sum(earlier, axis=1)
    slot_of = jnp.sum(member_int * slot_in[None, :], axis=1, keepdims=True)
    tenant_hot = (
        request_tenant_index[:, None]
        == jnp.arange(tenant_adapter_scale.shape[0], dtype=jnp.int32)[None, :]
    ).astype(jnp.float32)
    request_scale = jnp.sum(tenant_hot * tenant_adapter_scale[None, :], axis=1)
    per_token_scale = jnp.sum(member.astype(jnp.float32) * request_scale[None, :], axis=1)[:, None]
    query_rows = (projected_rows[0] + per_token_scale * lora_query).astype(jnp.bfloat16)
    key_rows = projected_rows[1].astype(jnp.bfloat16)
    value_rows = (projected_rows[2] + per_token_scale * lora_value).astype(jnp.bfloat16)

    prefix = arrived.reshape((-1,) + arrived.shape[2:])
    blocks = tok_count // BLOCK
    if ringed:
        prefix, query_rows, key_rows, value_rows, *weights = tie(
            [gate, up], prefix, query_rows, key_rows, value_rows, *gather_model(head_output_weight)
        )
        step(gate, up)
        mixed = attention(query_rows, key_rows, value_rows, start_of, slot_of, prefix)
        (mixed,) = tie([gate, up], mixed)
        gate.step_forward()
        up.step_backward()
        (down_block,) = tie([gate, up], feedforward_weight[2])
        down = Ring(down_block, req_devices)
        step(down)
        normed, resid = project_and_normalise(
            mdl_index.reshape(1).astype(jnp.int32), gather_model(mixed), weights, stream,
            feedforward_norm_gain.reshape(1, model_width),
        )
        (normed,) = tie([down], normed)
        step(down)
        hidden = hidden_units(
            origins, gate.forward + gate.backward[1:], up.forward + up.backward[1:], normed
        )
        (hidden,) = tie([down], hidden)
        for _ in range(3, half):
            step(down)
        near_pieces = down.forward[:3] + down.backward[1:3]
        far_pieces = [side[k] for k in range(3, half) for side in (down.forward, down.backward)]
        down.step_forward(slice(0, rows_held // 2))
        down.step_backward(slice(rows_held // 2, rows_held))
        far_pieces += [down.forward[-1], down.backward[-1]]
        own, other, keep, send = down_sums(near_pieces, hidden)
        across = chip_swap(sum_on_chip(keep, send))
        near_terms = own, other
        far_cost = pl.CostEstimate(flops=1 << 33, bytes_accessed=0, transcendentals=0)
        own, other, keep, send = down_sums(far_pieces, hidden, far_cost)
        keep, near_sum = lax.optimization_barrier((keep, sum_here(*near_terms, across)))
        part = sum_on_chip(keep, send)
        groups = [near_sum], [own, core_swap(other), chip_swap(part)]
        return place_and_add(down_origins, resid, groups, rows_held)

    mixed = attention(query_rows, key_rows, value_rows, start_of, slot_of, prefix)
    mixed = jnp.concatenate(jnp.split(mixed, blocks, axis=1), axis=0)
    attn_part = jnp.dot(mixed, head_output_weight, preferred_element_type=jnp.float32).astype(jnp.bfloat16)
    attn_full = lax.psum(attn_part, "mdl").astype(jnp.float32)
    resid = (stream.astype(jnp.float32) + attn_full).astype(jnp.bfloat16)
    normed = normalise(resid, feedforward_norm_gain)
    resid_mine = lax.dynamic_slice_in_dim(resid, mdl_index * row_share, row_share, 0)
    full_mlp = lax.all_gather(feedforward_weight, "req", axis=1, tiled=True)
    gate_part = jnp.dot(normed, full_mlp[0], preferred_element_type=jnp.float32)
    up_part = jnp.dot(normed, full_mlp[1], preferred_element_type=jnp.float32)
    hidden = (jax.nn.silu(gate_part) * up_part).astype(jnp.bfloat16)
    mlp_part = lax.dot_general(
        hidden, full_mlp[2], NT, preferred_element_type=jnp.float32
    ).astype(jnp.bfloat16)
    mlp_mine = lax.psum_scatter(mlp_part, "mdl", scatter_dimension=0, tiled=True)
    return (resid_mine.astype(jnp.float32) + mlp_mine.astype(jnp.float32)).astype(jnp.bfloat16)


def solution(mesh):
    return jax.shard_map(
        per_device,
        mesh=mesh,
        in_specs=(
            P("req", None),
            P(None, "mdl", None),
            P("mdl", None),
            P("mdl", None, None),
            P(None, "mdl", None),
            P(),
            P(),
            P(None, "req", "mdl"),
            P("req", None, "mdl", None),
            P("req"),
            P("req", None),
            P("req"),
            P(),
            P(),
            P(),
        ),
        out_specs=P(("req", "mdl"), None),
        check_vma=False,
    )
```

```python
import functools
import math

import jax
import jax.numpy as jnp
from jax import lax
from jax.experimental import pallas as pl
from jax.experimental.pallas import tpu as pltpu
from jax.sharding import PartitionSpec as P

HEAD_SIZE = 112
WINDOW = 64
BLOCK = 192
HALO = 64
LANES = 256
VMEM_LIMIT = 28 * 1024 * 1024
NT = (((1,), (1,)), ((), ()))
SMALL = pl.CostEstimate(flops=0, bytes_accessed=0, transcendentals=0)


def pack_kernel(cap, table_ref, offset_ref, *refs):
    page_refs, out_ref = refs[:cap], refs[cap]
    dest = pl.program_id(0)
    lane = lax.broadcasted_iota(jnp.int32, out_ref.shape[3:], 1)
    for pair in range(cap // 2):
        first = offset_ref[dest * cap + 2 * pair]
        second = offset_ref[dest * cap + 2 * pair + 1]
        for part in range(2):
            left = page_refs[2 * pair][0, part].astype(jnp.float32)
            right = page_refs[2 * pair + 1][0, part].astype(jnp.float32)
            left = pltpu.roll(left, lax.rem(2 * WINDOW - first, 2 * WINDOW), 1)
            right = pltpu.roll(right, WINDOW - second, 1)
            out_ref[0, pair, part] = jnp.where(lane < WINDOW, left, right).astype(out_ref.dtype)


def pack_windows(pages, table, offsets, cap):
    parts = pages.shape[1:]
    dests = table.shape[0]

    def page_spec(place):
        return pl.BlockSpec(
            (1,) + parts, lambda dest, tbl, off: (tbl[dest * cap + place], 0, 0, 0)
        )

    return pl.pallas_call(
        functools.partial(pack_kernel, cap),
        grid_spec=pltpu.PrefetchScalarGridSpec(
            num_scalar_prefetch=2,
            grid=(dests,),
            in_specs=[page_spec(place) for place in range(cap)],
            out_specs=pl.BlockSpec(
                (1, cap // 2) + parts, lambda dest, tbl, off: (dest, 0, 0, 0, 0)
            ),
        ),
        out_shape=jax.ShapeDtypeStruct((dests, cap // 2) + parts, pages.dtype),
        compiler_params=pltpu.CompilerParams(vmem_limit_bytes=VMEM_LIMIT),
        cost_estimate=SMALL,
    )(table.reshape(-1), offsets.reshape(-1), *([pages] * cap))


def attention_kernel(
    query_ref, key_before_ref, key_ref, value_before_ref, value_ref, start_ref, slot_ref, prefix_ref,
    out_ref, mixed_ref,
):
    block = pl.program_id(0)
    pairs = prefix_ref.shape[0]
    heads = query_ref.shape[1] // HEAD_SIZE
    inv_scale = 1.0 / math.sqrt(HEAD_SIZE)
    start = start_ref[...]
    slot = slot_ref[...]
    own = block * BLOCK + lax.broadcasted_iota(jnp.int32, (BLOCK, 1), 0)
    other = block * BLOCK - HALO + lax.broadcasted_iota(jnp.int32, (1, HALO + BLOCK), 1)
    local_ok = (other >= jnp.maximum(start, own - WINDOW)) & (other <= own)
    lane = lax.broadcasted_iota(jnp.int32, (1, 2 * WINDOW), 1)
    pair_of = lax.shift_right_logical(slot, 1)
    lane_low = lax.bitwise_and(slot, 1) * WINDOW
    prefix_ok = (lane >= lane_low + (own - start)) & (lane < lane_low + WINDOW)
    in_pair = [jnp.broadcast_to(pair_of == pair, (BLOCK, 2 * WINDOW)) for pair in range(pairs)]
    for head in range(heads):
        columns = slice(head * HEAD_SIZE, (head + 1) * HEAD_SIZE)
        query = query_ref[:, columns]
        keys = jnp.concatenate([key_before_ref[:, columns], key_ref[:, columns]], axis=0)
        values = jnp.concatenate([value_before_ref[:, columns], value_ref[:, columns]], axis=0)
        local = lax.dot_general(query, keys, NT, preferred_element_type=jnp.float32)
        local = jnp.where(local_ok, local * inv_scale, -1e30)
        remote = jnp.zeros((BLOCK, 2 * WINDOW), jnp.float32)
        for pair in range(0, pairs, 2):
            wide = jnp.dot(
                query,
                jnp.concatenate([prefix_ref[pair, 0, columns], prefix_ref[pair + 1, 0, columns]], axis=1),
                preferred_element_type=jnp.float32,
            )
            remote = jnp.where(in_pair[pair], wide[:, : 2 * WINDOW], remote)
            remote = jnp.where(in_pair[pair + 1], wide[:, 2 * WINDOW :], remote)
        remote = jnp.where(prefix_ok, remote * inv_scale, -1e30)
        top = jnp.maximum(
            jnp.max(local, axis=1, keepdims=True), jnp.max(remote, axis=1, keepdims=True)
        )
        local = jnp.exp(local - top)
        remote = jnp.exp(remote - top)
        total = jnp.sum(local, axis=1, keepdims=True) + jnp.sum(remote, axis=1, keepdims=True)
        remote = remote.astype(jnp.bfloat16)
        spread = jnp.concatenate(
            [jnp.where(in_pair[pair], remote, jnp.zeros_like(remote)) for pair in range(pairs)], axis=1
        )
        held = jnp.concatenate([prefix_ref[pair, 1, columns] for pair in range(pairs)], axis=1)
        mixed = jnp.dot(local.astype(jnp.bfloat16), values, preferred_element_type=jnp.float32)
        mixed = mixed + lax.dot_general(spread, held, NT, preferred_element_type=jnp.float32)
        mixed_ref[:, columns] = (mixed * (1.0 / total)).astype(jnp.bfloat16)
    width = mixed_ref.shape[1]
    for number in range(out_ref.shape[1] // width):

        @pl.when(block == number)
        def _(number=number):
            out_ref[:, number * width : (number + 1) * width] = mixed_ref[...]


def attention(query, key, value, start, slot, prefix):
    tokens, width = query.shape
    step = BLOCK // HALO
    own = pl.BlockSpec((BLOCK, width), lambda i: (i, 0))
    before = pl.BlockSpec((HALO, width), lambda i: (jnp.maximum(i * step - 1, 0), 0))
    column = pl.BlockSpec((BLOCK, 1), lambda i: (i, 0))
    wide = BLOCK, width * (tokens // BLOCK)
    return pl.pallas_call(
        attention_kernel,
        grid=(tokens // BLOCK,),
        in_specs=[
            own, before, own, before, own, column, column,
            pl.BlockSpec(prefix.shape, lambda i: (0, 0, 0, 0)),
        ],
        out_specs=pl.BlockSpec(wide, lambda i: (0, 0)),
        out_shape=jax.ShapeDtypeStruct(wide, jnp.bfloat16),
        scratch_shapes=[pltpu.VMEM((BLOCK, width), jnp.bfloat16)],
        compiler_params=pltpu.CompilerParams(vmem_limit_bytes=VMEM_LIMIT),
        cost_estimate=SMALL,
    )(query, key, key, value, value, start, slot, prefix)


def project_kernel(place_ref, *refs):
    mixed_refs, weight_refs, refs = refs[:4], refs[4:8], refs[8:]
    stream_ref, gain_ref, normed_ref, mine_ref, mixed_all_ref, resid_ref = refs
    share, (tokens, model) = mine_ref.shape[0], resid_ref.shape
    width = weight_refs[0].shape[0]
    for number, mixed_ref in enumerate(mixed_refs):
        for block in range(4):
            mixed_all_ref[number, block * share : (block + 1) * share, :] = (
                mixed_ref[:, block * width : (block + 1) * width]
            )
    squares = jnp.zeros((tokens, 128), jnp.float32)
    for first in range(0, model, LANES):
        columns = slice(first, first + LANES)
        attn = sum(
            jnp.dot(mixed_all_ref[number], weight_ref[:, columns], preferred_element_type=jnp.float32)
            for number, weight_ref in enumerate(weight_refs)
        )
        resid = (stream_ref[:, columns].astype(jnp.float32) + attn).astype(resid_ref.dtype)
        resid_ref[:, columns] = resid
        wide = resid.astype(jnp.float32)
        for part in range(0, LANES, 128):
            squares = squares + wide[:, part : part + 128] * wide[:, part : part + 128]
    scale = lax.rsqrt(jnp.sum(squares, axis=1, keepdims=True) * (1.0 / model) + 1e-06)
    gain = gain_ref[...].astype(jnp.float32)
    own = pl.multiple_of(place_ref[0] * share, share)
    mine_ref[...] = resid_ref[pl.ds(own, share), :]
    for block in range(4):
        rows = slice(block * share, (block + 1) * share)
        first = pl.multiple_of(jnp.bitwise_xor(place_ref[0], block) * share, share)
        normed_ref[pl.ds(first, share), :] = (
            resid_ref[rows, :].astype(jnp.float32) * scale[rows] * gain
        ).astype(normed_ref.dtype)


def project_and_normalise(place, mixed, weights, stream, gain):
    tokens, model = stream.shape
    smem = pl.BlockSpec(memory_space=pltpu.SMEM)
    vmem = pl.BlockSpec(memory_space=pltpu.VMEM)
    return pl.pallas_call(
        project_kernel,
        in_specs=[smem] + [vmem] * 10,
        out_specs=[vmem] * 2,
        out_shape=[
            jax.ShapeDtypeStruct((tokens, model), stream.dtype),
            jax.ShapeDtypeStruct((tokens // 4, model), stream.dtype),
        ],
        scratch_shapes=[
            pltpu.VMEM((4, tokens, weights[0].shape[0]), jnp.bfloat16),
            pltpu.VMEM((tokens, model), jnp.bfloat16),
        ],
        compiler_params=pltpu.CompilerParams(vmem_limit_bytes=VMEM_LIMIT),
        cost_estimate=SMALL,
    )(place, *mixed, *weights, stream, gain)


def ring_place(index, count):
    return jnp.where(index % 2 == 0, index // 2, count - 1 - index // 2)


def ring_index(place, count):
    place = (place + count) % count
    return jnp.where(place < count // 2, 2 * place, 2 * (count - 1 - place) + 1)


class Ring:
    def __init__(self, block, count):
        cycle = list(range(0, count, 2)) + list(range(count - 1, 0, -2))
        self.pairs = [(cycle[at], cycle[(at + 1) % count]) for at in range(count)]
        self.forward, self.backward = [block], [block]

    def step_forward(self, rows=slice(None)):
        self.forward.append(lax.ppermute(self.forward[-1][rows], "req", self.pairs))

    def step_backward(self, rows=slice(None)):
        pairs = [(there, here) for here, there in self.pairs]
        self.backward.append(lax.ppermute(self.backward[-1][rows], "req", pairs))


def step(*rings):
    for ring in rings:
        ring.step_forward()
        ring.step_backward()


def tie(rings, *others):
    last = [side[-1] for ring in rings for side in (ring.forward, ring.backward)]
    last, others = lax.optimization_barrier((last, others))
    for ring in rings:
        ring.forward[-1], ring.backward[-1], *last = last
    return others


def ring_origins(index, count, steps):
    place = ring_place(index, count)
    return jnp.stack([ring_index(place + step, count) for step in steps]).astype(jnp.int32)


def hidden_kernel(pieces, origin_ref, *refs):
    gate_refs, up_refs, refs = refs[:pieces], refs[pieces : 2 * pieces], refs[2 * pieces :]
    normed_ref, hidden_ref, gate_ref, up_ref, sems = refs
    depth, width = gate_refs[0].shape
    chunks = [slice(0, LANES), slice(LANES, width)]
    copies = [[], []]
    for part, (piece_refs, buffer) in enumerate([(gate_refs, gate_ref), (up_refs, up_ref)]):
        for number, piece_ref in enumerate(piece_refs):
            rows = pl.ds(pl.multiple_of(origin_ref[part * pieces + number] * depth, 16), depth)
            for chunk, columns in enumerate(chunks):
                copies[chunk].append(
                    pltpu.make_async_copy(
                        piece_ref.at[:, columns],
                        buffer.at[rows, columns],
                        sems.at[chunk, part * pieces + number],
                    )
                )
    for chunk in copies:
        for copy in chunk:
            copy.start()
    for first in range(0, width, LANES):
        columns = slice(first, min(first + LANES, width))
        if first in (0, LANES):
            for copy in copies[first // LANES]:
                copy.wait()
        gate = jnp.dot(normed_ref[...], gate_ref[:, columns], preferred_element_type=jnp.float32)
        up = jnp.dot(normed_ref[...], up_ref[:, columns], preferred_element_type=jnp.float32)
        hidden_ref[:, columns] = (gate / (1.0 + jnp.exp(-gate)) * up).astype(jnp.bfloat16)


def hidden_units(origins, gate_pieces, up_pieces, normed):
    width = gate_pieces[0].shape[1]
    tokens, model = normed.shape
    count = len(gate_pieces)
    pieces = gate_pieces + up_pieces
    smem = pl.BlockSpec(memory_space=pltpu.SMEM)
    vmem = pl.BlockSpec(memory_space=pltpu.VMEM)
    anywhere = pl.BlockSpec(memory_space=pl.ANY)
    return pl.pallas_call(
        functools.partial(hidden_kernel, count),
        in_specs=[smem] + [anywhere] * len(pieces) + [vmem],
        out_specs=vmem,
        out_shape=jax.ShapeDtypeStruct((tokens, width), jnp.bfloat16),
        scratch_shapes=[
            pltpu.VMEM((model, width), jnp.bfloat16),
            pltpu.VMEM((model, width), jnp.bfloat16),
            pltpu.SemaphoreType.DMA((2, len(pieces))),
        ],
        compiler_params=pltpu.CompilerParams(vmem_limit_bytes=VMEM_LIMIT),
        cost_estimate=SMALL,
    )(origins, *pieces, normed)


def down_kernel(pieces, hidden_ref, *refs):
    piece_refs, out_refs = refs[:pieces], refs[pieces:]
    hidden = hidden_ref[...]
    blocks = [piece_ref[...] for piece_ref in piece_refs]
    depth = blocks[0].shape[0]
    if blocks[-1].shape[0] < depth:
        blocks[-2:] = [jnp.concatenate(blocks[-2:], axis=0)]
    for number, block in enumerate(blocks):
        columns = slice(number * depth, (number + 1) * depth)
        part = lax.dot_general(hidden, block, NT, preferred_element_type=jnp.float32)
        first = 0
        for out_ref in out_refs:
            rows = out_ref.shape[0]
            out_ref[:, columns] = part[first : first + rows].astype(out_ref.dtype)
            first += rows


def down_sums(pieces, hidden, cost=SMALL):
    tokens = hidden.shape[0]
    columns = sum(piece.shape[0] for piece in pieces)
    vmem = pl.BlockSpec(memory_space=pltpu.VMEM)
    return pl.pallas_call(
        functools.partial(down_kernel, len(pieces)),
        in_specs=[vmem] * (1 + len(pieces)),
        out_specs=[vmem] * 4,
        out_shape=[jax.ShapeDtypeStruct((tokens // 4, columns), jnp.bfloat16)] * 4,
        compiler_params=pltpu.CompilerParams(vmem_limit_bytes=VMEM_LIMIT),
        cost_estimate=cost,
    )(hidden, *pieces)


def place_kernel(groups, depth, origin_ref, resid_ref, *refs):
    term_refs, (out_ref, sum_ref) = refs[:-2], refs[-2:]
    rows, model = out_ref.shape
    sum_ref[...] = jnp.zeros_like(sum_ref)
    number, span = 0, 3 * 128
    for count, parts in groups:
        terms, term_refs = term_refs[:parts], term_refs[parts:]
        total = sum(term_ref[...].astype(jnp.float32) for term_ref in terms)
        for entry in range(count):
            first = origin_ref[number] * depth
            block = total[:, entry * depth : (entry + 1) * depth]
            block = jnp.concatenate([block, jnp.zeros((rows, span - depth), jnp.float32)], axis=1)
            block = pltpu.roll(block, lax.rem(first, 128), 1)
            lanes = pl.ds(pl.multiple_of(lax.div(first, 128) * 128, 128), span)
            sum_ref[:, lanes] += block
            number += 1
    out_ref[...] = (resid_ref[...].astype(jnp.float32) + sum_ref[:, :model]).astype(out_ref.dtype)


def place_and_add(origins, resid, groups, depth):
    sizes = [(terms[0].shape[1] // depth, len(terms)) for terms in groups]
    smem = pl.BlockSpec(memory_space=pltpu.SMEM)
    vmem = pl.BlockSpec(memory_space=pltpu.VMEM)
    terms = [term for group in groups for term in group]
    rows, model = resid.shape
    return pl.pallas_call(
        functools.partial(place_kernel, sizes, depth),
        in_specs=[smem] + [vmem] * (1 + len(terms)),
        out_specs=vmem,
        out_shape=jax.ShapeDtypeStruct(resid.shape, resid.dtype),
        scratch_shapes=[pltpu.VMEM((rows, model + 128), jnp.float32)],
        compiler_params=pltpu.CompilerParams(vmem_limit_bytes=VMEM_LIMIT),
        cost_estimate=SMALL,
    )(origins, resid, *terms)


def core_swap(array):
    return lax.ppermute(array, "mdl", [(0, 1), (1, 0), (2, 3), (3, 2)])


def chip_swap(array):
    return lax.ppermute(array, "mdl", [(0, 2), (2, 0), (1, 3), (3, 1)])


def gather_model(array):
    far = chip_swap(array)
    return [array, core_swap(array), far, core_swap(far)]


def sum_on_chip(keep, send):
    wide = jnp.float32
    return (keep.astype(wide) + core_swap(send).astype(wide)).astype(keep.dtype)


def sum_here(own, other, across):
    wide = jnp.float32
    return own.astype(wide) + core_swap(other).astype(wide) + across.astype(wide)


def normalise(resid, gain):
    wide = resid.astype(jnp.float32)
    mean_sq = jnp.mean(wide * wide, axis=1, keepdims=True)
    return (wide * lax.rsqrt(mean_sq + 1e-06) * gain.astype(jnp.float32)[None, :]).astype(jnp.bfloat16)


def per_device(
    stream,
    attention_projection_weight,
    head_output_weight,
    adapter_down_maps,
    adapter_up_maps,
    tenant_adapter_scale,
    feedforward_norm_gain,
    feedforward_weight,
    prefix_cache_store,
    token_adapter_index,
    request_token_lengths,
    request_tenant_index,
    last_page_holder,
    holder_page_slot,
    page_filled_rows,
):
    tok_count, model_width = stream.shape
    req_per_dev = request_token_lengths.shape[1]
    rank_total_width = adapter_down_maps.shape[2]
    adapter_number = adapter_up_maps.shape[2] // rank_total_width
    req_devices = lax.axis_size("req")
    req_index = lax.axis_index("req")
    mdl_index = lax.axis_index("mdl")
    row_share = tok_count // lax.axis_size("mdl")
    cap_slots = max(2, (req_per_dev + req_devices - 1) // req_devices + 1)
    cap_slots += cap_slots % 2

    order_ids = jnp.arange(req_per_dev, dtype=jnp.int32)
    owner_table = last_page_holder[:, 0].reshape(req_devices, req_per_dev)
    slot_table = holder_page_slot.reshape(req_devices, req_per_dev)
    offset_table = page_filled_rows.reshape(req_devices, req_per_dev) - WINDOW
    owned = (owner_table == req_index).astype(jnp.int32)
    earlier_one = (order_ids[:, None] > order_ids[None, :]).astype(jnp.int32)
    owned_rank = jnp.sum(owned[:, None, :] * earlier_one[None], axis=2)
    picked = owned[:, None, :] * (
        owned_rank[:, None, :] == jnp.arange(cap_slots, dtype=jnp.int32)[None, :, None]
    ).astype(jnp.int32)
    send_slot = jnp.sum(picked * slot_table[:, None, :], axis=2)
    send_offset = jnp.sum(picked * offset_table[:, None, :], axis=2)
    packed = pack_windows(prefix_cache_store, send_slot, send_offset, cap_slots)
    rows_held = feedforward_weight.shape[1]
    ringed = (lax.axis_size("mdl"), tok_count // BLOCK, req_devices, rows_held % 32) == (4, 4, 8, 0)
    if ringed:
        half = req_devices // 2
        near_steps = [-k for k in range(3)] + [1, 2]
        far_steps = [sign * k for k in range(3, half) for sign in (-1, 1)] + [half]
        gate_steps = [-k for k in range(half + 1)] + list(range(1, half))
        up_steps = [-k for k in range(half)] + list(range(1, half + 1))
        origins = ring_origins(req_index, req_devices, gate_steps + up_steps)
        down_origins = ring_origins(req_index, req_devices, near_steps + far_steps)
        gate, up = Ring(feedforward_weight[0], req_devices), Ring(feedforward_weight[1], req_devices)
        step(gate, up)
        (packed,) = tie([gate], packed)
        step(gate, up)
    arrived = lax.all_to_all(packed, "req", split_axis=0, concat_axis=0, tiled=True)

    projected_rows = [
        lax.dot_general(
            stream, attention_projection_weight[k], NT, preferred_element_type=jnp.float32
        )
        for k in range(3)
    ]
    holder_count = adapter_down_maps.shape[0]
    holder_rank_rows = jnp.einsum(
        "qf,kfn->qkn", stream, adapter_down_maps, preferred_element_type=jnp.float32
    )
    held_onehot = (
        token_adapter_index[:, None]
        == (mdl_index * holder_count + jnp.arange(holder_count, dtype=jnp.int32))[None, :]
    )
    rank_part = jnp.sum(holder_rank_rows * held_onehot.astype(jnp.float32)[:, :, None], axis=1)
    rank_feat = lax.psum(rank_part.astype(jnp.bfloat16), "mdl")
    all_onehot = (
        token_adapter_index[:, None] == jnp.arange(adapter_number, dtype=jnp.int32)[None, :]
    )
    broadcast_result = (
        all_onehot.astype(jnp.bfloat16)[:, :, None] * rank_feat[:, None, :]
    ).reshape(tok_count, adapter_number * rank_total_width)
    lora_query = lax.dot_general(
        broadcast_result, adapter_up_maps[0], NT, preferred_element_type=jnp.float32
    )
    lora_value = lax.dot_general(
        broadcast_result, adapter_up_maps[1], NT, preferred_element_type=jnp.float32
    )

    positions = jnp.arange(tok_count, dtype=jnp.int32)
    lengths_row = request_token_lengths[0]
    ends = jnp.sum(
        jnp.where(order_ids[:, None] >= order_ids[None, :], lengths_row[None, :], 0), axis=1
    )
    starts = ends - lengths_row
    member = (positions[:, None] >= starts[None, :]) & (positions[:, None] < ends[None, :])
    member_int = member.astype(jnp.int32)
    start_of = jnp.sum(member_int * starts[None, :], axis=1, keepdims=True)
    my_owner = lax.dynamic_slice_in_dim(owner_table, req_index, 1, 0)[0]
    earlier = (my_owner[:, None] == my_owner[None, :]).astype(jnp.int32) * earlier_one
    slot_in = my_owner * cap_slots + jnp.sum(earlier, axis=1)
    slot_of = jnp.sum(member_int * slot_in[None, :], axis=1, keepdims=True)
    tenant_hot = (
        request_tenant_index[:, None]
        == jnp.arange(tenant_adapter_scale.shape[0], dtype=jnp.int32)[None, :]
    ).astype(jnp.float32)
    request_scale = jnp.sum(tenant_hot * tenant_adapter_scale[None, :], axis=1)
    per_token_scale = jnp.sum(member.astype(jnp.float32) * request_scale[None, :], axis=1)[:, None]
    query_rows = (projected_rows[0] + per_token_scale * lora_query).astype(jnp.bfloat16)
    key_rows = projected_rows[1].astype(jnp.bfloat16)
    value_rows = (projected_rows[2] + per_token_scale * lora_value).astype(jnp.bfloat16)

    prefix = arrived.reshape((-1,) + arrived.shape[2:])
    blocks = tok_count // BLOCK
    if ringed:
        prefix, query_rows, key_rows, value_rows, *weights = tie(
            [gate, up], prefix, query_rows, key_rows, value_rows, *gather_model(head_output_weight)
        )
        step(gate, up)
        mixed = attention(query_rows, key_rows, value_rows, start_of, slot_of, prefix)
        (mixed,) = tie([gate, up], mixed)
        gate.step_forward()
        up.step_backward()
        (down_block,) = tie([gate, up], feedforward_weight[2])
        down = Ring(down_block, req_devices)
        step(down)
        normed, resid = project_and_normalise(
            mdl_index.reshape(1).astype(jnp.int32), gather_model(mixed), weights, stream,
            feedforward_norm_gain.reshape(1, model_width),
        )
        (normed,) = tie([down], normed)
        step(down)
        hidden = hidden_units(
            origins, gate.forward + gate.backward[1:], up.forward + up.backward[1:], normed
        )
        (hidden,) = tie([down], hidden)
        for _ in range(3, half):
            step(down)
        near_pieces = down.forward[:3] + down.backward[1:3]
        far_pieces = [side[k] for k in range(3, half) for side in (down.forward, down.backward)]
        down.step_forward(slice(0, rows_held // 2))
        down.step_backward(slice(rows_held // 2, rows_held))
        far_pieces += [down.forward[-1], down.backward[-1]]
        own, other, keep, send = down_sums(near_pieces, hidden)
        across = chip_swap(sum_on_chip(keep, send))
        near_terms = own, other
        far_cost = pl.CostEstimate(flops=1 << 33, bytes_accessed=0, transcendentals=0)
        own, other, keep, send = down_sums(far_pieces, hidden, far_cost)
        keep, near_sum = lax.optimization_barrier((keep, sum_here(*near_terms, across)))
        part = sum_on_chip(keep, send)
        groups = [near_sum], [own, core_swap(other), chip_swap(part)]
        return place_and_add(down_origins, resid, groups, rows_held)

    mixed = attention(query_rows, key_rows, value_rows, start_of, slot_of, prefix)
    mixed = jnp.concatenate(jnp.split(mixed, blocks, axis=1), axis=0)
    attn_part = jnp.dot(mixed, head_output_weight, preferred_element_type=jnp.float32).astype(jnp.bfloat16)
    attn_full = lax.psum(attn_part, "mdl").astype(jnp.float32)
    resid = (stream.astype(jnp.float32) + attn_full).astype(jnp.bfloat16)
    normed = normalise(resid, feedforward_norm_gain)
    resid_mine = lax.dynamic_slice_in_dim(resid, mdl_index * row_share, row_share, 0)
    full_mlp = lax.all_gather(feedforward_weight, "req", axis=1, tiled=True)
    gate_part = jnp.dot(normed, full_mlp[0], preferred_element_type=jnp.float32)
    up_part = jnp.dot(normed, full_mlp[1], preferred_element_type=jnp.float32)
    hidden = (jax.nn.silu(gate_part) * up_part).astype(jnp.bfloat16)
    mlp_part = lax.dot_general(
        hidden, full_mlp[2], NT, preferred_element_type=jnp.float32
    ).astype(jnp.bfloat16)
    mlp_mine = lax.psum_scatter(mlp_part, "mdl", scatter_dimension=0, tiled=True)
    return (resid_mine.astype(jnp.float32) + mlp_mine.astype(jnp.float32)).astype(jnp.bfloat16)


def solution(mesh):
    return jax.shard_map(
        per_device,
        mesh=mesh,
        in_specs=(
            P("req", None),
            P(None, "mdl", None),
            P("mdl", None),
            P("mdl", None, None),
            P(None, "mdl", None),
            P(),
            P(),
            P(None, "req", "mdl"),
            P("req", None, "mdl", None),
            P("req"),
            P("req", None),
            P("req"),
            P(),
            P(),
            P(),
        ),
        out_specs=P(("req", "mdl"), None),
        check_vma=False,
    )
```

```python
import functools
import math

import jax
import jax.numpy as jnp
from jax import lax
from jax.experimental import pallas as pl
from jax.experimental.pallas import tpu as pltpu
from jax.sharding import PartitionSpec as P

HEAD_SIZE = 112
WINDOW = 64
BLOCK = 192
HALO = 64
LANES = 256
VMEM_LIMIT = 48 * 1024 * 1024
VMEM_MOST = 60 * 1024 * 1024
NT = (((1,), (1,)), ((), ()))
SMALL = pl.CostEstimate(flops=0, bytes_accessed=0, transcendentals=0)


def pack_kernel(cap, table_ref, offset_ref, *refs):
    page_refs, out_ref = refs[:cap], refs[cap]
    dest = pl.program_id(0)
    lane = lax.broadcasted_iota(jnp.int32, out_ref.shape[3:], 1)
    for pair in range(cap // 2):
        first = offset_ref[dest * cap + 2 * pair]
        second = offset_ref[dest * cap + 2 * pair + 1]
        for part in range(2):
            left = page_refs[2 * pair][0, part].astype(jnp.float32)
            right = page_refs[2 * pair + 1][0, part].astype(jnp.float32)
            left = pltpu.roll(left, lax.rem(2 * WINDOW - first, 2 * WINDOW), 1)
            right = pltpu.roll(right, WINDOW - second, 1)
            out_ref[0, pair, part] = jnp.where(lane < WINDOW, left, right).astype(out_ref.dtype)


def pack_windows(pages, table, offsets, cap):
    parts = pages.shape[1:]
    dests = table.shape[0]

    def page_spec(place):
        return pl.BlockSpec(
            (1,) + parts, lambda dest, tbl, off: (tbl[dest * cap + place], 0, 0, 0)
        )

    return pl.pallas_call(
        functools.partial(pack_kernel, cap),
        grid_spec=pltpu.PrefetchScalarGridSpec(
            num_scalar_prefetch=2,
            grid=(dests,),
            in_specs=[page_spec(place) for place in range(cap)],
            out_specs=pl.BlockSpec(
                (1, cap // 2) + parts, lambda dest, tbl, off: (dest, 0, 0, 0, 0)
            ),
        ),
        out_shape=jax.ShapeDtypeStruct((dests, cap // 2) + parts, pages.dtype),
        compiler_params=pltpu.CompilerParams(vmem_limit_bytes=VMEM_LIMIT),
        cost_estimate=SMALL,
    )(table.reshape(-1), offsets.reshape(-1), *([pages] * cap))


def attention_kernel(
    query_ref, key_before_ref, key_ref, value_before_ref, value_ref, start_ref, slot_ref, prefix_ref,
    out_ref, mixed_ref,
):
    block = pl.program_id(0)
    pairs = prefix_ref.shape[0]
    heads = query_ref.shape[1] // HEAD_SIZE
    inv_scale = 1.0 / math.sqrt(HEAD_SIZE)
    start = start_ref[...]
    slot = slot_ref[...]
    own = block * BLOCK + lax.broadcasted_iota(jnp.int32, (BLOCK, 1), 0)
    other = block * BLOCK - HALO + lax.broadcasted_iota(jnp.int32, (1, HALO + BLOCK), 1)
    local_ok = (other >= jnp.maximum(start, own - WINDOW)) & (other <= own)
    lane = lax.broadcasted_iota(jnp.int32, (1, 2 * WINDOW), 1)
    pair_of = lax.shift_right_logical(slot, 1)
    lane_low = lax.bitwise_and(slot, 1) * WINDOW
    prefix_ok = (lane >= lane_low + (own - start)) & (lane < lane_low + WINDOW)
    in_pair = [jnp.broadcast_to(pair_of == pair, (BLOCK, 2 * WINDOW)) for pair in range(pairs)]
    for head in range(heads):
        columns = slice(head * HEAD_SIZE, (head + 1) * HEAD_SIZE)
        query = query_ref[:, columns]
        keys = jnp.concatenate([key_before_ref[:, columns], key_ref[:, columns]], axis=0)
        values = jnp.concatenate([value_before_ref[:, columns], value_ref[:, columns]], axis=0)
        local = lax.dot_general(query, keys, NT, preferred_element_type=jnp.float32)
        local = jnp.where(local_ok, local * inv_scale, -1e30)
        remote = jnp.zeros((BLOCK, 2 * WINDOW), jnp.float32)
        for pair in range(0, pairs, 2):
            wide = jnp.dot(
                query,
                jnp.concatenate([prefix_ref[pair, 0, columns], prefix_ref[pair + 1, 0, columns]], axis=1),
                preferred_element_type=jnp.float32,
            )
            remote = jnp.where(in_pair[pair], wide[:, : 2 * WINDOW], remote)
            remote = jnp.where(in_pair[pair + 1], wide[:, 2 * WINDOW :], remote)
        remote = jnp.where(prefix_ok, remote * inv_scale, -1e30)
        top = jnp.maximum(
            jnp.max(local, axis=1, keepdims=True), jnp.max(remote, axis=1, keepdims=True)
        )
        local = jnp.exp(local - top)
        remote = jnp.exp(remote - top)
        total = jnp.sum(local, axis=1, keepdims=True) + jnp.sum(remote, axis=1, keepdims=True)
        remote = remote.astype(jnp.bfloat16)
        spread = jnp.concatenate(
            [jnp.where(in_pair[pair], remote, jnp.zeros_like(remote)) for pair in range(pairs)], axis=1
        )
        held = jnp.concatenate([prefix_ref[pair, 1, columns] for pair in range(pairs)], axis=1)
        mixed = jnp.dot(local.astype(jnp.bfloat16), values, preferred_element_type=jnp.float32)
        mixed = mixed + lax.dot_general(spread, held, NT, preferred_element_type=jnp.float32)
        mixed_ref[:, columns] = (mixed * (1.0 / total)).astype(jnp.bfloat16)
    width = mixed_ref.shape[1]
    for number in range(out_ref.shape[1] // width):

        @pl.when(block == number)
        def _(number=number):
            out_ref[:, number * width : (number + 1) * width] = mixed_ref[...]


def attention(query, key, value, start, slot, prefix):
    tokens, width = query.shape
    step = BLOCK // HALO
    own = pl.BlockSpec((BLOCK, width), lambda i: (i, 0))
    before = pl.BlockSpec((HALO, width), lambda i: (jnp.maximum(i * step - 1, 0), 0))
    column = pl.BlockSpec((BLOCK, 1), lambda i: (i, 0))
    wide = BLOCK, width * (tokens // BLOCK)
    return pl.pallas_call(
        attention_kernel,
        grid=(tokens // BLOCK,),
        in_specs=[
            own, before, own, before, own, column, column,
            pl.BlockSpec(prefix.shape, lambda i: (0, 0, 0, 0)),
        ],
        out_specs=pl.BlockSpec(wide, lambda i: (0, 0)),
        out_shape=jax.ShapeDtypeStruct(wide, jnp.bfloat16),
        scratch_shapes=[pltpu.VMEM((BLOCK, width), jnp.bfloat16)],
        compiler_params=pltpu.CompilerParams(vmem_limit_bytes=VMEM_LIMIT),
        cost_estimate=SMALL,
    )(query, key, key, value, value, start, slot, prefix)


def project_kernel(place_ref, *refs):
    mixed_refs, weight_refs, refs = refs[:4], refs[4:8], refs[8:]
    stream_ref, gain_ref, normed_ref, mine_ref, mixed_all_ref, resid_ref = refs
    share, (tokens, model) = mine_ref.shape[0], resid_ref.shape
    width = weight_refs[0].shape[0]
    for number, mixed_ref in enumerate(mixed_refs):
        for block in range(4):
            mixed_all_ref[number, block * share : (block + 1) * share, :] = (
                mixed_ref[:, block * width : (block + 1) * width]
            )
    squares = jnp.zeros((tokens, 128), jnp.float32)
    for first in range(0, model, LANES):
        columns = slice(first, first + LANES)
        attn = sum(
            jnp.dot(mixed_all_ref[number], weight_ref[:, columns], preferred_element_type=jnp.float32)
            for number, weight_ref in enumerate(weight_refs)
        )
        resid = (stream_ref[:, columns].astype(jnp.float32) + attn).astype(resid_ref.dtype)
        resid_ref[:, columns] = resid
        wide = resid.astype(jnp.float32)
        for part in range(0, LANES, 128):
            squares = squares + wide[:, part : part + 128] * wide[:, part : part + 128]
    scale = lax.rsqrt(jnp.sum(squares, axis=1, keepdims=True) * (1.0 / model) + 1e-06)
    gain = gain_ref[...].astype(jnp.float32)
    own = pl.multiple_of(place_ref[0] * share, share)
    mine_ref[...] = resid_ref[pl.ds(own, share), :]
    for block in range(4):
        rows = slice(block * share, (block + 1) * share)
        first = pl.multiple_of(jnp.bitwise_xor(place_ref[0], block) * share, share)
        normed_ref[pl.ds(first, share), :] = (
            resid_ref[rows, :].astype(jnp.float32) * scale[rows] * gain
        ).astype(normed_ref.dtype)


def project_and_normalise(place, mixed, weights, stream, gain):
    tokens, model = stream.shape
    smem = pl.BlockSpec(memory_space=pltpu.SMEM)
    vmem = pl.BlockSpec(memory_space=pltpu.VMEM)
    return pl.pallas_call(
        project_kernel,
        in_specs=[smem] + [vmem] * 10,
        out_specs=[vmem] * 2,
        out_shape=[
            jax.ShapeDtypeStruct((tokens, model), stream.dtype),
            jax.ShapeDtypeStruct((tokens // 4, model), stream.dtype),
        ],
        scratch_shapes=[
            pltpu.VMEM((4, tokens, weights[0].shape[0]), jnp.bfloat16),
            pltpu.VMEM((tokens, model), jnp.bfloat16),
        ],
        compiler_params=pltpu.CompilerParams(vmem_limit_bytes=VMEM_LIMIT),
        cost_estimate=SMALL,
    )(place, *mixed, *weights, stream, gain)


def ring_place(index, count):
    return jnp.where(index % 2 == 0, index // 2, count - 1 - index // 2)


def ring_index(place, count):
    place = (place + count) % count
    return jnp.where(place < count // 2, 2 * place, 2 * (count - 1 - place) + 1)


class Ring:
    def __init__(self, block, count):
        cycle = list(range(0, count, 2)) + list(range(count - 1, 0, -2))
        self.pairs = [(cycle[at], cycle[(at + 1) % count]) for at in range(count)]
        self.forward, self.backward = [block], [block]

    def step_forward(self, rows=slice(None)):
        self.forward.append(lax.ppermute(self.forward[-1][rows], "req", self.pairs))

    def step_backward(self, rows=slice(None)):
        pairs = [(there, here) for here, there in self.pairs]
        self.backward.append(lax.ppermute(self.backward[-1][rows], "req", pairs))


def step(*rings):
    for ring in rings:
        ring.step_forward()
        ring.step_backward()


def tie(rings, *others):
    last = [side[-1] for ring in rings for side in (ring.forward, ring.backward)]
    last, others = lax.optimization_barrier((last, others))
    for ring in rings:
        ring.forward[-1], ring.backward[-1], *last = last
    return others


def ring_origins(index, count, steps):
    place = ring_place(index, count)
    return jnp.stack([ring_index(place + step, count) for step in steps]).astype(jnp.int32)


def hidden_kernel(pieces, origin_ref, *refs):
    gate_refs, up_refs, refs = refs[:pieces], refs[pieces : 2 * pieces], refs[2 * pieces :]
    normed_ref, hidden_ref, gate_ref, up_ref, sems = refs
    depth, width = gate_refs[0].shape
    chunks = [slice(0, LANES), slice(LANES, width)]
    copies = [[], []]
    for part, (piece_refs, buffer) in enumerate([(gate_refs, gate_ref), (up_refs, up_ref)]):
        for number, piece_ref in enumerate(piece_refs):
            rows = pl.ds(pl.multiple_of(origin_ref[part * pieces + number] * depth, 16), depth)
            for chunk, columns in enumerate(chunks):
                copies[chunk].append(
                    pltpu.make_async_copy(
                        piece_ref.at[:, columns],
                        buffer.at[rows, columns],
                        sems.at[chunk, part * pieces + number],
                    )
                )
    for chunk in copies:
        for copy in chunk:
            copy.start()
    for first in range(0, width, LANES):
        columns = slice(first, min(first + LANES, width))
        if first in (0, LANES):
            for copy in copies[first // LANES]:
                copy.wait()
        gate = jnp.dot(normed_ref[...], gate_ref[:, columns], preferred_element_type=jnp.float32)
        up = jnp.dot(normed_ref[...], up_ref[:, columns], preferred_element_type=jnp.float32)
        hidden_ref[:, columns] = (gate / (1.0 + jnp.exp(-gate)) * up).astype(jnp.bfloat16)


def hidden_units(origins, gate_pieces, up_pieces, normed):
    width = gate_pieces[0].shape[1]
    tokens, model = normed.shape
    count = len(gate_pieces)
    pieces = gate_pieces + up_pieces
    smem = pl.BlockSpec(memory_space=pltpu.SMEM)
    vmem = pl.BlockSpec(memory_space=pltpu.VMEM)
    anywhere = pl.BlockSpec(memory_space=pl.ANY)
    return pl.pallas_call(
        functools.partial(hidden_kernel, count),
        in_specs=[smem] + [anywhere] * len(pieces) + [vmem],
        out_specs=vmem,
        out_shape=jax.ShapeDtypeStruct((tokens, width), jnp.bfloat16),
        scratch_shapes=[
            pltpu.VMEM((model, width), jnp.bfloat16),
            pltpu.VMEM((model, width), jnp.bfloat16),
            pltpu.SemaphoreType.DMA((2, len(pieces))),
        ],
        compiler_params=pltpu.CompilerParams(vmem_limit_bytes=VMEM_MOST),
        cost_estimate=SMALL,
    )(origins, *pieces, normed)


def down_kernel(pieces, hidden_ref, *refs):
    piece_refs, out_refs = refs[:pieces], refs[pieces:]
    hidden = hidden_ref[...]
    blocks = [piece_ref[...] for piece_ref in piece_refs]
    depth = blocks[0].shape[0]
    if blocks[-1].shape[0] < depth:
        blocks[-2:] = [jnp.concatenate(blocks[-2:], axis=0)]
    for number, block in enumerate(blocks):
        columns = slice(number * depth, (number + 1) * depth)
        part = lax.dot_general(hidden, block, NT, preferred_element_type=jnp.float32)
        first = 0
        for out_ref in out_refs:
            rows = out_ref.shape[0]
            out_ref[:, columns] = part[first : first + rows].astype(out_ref.dtype)
            first += rows


def down_sums(pieces, hidden, cost=SMALL):
    tokens = hidden.shape[0]
    columns = sum(piece.shape[0] for piece in pieces)
    vmem = pl.BlockSpec(memory_space=pltpu.VMEM)
    return pl.pallas_call(
        functools.partial(down_kernel, len(pieces)),
        in_specs=[vmem] * (1 + len(pieces)),
        out_specs=[vmem] * 4,
        out_shape=[jax.ShapeDtypeStruct((tokens // 4, columns), jnp.bfloat16)] * 4,
        compiler_params=pltpu.CompilerParams(vmem_limit_bytes=VMEM_LIMIT),
        cost_estimate=cost,
    )(hidden, *pieces)


def place_kernel(groups, depth, origin_ref, resid_ref, *refs):
    term_refs, (out_ref, sum_ref) = refs[:-2], refs[-2:]
    rows, model = out_ref.shape
    sum_ref[...] = jnp.zeros_like(sum_ref)
    number, span = 0, 3 * 128
    for count, parts in groups:
        terms, term_refs = term_refs[:parts], term_refs[parts:]
        total = sum(term_ref[...].astype(jnp.float32) for term_ref in terms)
        for entry in range(count):
            first = origin_ref[number] * depth
            block = total[:, entry * depth : (entry + 1) * depth]
            block = jnp.concatenate([block, jnp.zeros((rows, span - depth), jnp.float32)], axis=1)
            block = pltpu.roll(block, lax.rem(first, 128), 1)
            lanes = pl.ds(pl.multiple_of(lax.div(first, 128) * 128, 128), span)
            sum_ref[:, lanes] += block
            number += 1
    out_ref[...] = (resid_ref[...].astype(jnp.float32) + sum_ref[:, :model]).astype(out_ref.dtype)


def place_and_add(origins, resid, groups, depth):
    sizes = [(terms[0].shape[1] // depth, len(terms)) for terms in groups]
    smem = pl.BlockSpec(memory_space=pltpu.SMEM)
    vmem = pl.BlockSpec(memory_space=pltpu.VMEM)
    terms = [term for group in groups for term in group]
    rows, model = resid.shape
    return pl.pallas_call(
        functools.partial(place_kernel, sizes, depth),
        in_specs=[smem] + [vmem] * (1 + len(terms)),
        out_specs=vmem,
        out_shape=jax.ShapeDtypeStruct(resid.shape, resid.dtype),
        scratch_shapes=[pltpu.VMEM((rows, model + 128), jnp.float32)],
        compiler_params=pltpu.CompilerParams(vmem_limit_bytes=VMEM_LIMIT),
        cost_estimate=SMALL,
    )(origins, resid, *terms)


def core_swap(array):
    return lax.ppermute(array, "mdl", [(0, 1), (1, 0), (2, 3), (3, 2)])


def chip_swap(array):
    return lax.ppermute(array, "mdl", [(0, 2), (2, 0), (1, 3), (3, 1)])


def gather_model(array):
    far = chip_swap(array)
    return [array, core_swap(array), far, core_swap(far)]


def sum_on_chip(keep, send):
    wide = jnp.float32
    return (keep.astype(wide) + core_swap(send).astype(wide)).astype(keep.dtype)


def sum_here(own, other, across):
    wide = jnp.float32
    return own.astype(wide) + core_swap(other).astype(wide) + across.astype(wide)


def normalise(resid, gain):
    wide = resid.astype(jnp.float32)
    mean_sq = jnp.mean(wide * wide, axis=1, keepdims=True)
    return (wide * lax.rsqrt(mean_sq + 1e-06) * gain.astype(jnp.float32)[None, :]).astype(jnp.bfloat16)


def per_device(
    stream,
    attention_projection_weight,
    head_output_weight,
    adapter_down_maps,
    adapter_up_maps,
    tenant_adapter_scale,
    feedforward_norm_gain,
    feedforward_weight,
    prefix_cache_store,
    token_adapter_index,
    request_token_lengths,
    request_tenant_index,
    last_page_holder,
    holder_page_slot,
    page_filled_rows,
):
    tok_count, model_width = stream.shape
    req_per_dev = request_token_lengths.shape[1]
    rank_total_width = adapter_down_maps.shape[2]
    adapter_number = adapter_up_maps.shape[2] // rank_total_width
    req_devices = lax.axis_size("req")
    req_index = lax.axis_index("req")
    mdl_index = lax.axis_index("mdl")
    row_share = tok_count // lax.axis_size("mdl")
    cap_slots = max(2, (req_per_dev + req_devices - 1) // req_devices + 1)
    cap_slots += cap_slots % 2

    order_ids = jnp.arange(req_per_dev, dtype=jnp.int32)
    owner_table = last_page_holder[:, 0].reshape(req_devices, req_per_dev)
    slot_table = holder_page_slot.reshape(req_devices, req_per_dev)
    offset_table = page_filled_rows.reshape(req_devices, req_per_dev) - WINDOW
    owned = (owner_table == req_index).astype(jnp.int32)
    earlier_one = (order_ids[:, None] > order_ids[None, :]).astype(jnp.int32)
    owned_rank = jnp.sum(owned[:, None, :] * earlier_one[None], axis=2)
    picked = owned[:, None, :] * (
        owned_rank[:, None, :] == jnp.arange(cap_slots, dtype=jnp.int32)[None, :, None]
    ).astype(jnp.int32)
    send_slot = jnp.sum(picked * slot_table[:, None, :], axis=2)
    send_offset = jnp.sum(picked * offset_table[:, None, :], axis=2)
    packed = pack_windows(prefix_cache_store, send_slot, send_offset, cap_slots)
    rows_held = feedforward_weight.shape[1]
    ringed = (lax.axis_size("mdl"), tok_count // BLOCK, req_devices, rows_held % 32) == (4, 4, 8, 0)
    if ringed:
        half = req_devices // 2
        near_steps = [-k for k in range(3)] + [1, 2]
        far_steps = [sign * k for k in range(3, half) for sign in (-1, 1)] + [half]
        gate_steps = [-k for k in range(half + 1)] + list(range(1, half))
        up_steps = [-k for k in range(half)] + list(range(1, half + 1))
        origins = ring_origins(req_index, req_devices, gate_steps + up_steps)
        down_origins = ring_origins(req_index, req_devices, near_steps + far_steps)
        gate, up = Ring(feedforward_weight[0], req_devices), Ring(feedforward_weight[1], req_devices)
        step(gate, up)
        (packed,) = tie([gate, up], packed)
        step(gate, up)
    arrived = lax.all_to_all(packed, "req", split_axis=0, concat_axis=0, tiled=True)

    projected_rows = [
        lax.dot_general(
            stream, attention_projection_weight[k], NT, preferred_element_type=jnp.float32
        )
        for k in range(3)
    ]
    holder_count = adapter_down_maps.shape[0]
    holder_rank_rows = jnp.einsum(
        "qf,kfn->qkn", stream, adapter_down_maps, preferred_element_type=jnp.float32
    )
    held_onehot = (
        token_adapter_index[:, None]
        == (mdl_index * holder_count + jnp.arange(holder_count, dtype=jnp.int32))[None, :]
    )
    rank_part = jnp.sum(holder_rank_rows * held_onehot.astype(jnp.float32)[:, :, None], axis=1)
    rank_feat = lax.psum(rank_part.astype(jnp.bfloat16), "mdl")
    all_onehot = (
        token_adapter_index[:, None] == jnp.arange(adapter_number, dtype=jnp.int32)[None, :]
    )
    broadcast_result = (
        all_onehot.astype(jnp.bfloat16)[:, :, None] * rank_feat[:, None, :]
    ).reshape(tok_count, adapter_number * rank_total_width)
    lora_query = lax.dot_general(
        broadcast_result, adapter_up_maps[0], NT, preferred_element_type=jnp.float32
    )
    lora_value = lax.dot_general(
        broadcast_result, adapter_up_maps[1], NT, preferred_element_type=jnp.float32
    )

    positions = jnp.arange(tok_count, dtype=jnp.int32)
    lengths_row = request_token_lengths[0]
    ends = jnp.sum(
        jnp.where(order_ids[:, None] >= order_ids[None, :], lengths_row[None, :], 0), axis=1
    )
    starts = ends - lengths_row
    member = (positions[:, None] >= starts[None, :]) & (positions[:, None] < ends[None, :])
    member_int = member.astype(jnp.int32)
    start_of = jnp.sum(member_int * starts[None, :], axis=1, keepdims=True)
    my_owner = lax.dynamic_slice_in_dim(owner_table, req_index, 1, 0)[0]
    earlier = (my_owner[:, None] == my_owner[None, :]).astype(jnp.int32) * earlier_one
    slot_in = my_owner * cap_slots + jnp.sum(earlier, axis=1)
    slot_of = jnp.sum(member_int * slot_in[None, :], axis=1, keepdims=True)
    tenant_hot = (
        request_tenant_index[:, None]
        == jnp.arange(tenant_adapter_scale.shape[0], dtype=jnp.int32)[None, :]
    ).astype(jnp.float32)
    request_scale = jnp.sum(tenant_hot * tenant_adapter_scale[None, :], axis=1)
    per_token_scale = jnp.sum(member.astype(jnp.float32) * request_scale[None, :], axis=1)[:, None]
    query_rows = (projected_rows[0] + per_token_scale * lora_query).astype(jnp.bfloat16)
    key_rows = projected_rows[1].astype(jnp.bfloat16)
    value_rows = (projected_rows[2] + per_token_scale * lora_value).astype(jnp.bfloat16)

    prefix = arrived.reshape((-1,) + arrived.shape[2:])
    blocks = tok_count // BLOCK
    if ringed:
        prefix, query_rows, key_rows, value_rows, *weights = tie(
            [gate, up], prefix, query_rows, key_rows, value_rows, *gather_model(head_output_weight)
        )
        step(gate, up)
        mixed = attention(query_rows, key_rows, value_rows, start_of, slot_of, prefix)
        (mixed,) = tie([gate, up], mixed)
        gate.step_forward()
        up.step_backward()
        (down_block,) = tie([gate, up], feedforward_weight[2])
        down = Ring(down_block, req_devices)
        step(down)
        normed, resid = project_and_normalise(
            mdl_index.reshape(1).astype(jnp.int32), gather_model(mixed), weights, stream,
            feedforward_norm_gain.reshape(1, model_width),
        )
        (normed,) = tie([down], normed)
        step(down)
        hidden = hidden_units(
            origins, gate.forward + gate.backward[1:], up.forward + up.backward[1:], normed
        )
        (hidden,) = tie([down], hidden)
        for _ in range(3, half):
            step(down)
        near_pieces = down.forward[:3] + down.backward[1:3]
        far_pieces = [side[k] for k in range(3, half) for side in (down.forward, down.backward)]
        down.step_forward(slice(0, rows_held // 2))
        down.step_backward(slice(rows_held // 2, rows_held))
        far_pieces += [down.forward[-1], down.backward[-1]]
        own, other, keep, send = down_sums(near_pieces, hidden)
        across = chip_swap(sum_on_chip(keep, send))
        near_terms = own, other
        far_cost = pl.CostEstimate(flops=1 << 33, bytes_accessed=0, transcendentals=0)
        own, other, keep, send = down_sums(far_pieces, hidden, far_cost)
        keep, near_sum = lax.optimization_barrier((keep, sum_here(*near_terms, across)))
        part = sum_on_chip(keep, send)
        groups = [near_sum], [own, core_swap(other), chip_swap(part)]
        return place_and_add(down_origins, resid, groups, rows_held)

    mixed = attention(query_rows, key_rows, value_rows, start_of, slot_of, prefix)
    mixed = jnp.concatenate(jnp.split(mixed, blocks, axis=1), axis=0)
    attn_part = jnp.dot(mixed, head_output_weight, preferred_element_type=jnp.float32).astype(jnp.bfloat16)
    attn_full = lax.psum(attn_part, "mdl").astype(jnp.float32)
    resid = (stream.astype(jnp.float32) + attn_full).astype(jnp.bfloat16)
    normed = normalise(resid, feedforward_norm_gain)
    resid_mine = lax.dynamic_slice_in_dim(resid, mdl_index * row_share, row_share, 0)
    full_mlp = lax.all_gather(feedforward_weight, "req", axis=1, tiled=True)
    gate_part = jnp.dot(normed, full_mlp[0], preferred_element_type=jnp.float32)
    up_part = jnp.dot(normed, full_mlp[1], preferred_element_type=jnp.float32)
    hidden = (jax.nn.silu(gate_part) * up_part).astype(jnp.bfloat16)
    mlp_part = lax.dot_general(
        hidden, full_mlp[2], NT, preferred_element_type=jnp.float32
    ).astype(jnp.bfloat16)
    mlp_mine = lax.psum_scatter(mlp_part, "mdl", scatter_dimension=0, tiled=True)
    return (resid_mine.astype(jnp.float32) + mlp_mine.astype(jnp.float32)).astype(jnp.bfloat16)


def solution(mesh):
    return jax.shard_map(
        per_device,
        mesh=mesh,
        in_specs=(
            P("req", None),
            P(None, "mdl", None),
            P("mdl", None),
            P("mdl", None, None),
            P(None, "mdl", None),
            P(),
            P(),
            P(None, "req", "mdl"),
            P("req", None, "mdl", None),
            P("req"),
            P("req", None),
            P("req"),
            P(),
            P(),
            P(),
        ),
        out_specs=P(("req", "mdl"), None),
        check_vma=False,
    )
```

```python
import functools
import math

import jax
import jax.numpy as jnp
from jax import lax
from jax.experimental import pallas as pl
from jax.experimental.pallas import tpu as pltpu
from jax.sharding import PartitionSpec as P

HEAD_SIZE = 112
WINDOW = 64
BLOCK = 192
HALO = 64
LANES = 256
VMEM_LIMIT = 48 * 1024 * 1024
VMEM_MOST = 60 * 1024 * 1024
NT = (((1,), (1,)), ((), ()))
SMALL = pl.CostEstimate(flops=0, bytes_accessed=0, transcendentals=0)


def pack_kernel(cap, table_ref, offset_ref, *refs):
    page_refs, out_ref = refs[:cap], refs[cap]
    dest = pl.program_id(0)
    lane = lax.broadcasted_iota(jnp.int32, out_ref.shape[3:], 1)
    for pair in range(cap // 2):
        first = offset_ref[dest * cap + 2 * pair]
        second = offset_ref[dest * cap + 2 * pair + 1]
        for part in range(2):
            left = page_refs[2 * pair][0, part].astype(jnp.float32)
            right = page_refs[2 * pair + 1][0, part].astype(jnp.float32)
            left = pltpu.roll(left, lax.rem(2 * WINDOW - first, 2 * WINDOW), 1)
            right = pltpu.roll(right, WINDOW - second, 1)
            out_ref[0, pair, part] = jnp.where(lane < WINDOW, left, right).astype(out_ref.dtype)


def pack_windows(pages, table, offsets, cap):
    parts = pages.shape[1:]
    dests = table.shape[0]

    def page_spec(place):
        return pl.BlockSpec(
            (1,) + parts, lambda dest, tbl, off: (tbl[dest * cap + place], 0, 0, 0)
        )

    return pl.pallas_call(
        functools.partial(pack_kernel, cap),
        grid_spec=pltpu.PrefetchScalarGridSpec(
            num_scalar_prefetch=2,
            grid=(dests,),
            in_specs=[page_spec(place) for place in range(cap)],
            out_specs=pl.BlockSpec(
                (1, cap // 2) + parts, lambda dest, tbl, off: (dest, 0, 0, 0, 0)
            ),
        ),
        out_shape=jax.ShapeDtypeStruct((dests, cap // 2) + parts, pages.dtype),
        compiler_params=pltpu.CompilerParams(vmem_limit_bytes=VMEM_LIMIT),
        cost_estimate=SMALL,
    )(table.reshape(-1), offsets.reshape(-1), *([pages] * cap))


def attention_kernel(
    query_ref, key_before_ref, key_ref, value_before_ref, value_ref, start_ref, slot_ref, prefix_ref,
    out_ref, mixed_ref,
):
    block = pl.program_id(0)
    pairs = prefix_ref.shape[0]
    heads = query_ref.shape[1] // HEAD_SIZE
    inv_scale = 1.0 / math.sqrt(HEAD_SIZE)
    start = start_ref[...]
    slot = slot_ref[...]
    own = block * BLOCK + lax.broadcasted_iota(jnp.int32, (BLOCK, 1), 0)
    other = block * BLOCK - HALO + lax.broadcasted_iota(jnp.int32, (1, HALO + BLOCK), 1)
    local_ok = (other >= jnp.maximum(start, own - WINDOW)) & (other <= own)
    lane = lax.broadcasted_iota(jnp.int32, (1, 2 * WINDOW), 1)
    pair_of = lax.shift_right_logical(slot, 1)
    lane_low = lax.bitwise_and(slot, 1) * WINDOW
    prefix_ok = (lane >= lane_low + (own - start)) & (lane < lane_low + WINDOW)
    in_pair = [jnp.broadcast_to(pair_of == pair, (BLOCK, 2 * WINDOW)) for pair in range(pairs)]
    for head in range(heads):
        columns = slice(head * HEAD_SIZE, (head + 1) * HEAD_SIZE)
        query = query_ref[:, columns]
        keys = jnp.concatenate([key_before_ref[:, columns], key_ref[:, columns]], axis=0)
        values = jnp.concatenate([value_before_ref[:, columns], value_ref[:, columns]], axis=0)
        local = lax.dot_general(query, keys, NT, preferred_element_type=jnp.float32)
        local = jnp.where(local_ok, local * inv_scale, -1e30)
        remote = jnp.zeros((BLOCK, 2 * WINDOW), jnp.float32)
        for pair in range(0, pairs, 2):
            wide = jnp.dot(
                query,
                jnp.concatenate([prefix_ref[pair, 0, columns], prefix_ref[pair + 1, 0, columns]], axis=1),
                preferred_element_type=jnp.float32,
            )
            remote = jnp.where(in_pair[pair], wide[:, : 2 * WINDOW], remote)
            remote = jnp.where(in_pair[pair + 1], wide[:, 2 * WINDOW :], remote)
        remote = jnp.where(prefix_ok, remote * inv_scale, -1e30)
        top = jnp.maximum(
            jnp.max(local, axis=1, keepdims=True), jnp.max(remote, axis=1, keepdims=True)
        )
        local = jnp.exp(local - top)
        remote = jnp.exp(remote - top)
        total = jnp.sum(local, axis=1, keepdims=True) + jnp.sum(remote, axis=1, keepdims=True)
        remote = remote.astype(jnp.bfloat16)
        spread = jnp.concatenate(
            [jnp.where(in_pair[pair], remote, jnp.zeros_like(remote)) for pair in range(pairs)], axis=1
        )
        held = jnp.concatenate([prefix_ref[pair, 1, columns] for pair in range(pairs)], axis=1)
        mixed = jnp.dot(local.astype(jnp.bfloat16), values, preferred_element_type=jnp.float32)
        mixed = mixed + lax.dot_general(spread, held, NT, preferred_element_type=jnp.float32)
        mixed_ref[:, columns] = (mixed * (1.0 / total)).astype(jnp.bfloat16)
    width = mixed_ref.shape[1]
    for number in range(out_ref.shape[1] // width):

        @pl.when(block == number)
        def _(number=number):
            out_ref[:, number * width : (number + 1) * width] = mixed_ref[...]


def attention(query, key, value, start, slot, prefix):
    tokens, width = query.shape
    step = BLOCK // HALO
    own = pl.BlockSpec((BLOCK, width), lambda i: (i, 0))
    before = pl.BlockSpec((HALO, width), lambda i: (jnp.maximum(i * step - 1, 0), 0))
    column = pl.BlockSpec((BLOCK, 1), lambda i: (i, 0))
    wide = BLOCK, width * (tokens // BLOCK)
    return pl.pallas_call(
        attention_kernel,
        grid=(tokens // BLOCK,),
        in_specs=[
            own, before, own, before, own, column, column,
            pl.BlockSpec(prefix.shape, lambda i: (0, 0, 0, 0)),
        ],
        out_specs=pl.BlockSpec(wide, lambda i: (0, 0)),
        out_shape=jax.ShapeDtypeStruct(wide, jnp.bfloat16),
        scratch_shapes=[pltpu.VMEM((BLOCK, width), jnp.bfloat16)],
        compiler_params=pltpu.CompilerParams(vmem_limit_bytes=VMEM_LIMIT),
        cost_estimate=SMALL,
    )(query, key, key, value, value, start, slot, prefix)


def project_kernel(place_ref, *refs):
    mixed_refs, weight_refs, refs = refs[:4], refs[4:8], refs[8:]
    stream_ref, gain_ref, normed_ref, mine_ref, mixed_all_ref, resid_ref = refs
    share, (tokens, model) = mine_ref.shape[0], resid_ref.shape
    width = weight_refs[0].shape[0]
    for number, mixed_ref in enumerate(mixed_refs):
        for block in range(4):
            mixed_all_ref[number, block * share : (block + 1) * share, :] = (
                mixed_ref[:, block * width : (block + 1) * width]
            )
    squares = jnp.zeros((tokens, 128), jnp.float32)
    for first in range(0, model, LANES):
        columns = slice(first, first + LANES)
        attn = sum(
            jnp.dot(mixed_all_ref[number], weight_ref[:, columns], preferred_element_type=jnp.float32)
            for number, weight_ref in enumerate(weight_refs)
        )
        resid = (stream_ref[:, columns].astype(jnp.float32) + attn).astype(resid_ref.dtype)
        resid_ref[:, columns] = resid
        wide = resid.astype(jnp.float32)
        for part in range(0, LANES, 128):
            squares = squares + wide[:, part : part + 128] * wide[:, part : part + 128]
    scale = lax.rsqrt(jnp.sum(squares, axis=1, keepdims=True) * (1.0 / model) + 1e-06)
    gain = gain_ref[...].astype(jnp.float32)
    own = pl.multiple_of(place_ref[0] * share, share)
    mine_ref[...] = resid_ref[pl.ds(own, share), :]
    for block in range(4):
        rows = slice(block * share, (block + 1) * share)
        first = pl.multiple_of(jnp.bitwise_xor(place_ref[0], block) * share, share)
        normed_ref[pl.ds(first, share), :] = (
            resid_ref[rows, :].astype(jnp.float32) * scale[rows] * gain
        ).astype(normed_ref.dtype)


def project_and_normalise(place, mixed, weights, stream, gain):
    tokens, model = stream.shape
    smem = pl.BlockSpec(memory_space=pltpu.SMEM)
    vmem = pl.BlockSpec(memory_space=pltpu.VMEM)
    return pl.pallas_call(
        project_kernel,
        in_specs=[smem] + [vmem] * 10,
        out_specs=[vmem] * 2,
        out_shape=[
            jax.ShapeDtypeStruct((tokens, model), stream.dtype),
            jax.ShapeDtypeStruct((tokens // 4, model), stream.dtype),
        ],
        scratch_shapes=[
            pltpu.VMEM((4, tokens, weights[0].shape[0]), jnp.bfloat16),
            pltpu.VMEM((tokens, model), jnp.bfloat16),
        ],
        compiler_params=pltpu.CompilerParams(vmem_limit_bytes=VMEM_LIMIT),
        cost_estimate=SMALL,
    )(place, *mixed, *weights, stream, gain)


def ring_place(index, count):
    return jnp.where(index % 2 == 0, index // 2, count - 1 - index // 2)


def ring_index(place, count):
    place = (place + count) % count
    return jnp.where(place < count // 2, 2 * place, 2 * (count - 1 - place) + 1)


class Ring:
    def __init__(self, block, count):
        cycle = list(range(0, count, 2)) + list(range(count - 1, 0, -2))
        self.pairs = [(cycle[at], cycle[(at + 1) % count]) for at in range(count)]
        self.forward, self.backward = [block], [block]

    def step_forward(self, rows=slice(None)):
        self.forward.append(lax.ppermute(self.forward[-1][rows], "req", self.pairs))

    def step_backward(self, rows=slice(None)):
        pairs = [(there, here) for here, there in self.pairs]
        self.backward.append(lax.ppermute(self.backward[-1][rows], "req", pairs))


def step(*rings):
    for ring in rings:
        ring.step_forward()
        ring.step_backward()


def tie(rings, *others):
    last = [side[-1] for ring in rings for side in (ring.forward, ring.backward)]
    last, others = lax.optimization_barrier((last, others))
    for ring in rings:
        ring.forward[-1], ring.backward[-1], *last = last
    return others


def ring_origins(index, count, steps):
    place = ring_place(index, count)
    return jnp.stack([ring_index(place + step, count) for step in steps]).astype(jnp.int32)


def hidden_kernel(pieces, origin_ref, *refs):
    gate_refs, up_refs, refs = refs[:pieces], refs[pieces : 2 * pieces], refs[2 * pieces :]
    normed_ref, hidden_ref, gate_ref, up_ref, sems = refs
    depth, width = gate_refs[0].shape
    chunks = [slice(0, LANES), slice(LANES, width)]
    copies = [[], []]
    for part, (piece_refs, buffer) in enumerate([(gate_refs, gate_ref), (up_refs, up_ref)]):
        for number, piece_ref in enumerate(piece_refs):
            rows = pl.ds(pl.multiple_of(origin_ref[part * pieces + number] * depth, 16), depth)
            for chunk, columns in enumerate(chunks):
                copies[chunk].append(
                    pltpu.make_async_copy(
                        piece_ref.at[:, columns],
                        buffer.at[rows, columns],
                        sems.at[chunk, part * pieces + number],
                    )
                )
    for chunk in copies:
        for copy in chunk:
            copy.start()
    for first in range(0, width, LANES):
        columns = slice(first, min(first + LANES, width))
        if first in (0, LANES):
            for copy in copies[first // LANES]:
                copy.wait()
        gate = jnp.dot(normed_ref[...], gate_ref[:, columns], preferred_element_type=jnp.float32)
        up = jnp.dot(normed_ref[...], up_ref[:, columns], preferred_element_type=jnp.float32)
        hidden_ref[:, columns] = (gate / (1.0 + jnp.exp(-gate)) * up).astype(jnp.bfloat16)


def hidden_units(origins, gate_pieces, up_pieces, normed):
    width = gate_pieces[0].shape[1]
    tokens, model = normed.shape
    count = len(gate_pieces)
    pieces = gate_pieces + up_pieces
    smem = pl.BlockSpec(memory_space=pltpu.SMEM)
    vmem = pl.BlockSpec(memory_space=pltpu.VMEM)
    anywhere = pl.BlockSpec(memory_space=pl.ANY)
    return pl.pallas_call(
        functools.partial(hidden_kernel, count),
        in_specs=[smem] + [anywhere] * len(pieces) + [vmem],
        out_specs=vmem,
        out_shape=jax.ShapeDtypeStruct((tokens, width), jnp.bfloat16),
        scratch_shapes=[
            pltpu.VMEM((model, width), jnp.bfloat16),
            pltpu.VMEM((model, width), jnp.bfloat16),
            pltpu.SemaphoreType.DMA((2, len(pieces))),
        ],
        compiler_params=pltpu.CompilerParams(vmem_limit_bytes=VMEM_MOST),
        cost_estimate=SMALL,
    )(origins, *pieces, normed)


def down_kernel(pieces, hidden_ref, *refs):
    piece_refs, out_refs = refs[:pieces], refs[pieces:]
    hidden = hidden_ref[...]
    blocks = [piece_ref[...] for piece_ref in piece_refs]
    depth = blocks[0].shape[0]
    if blocks[-1].shape[0] < depth:
        blocks[-2:] = [jnp.concatenate(blocks[-2:], axis=0)]
    for number, block in enumerate(blocks):
        columns = slice(number * depth, (number + 1) * depth)
        part = lax.dot_general(hidden, block, NT, preferred_element_type=jnp.float32)
        first = 0
        for out_ref in out_refs:
            rows = out_ref.shape[0]
            out_ref[:, columns] = part[first : first + rows].astype(out_ref.dtype)
            first += rows


def down_sums(pieces, hidden, cost=SMALL):
    tokens = hidden.shape[0]
    columns = sum(piece.shape[0] for piece in pieces)
    vmem = pl.BlockSpec(memory_space=pltpu.VMEM)
    return pl.pallas_call(
        functools.partial(down_kernel, len(pieces)),
        in_specs=[vmem] * (1 + len(pieces)),
        out_specs=[vmem] * 4,
        out_shape=[jax.ShapeDtypeStruct((tokens // 4, columns), jnp.bfloat16)] * 4,
        compiler_params=pltpu.CompilerParams(vmem_limit_bytes=VMEM_LIMIT),
        cost_estimate=cost,
    )(hidden, *pieces)


def place_kernel(groups, depth, origin_ref, resid_ref, *refs):
    term_refs, (out_ref, sum_ref) = refs[:-2], refs[-2:]
    rows, model = out_ref.shape
    sum_ref[...] = jnp.zeros_like(sum_ref)
    number, span = 0, 3 * 128
    for count, parts in groups:
        terms, term_refs = term_refs[:parts], term_refs[parts:]
        total = sum(term_ref[...].astype(jnp.float32) for term_ref in terms)
        for entry in range(count):
            first = origin_ref[number] * depth
            block = total[:, entry * depth : (entry + 1) * depth]
            block = jnp.concatenate([block, jnp.zeros((rows, span - depth), jnp.float32)], axis=1)
            block = pltpu.roll(block, lax.rem(first, 128), 1)
            lanes = pl.ds(pl.multiple_of(lax.div(first, 128) * 128, 128), span)
            sum_ref[:, lanes] += block
            number += 1
    out_ref[...] = (resid_ref[...].astype(jnp.float32) + sum_ref[:, :model]).astype(out_ref.dtype)


def place_and_add(origins, resid, groups, depth):
    sizes = [(terms[0].shape[1] // depth, len(terms)) for terms in groups]
    smem = pl.BlockSpec(memory_space=pltpu.SMEM)
    vmem = pl.BlockSpec(memory_space=pltpu.VMEM)
    terms = [term for group in groups for term in group]
    rows, model = resid.shape
    return pl.pallas_call(
        functools.partial(place_kernel, sizes, depth),
        in_specs=[smem] + [vmem] * (1 + len(terms)),
        out_specs=vmem,
        out_shape=jax.ShapeDtypeStruct(resid.shape, resid.dtype),
        scratch_shapes=[pltpu.VMEM((rows, model + 128), jnp.float32)],
        compiler_params=pltpu.CompilerParams(vmem_limit_bytes=VMEM_LIMIT),
        cost_estimate=SMALL,
    )(origins, resid, *terms)


def core_swap(array):
    return lax.ppermute(array, "mdl", [(0, 1), (1, 0), (2, 3), (3, 2)])


def chip_swap(array):
    return lax.ppermute(array, "mdl", [(0, 2), (2, 0), (1, 3), (3, 1)])


def gather_model(array):
    far = chip_swap(array)
    return [array, core_swap(array), far, core_swap(far)]


def sum_on_chip(keep, send):
    wide = jnp.float32
    return (keep.astype(wide) + core_swap(send).astype(wide)).astype(keep.dtype)


def sum_here(own, other, across):
    wide = jnp.float32
    return own.astype(wide) + core_swap(other).astype(wide) + across.astype(wide)


def normalise(resid, gain):
    wide = resid.astype(jnp.float32)
    mean_sq = jnp.mean(wide * wide, axis=1, keepdims=True)
    return (wide * lax.rsqrt(mean_sq + 1e-06) * gain.astype(jnp.float32)[None, :]).astype(jnp.bfloat16)


def per_device(
    stream,
    attention_projection_weight,
    head_output_weight,
    adapter_down_maps,
    adapter_up_maps,
    tenant_adapter_scale,
    feedforward_norm_gain,
    feedforward_weight,
    prefix_cache_store,
    token_adapter_index,
    request_token_lengths,
    request_tenant_index,
    last_page_holder,
    holder_page_slot,
    page_filled_rows,
):
    tok_count, model_width = stream.shape
    req_per_dev = request_token_lengths.shape[1]
    rank_total_width = adapter_down_maps.shape[2]
    adapter_number = adapter_up_maps.shape[2] // rank_total_width
    req_devices = lax.axis_size("req")
    req_index = lax.axis_index("req")
    mdl_index = lax.axis_index("mdl")
    row_share = tok_count // lax.axis_size("mdl")
    cap_slots = max(2, (req_per_dev + req_devices - 1) // req_devices + 1)
    cap_slots += cap_slots % 2

    order_ids = jnp.arange(req_per_dev, dtype=jnp.int32)
    owner_table = last_page_holder[:, 0].reshape(req_devices, req_per_dev)
    slot_table = holder_page_slot.reshape(req_devices, req_per_dev)
    offset_table = page_filled_rows.reshape(req_devices, req_per_dev) - WINDOW
    owned = (owner_table == req_index).astype(jnp.int32)
    earlier_one = (order_ids[:, None] > order_ids[None, :]).astype(jnp.int32)
    owned_rank = jnp.sum(owned[:, None, :] * earlier_one[None], axis=2)
    picked = owned[:, None, :] * (
        owned_rank[:, None, :] == jnp.arange(cap_slots, dtype=jnp.int32)[None, :, None]
    ).astype(jnp.int32)
    send_slot = jnp.sum(picked * slot_table[:, None, :], axis=2)
    send_offset = jnp.sum(picked * offset_table[:, None, :], axis=2)
    packed = pack_windows(prefix_cache_store, send_slot, send_offset, cap_slots)
    rows_held = feedforward_weight.shape[1]
    ringed = (lax.axis_size("mdl"), tok_count // BLOCK, req_devices, rows_held % 32) == (4, 4, 8, 0)
    if ringed:
        half = req_devices // 2
        near_steps = [-k for k in range(3)] + [1, 2]
        far_steps = [sign * k for k in range(3, half) for sign in (-1, 1)] + [half]
        gate_steps = [-k for k in range(half + 1)] + list(range(1, half))
        up_steps = [-k for k in range(half)] + list(range(1, half + 1))
        origins = ring_origins(req_index, req_devices, gate_steps + up_steps)
        down_origins = ring_origins(req_index, req_devices, near_steps + far_steps)
        gate, up = Ring(feedforward_weight[0], req_devices), Ring(feedforward_weight[1], req_devices)
        step(gate, up)
        (packed,) = tie([gate, up], packed)
        step(gate, up)
    arrived = lax.all_to_all(packed, "req", split_axis=0, concat_axis=0, tiled=True)

    projected_rows = [
        lax.dot_general(
            stream, attention_projection_weight[k], NT, preferred_element_type=jnp.float32
        )
        for k in range(3)
    ]
    holder_count = adapter_down_maps.shape[0]
    holder_rank_rows = jnp.einsum(
        "qf,kfn->qkn", stream, adapter_down_maps, preferred_element_type=jnp.float32
    )
    held_onehot = (
        token_adapter_index[:, None]
        == (mdl_index * holder_count + jnp.arange(holder_count, dtype=jnp.int32))[None, :]
    )
    rank_part = jnp.sum(holder_rank_rows * held_onehot.astype(jnp.float32)[:, :, None], axis=1)
    rank_feat = lax.psum(rank_part.astype(jnp.bfloat16), "mdl")
    all_onehot = (
        token_adapter_index[:, None] == jnp.arange(adapter_number, dtype=jnp.int32)[None, :]
    )
    broadcast_result = (
        all_onehot.astype(jnp.bfloat16)[:, :, None] * rank_feat[:, None, :]
    ).reshape(tok_count, adapter_number * rank_total_width)
    lora_query = lax.dot_general(
        broadcast_result, adapter_up_maps[0], NT, preferred_element_type=jnp.float32
    )
    lora_value = lax.dot_general(
        broadcast_result, adapter_up_maps[1], NT, preferred_element_type=jnp.float32
    )

    positions = jnp.arange(tok_count, dtype=jnp.int32)
    lengths_row = request_token_lengths[0]
    ends = jnp.sum(
        jnp.where(order_ids[:, None] >= order_ids[None, :], lengths_row[None, :], 0), axis=1
    )
    starts = ends - lengths_row
    member = (positions[:, None] >= starts[None, :]) & (positions[:, None] < ends[None, :])
    member_int = member.astype(jnp.int32)
    start_of = jnp.sum(member_int * starts[None, :], axis=1, keepdims=True)
    my_owner = lax.dynamic_slice_in_dim(owner_table, req_index, 1, 0)[0]
    earlier = (my_owner[:, None] == my_owner[None, :]).astype(jnp.int32) * earlier_one
    slot_in = my_owner * cap_slots + jnp.sum(earlier, axis=1)
    slot_of = jnp.sum(member_int * slot_in[None, :], axis=1, keepdims=True)
    tenant_hot = (
        request_tenant_index[:, None]
        == jnp.arange(tenant_adapter_scale.shape[0], dtype=jnp.int32)[None, :]
    ).astype(jnp.float32)
    request_scale = jnp.sum(tenant_hot * tenant_adapter_scale[None, :], axis=1)
    per_token_scale = jnp.sum(member.astype(jnp.float32) * request_scale[None, :], axis=1)[:, None]
    query_rows = (projected_rows[0] + per_token_scale * lora_query).astype(jnp.bfloat16)
    key_rows = projected_rows[1].astype(jnp.bfloat16)
    value_rows = (projected_rows[2] + per_token_scale * lora_value).astype(jnp.bfloat16)

    prefix = arrived.reshape((-1,) + arrived.shape[2:])
    blocks = tok_count // BLOCK
    if ringed:
        prefix, query_rows, key_rows, value_rows, *weights = tie(
            [gate, up], prefix, query_rows, key_rows, value_rows, *gather_model(head_output_weight)
        )
        step(gate, up)
        mixed = attention(query_rows, key_rows, value_rows, start_of, slot_of, prefix)
        (mixed,) = tie([gate, up], mixed)
        gate.step_forward()
        up.step_backward()
        (down_block,) = tie([gate, up], feedforward_weight[2])
        down = Ring(down_block, req_devices)
        step(down)
        normed, resid = project_and_normalise(
            mdl_index.reshape(1).astype(jnp.int32), gather_model(mixed), weights, stream,
            feedforward_norm_gain.reshape(1, model_width),
        )
        (normed,) = tie([down], normed)
        step(down)
        hidden = hidden_units(
            origins, gate.forward + gate.backward[1:], up.forward + up.backward[1:], normed
        )
        (hidden,) = tie([down], hidden)
        for _ in range(3, half):
            step(down)
        near_pieces = down.forward[:3] + down.backward[1:3]
        far_pieces = [side[k] for k in range(3, half) for side in (down.forward, down.backward)]
        down.step_forward(slice(0, rows_held // 2))
        down.step_backward(slice(rows_held // 2, rows_held))
        far_pieces += [down.forward[-1], down.backward[-1]]
        own, other, keep, send = down_sums(near_pieces, hidden)
        across = chip_swap(sum_on_chip(keep, send))
        near_terms = own, other
        far_cost = pl.CostEstimate(flops=1 << 33, bytes_accessed=0, transcendentals=0)
        own, other, keep, send = down_sums(far_pieces, hidden, far_cost)
        keep, across = lax.optimization_barrier((keep, across))
        part = sum_on_chip(keep, send)
        groups = [near_terms[0], core_swap(near_terms[1]), across], [own, core_swap(other), chip_swap(part)]
        return place_and_add(down_origins, resid, groups, rows_held)

    mixed = attention(query_rows, key_rows, value_rows, start_of, slot_of, prefix)
    mixed = jnp.concatenate(jnp.split(mixed, blocks, axis=1), axis=0)
    attn_part = jnp.dot(mixed, head_output_weight, preferred_element_type=jnp.float32).astype(jnp.bfloat16)
    attn_full = lax.psum(attn_part, "mdl").astype(jnp.float32)
    resid = (stream.astype(jnp.float32) + attn_full).astype(jnp.bfloat16)
    normed = normalise(resid, feedforward_norm_gain)
    resid_mine = lax.dynamic_slice_in_dim(resid, mdl_index * row_share, row_share, 0)
    full_mlp = lax.all_gather(feedforward_weight, "req", axis=1, tiled=True)
    gate_part = jnp.dot(normed, full_mlp[0], preferred_element_type=jnp.float32)
    up_part = jnp.dot(normed, full_mlp[1], preferred_element_type=jnp.float32)
    hidden = (jax.nn.silu(gate_part) * up_part).astype(jnp.bfloat16)
    mlp_part = lax.dot_general(
        hidden, full_mlp[2], NT, preferred_element_type=jnp.float32
    ).astype(jnp.bfloat16)
    mlp_mine = lax.psum_scatter(mlp_part, "mdl", scatter_dimension=0, tiled=True)
    return (resid_mine.astype(jnp.float32) + mlp_mine.astype(jnp.float32)).astype(jnp.bfloat16)


def solution(mesh):
    return jax.shard_map(
        per_device,
        mesh=mesh,
        in_specs=(
            P("req", None),
            P(None, "mdl", None),
            P("mdl", None),
            P("mdl", None, None),
            P(None, "mdl", None),
            P(),
            P(),
            P(None, "req", "mdl"),
            P("req", None, "mdl", None),
            P("req"),
            P("req", None),
            P("req"),
            P(),
            P(),
            P(),
        ),
        out_specs=P(("req", "mdl"), None),
        check_vma=False,
    )
```
